128 devices in a mesh: tm: 4 (over x), space: 32 (over y, z, core).
Axes of the slice: x: 4, y: 4, z: 4, core: 2. Of those that a mesh axis runs over, the one named last changes fastest.
Arguments:
- dual_weights: float32 [1048576], P(('tm', 'space')), may hold values from -6 to 6
- direction: float32 [1048576], P(('tm', 'space')), may hold values from -20 to 20
- residual_dual: float32 [1048576], P(('tm', 'space')), may hold values from -20 to 20
- obs_var: float32 [1048576], P(('tm', 'space')), may hold values from 0.2 to 1
- obs_route: int32 [1048576, 1], P(('tm', 'space')), may hold values from 0 to 127; in each aligned block of 8192 rows (0 to 8191, 8192 to 16383, ...) at most 128 rows name the same one
- obs_cell: int32 [1048576], P(('tm', 'space')), may hold values from 0 to 524030, as said below
- obs_interp: float32 [4, 1048576], P(None, ('tm', 'space')), may hold values from 0 to 1, as said below
- wind_x: float32 [4, 16, 256, 256], P('tm', None, 'space'), may hold values from -0.35 to 0.35
- wind_y: float32 [4, 16, 256, 256], P('tm', None, 'space'), may hold values from -0.35 to 0.35
- coupling: float32 [4, 4], replicated, may hold values from -3 to 3
- cov_scale: float32 [4, 4, 16], P('tm'), may hold values from 1.5 to 4
Outputs:
- dual_next: float32 [1048576], P(('tm', 'space'))
- residual_next: float32 [1048576], P(('tm', 'space'))
- direction_next: float32 [1048576], P(('tm', 'space'))
The draws below stay inside these ranges and needn't reach their ends.
Inputs may be any that keep to these rules, and one draw needn't show every extreme that they name: `obs_route`: among the rows of one device, at most 128 observations name any one destination. `obs_cell`: A cell (step, variable, level, x, y) of the destination strip with x below 7 and y below 255. `obs_interp`: four nonnegative bilinear weights summing to one for each observation.
All inputs are finite; a program needn't handle non-finite values.
Results may differ from the reference program's by a relative error of at most 0.0001.
Values sent between devices are 32-bit elements; how exact they have to be, the bound alone decides.
A program may use at most 128 MiB of HBM per device.

```python
import math
import jax
import jax.numpy as jnp
import numpy as np
from jax import lax

NV = 4
LEV = 16
CX = 8
NY = 256
STEPS = 4
OBS_DEV = 8192
GROUPS = 4
NX = 256
OBS = 1048576
CAP = 128
N_SPACE = 32
DEVICES = 128


def scaled_rows(key, unit_values, floor_scale, spread, tilt):
    device_count = OBS // OBS_DEV
    block_index = (jnp.arange(OBS) // OBS_DEV).astype(jnp.float32)
    rise = jnp.sqrt(0.5 + tilt * block_index / max(device_count - 1, 1))
    level = jax.random.uniform(jax.random.fold_in(key, 7), (OBS,), jnp.float32)
    return unit_values * floor_scale * spread ** level * rise


def draw_direction(key, part):
    key = jax.random.fold_in(key, 11)
    unit_values = jnp.clip(jax.random.normal(key, (OBS,), jnp.float32), -4.0, 4.0)
    return scaled_rows(key, unit_values, 0.3, 10.0, 1.5)


def draw_residual_dual(key, part):
    key = jax.random.fold_in(key, 13)
    unit_values = jnp.clip(jax.random.normal(key, (OBS,), jnp.float32), -4.0, 4.0)
    return scaled_rows(key, unit_values, 0.3, 10.0, 1.5)


def draw_obs_interp(key, part):
    key = jax.random.fold_in(key, 17)
    fraction = jax.random.uniform(key, (2, OBS), jnp.float32)
    frac_x = fraction[0]
    frac_y = fraction[1]
    return jnp.stack([(1.0 - frac_x) * (1.0 - frac_y), frac_x * (1.0 - frac_y), (1.0 - frac_x) * frac_y, frac_x * frac_y])


def draw_obs_cell(key, part):
    key = jax.random.fold_in(key, 19)
    key_list = jax.random.split(key, 5)
    step_draw = jax.random.randint(key_list[0], (OBS,), 0, STEPS)
    variable_draw = jax.random.randint(key_list[1], (OBS,), 0, NV)
    level_draw = jax.random.randint(key_list[2], (OBS,), 0, LEV)
    x_draw = jax.random.randint(key_list[3], (OBS,), 0, CX - 1)
    y_draw = jax.random.randint(key_list[4], (OBS,), 0, NY - 1)
    cells = ((((step_draw * NV + variable_draw) * LEV + level_draw) * CX + x_draw) * NY + y_draw).astype(jnp.int32)
    top_cell = ((((STEPS - 1) * NV + NV - 1) * LEV + LEV - 1) * CX + CX - 2) * NY + NY - 2
    cells = cells.at[0].set(jnp.int32(top_cell))
    cells = cells.at[1].set(jnp.int32(0))
    return cells


def block_levels(key, dims, cuts, smallest, largest):
    def one(position, blocks):
        draws = jax.random.uniform(jax.random.fold_in(jax.random.fold_in(key, 6), position), (blocks,), jnp.float32, smallest / len(cuts), largest / len(cuts))
        return jnp.repeat(jnp.exp(draws), dims[position] // blocks).reshape((-1,) + (1,) * (len(dims) - position - 1))

    loudness = one(*cuts[0])
    for cut in cuts[1:]:
        loudness = loudness * one(*cut)
    return loudness


def routed_block(rng, own, number, rows, number_of, top, bound, skew):
    order = jax.random.permutation(rng, number_of)
    packed, usual = load_shares(number_of, rows * top, bound, skew, True), load_shares(number_of, rows * top, bound, skew, False)
    places = jnp.arange(number_of)

    def named(lengths, turn):
        used = int((lengths > 0).sum())
        fixed = max(1, used // 4)
        passed = fixed + (places - fixed + turn * (used - fixed)) % max(1, number_of - fixed)
        return jnp.zeros((number_of,), jnp.int32).at[order[jnp.where(places < fixed, places, passed)]].set(jnp.asarray(lengths, jnp.int32))

    lengths = jnp.where(number % 4 == 0, named(packed, number // 4), named(usual, number - number // 4 - 1))
    mixed = jax.random.permutation(jax.random.fold_in(own, 3), number_of)
    donor, sink = mixed[0:number_of // 2 * 2:2], mixed[1:number_of // 2 * 2:2]
    margin = jnp.minimum(lengths[donor] - 1, bound - lengths[sink]) // 2
    margin = jnp.where((donor == order[0]) | (sink == order[0]) | (lengths[sink] == 0), 0, jnp.maximum(margin, 0))
    passed = jax.random.randint(jax.random.fold_in(own, 4), (number_of // 2,), 0, 1 << 20) % (margin + 1)
    lengths = lengths.at[donor].add(-passed).at[sink].add(passed)
    items = jnp.searchsorted(jnp.cumsum(lengths), jnp.arange(rows * top), side="right").astype(jnp.int32)
    table = items.reshape(top, rows).T
    table = table[jax.random.permutation(jax.random.fold_in(own, 1), rows)]
    turn = jax.random.randint(jax.random.fold_in(own, 2), (rows, 1), 0, top)
    return jnp.take_along_axis(table, (jnp.arange(top)[None, :] + turn) % top, axis=1)


def load_shares(count, total, limit, skew, full):
    weights = [(1 << 20) // math.isqrt(rank ** skew) + 1 for rank in range(1, count + 1)]
    largest = limit if full else min(limit, max(-(-total // count), total * weights[0] // sum(weights)))
    least = 1 if total - largest >= count - 1 else 0
    holding, surplus = [largest] + [least] * (count - 1), total - largest - least * (count - 1)
    while surplus > 0:
        candidates = [i for i in range(1, count) if holding[i] < largest] or [i for i in range(1, count) if holding[i] < limit]
        whole, left = sum([weights[i] for i in candidates]), surplus
        for i in candidates:
            addition = min(limit - holding[i], max(1, left * weights[i] // whole), surplus)
            holding[i] = holding[i] + addition
            surplus = surplus - addition
    return np.array(holding)


def bell_draw(stream_key, dims, scale, reach, shards=(), held_as=jnp.bfloat16):
    array = scale * jax.random.normal(stream_key, dims, jnp.float32)
    if shards:
        array = array * block_levels(stream_key, dims, shards, -0.22, 0.18)
    return jnp.clip(array, -reach, reach).astype(held_as)


def setup_inputs(seed: int = 0) -> dict:
    seeds = jax.random.split(jax.random.key(seed), 12)
    dual_weights = bell_draw(seeds[0], (OBS,), 1.0, 6.0, ((0, 128),), jnp.float32)
    direction = draw_direction(jax.random.fold_in(seeds[11], 71), 0)
    residual_dual = draw_residual_dual(jax.random.fold_in(seeds[11], 71), 0)
    obs_var = jnp.clip(jnp.exp(math.log(1.0) - 1.609438 * jax.random.uniform(seeds[3], (OBS,), jnp.float32) ** block_levels(seeds[3], (OBS,), ((0, 128),), -0.2, 0.2)), 0.2, 1.0)
    obs_route_keys = jax.random.split(jax.random.fold_in(seeds[4], 1), OBS // OBS_DEV)
    obs_route_turns = jax.random.permutation(jax.random.fold_in(seeds[4], 3), OBS // OBS_DEV)
    obs_route = jax.vmap(lambda own, number: routed_block(jax.random.fold_in(seeds[4], 2), own, number, OBS_DEV, DEVICES, 1, CAP, 2))(obs_route_keys, obs_route_turns).reshape((OBS, 1))
    obs_cell = draw_obs_cell(jax.random.fold_in(seeds[11], 71), 0)
    obs_interp = draw_obs_interp(jax.random.fold_in(seeds[11], 71), 0)
    wind_x = jnp.clip(jax.random.uniform(seeds[7], (GROUPS, LEV, NX, NY), jnp.float32, -0.35, 0.35) * block_levels(seeds[7], (GROUPS, LEV, NX, NY), ((0, 4), (2, 32)), -0.4, 0.0), -0.35, 0.35)
    wind_y = jnp.clip(jax.random.uniform(seeds[8], (GROUPS, LEV, NX, NY), jnp.float32, -0.35, 0.35) * block_levels(seeds[8], (GROUPS, LEV, NX, NY), ((0, 4), (2, 32)), -0.4, 0.0), -0.35, 0.35)
    coupling = bell_draw(seeds[9], (NV, NV), NV ** -0.5, 3.0, (), jnp.float32)
    cov_scale = jnp.clip(jnp.exp(math.log(4.0) - 0.98082925 * jax.random.uniform(seeds[10], (GROUPS, NV, LEV), jnp.float32) ** block_levels(seeds[10], (GROUPS, NV, LEV), ((0, 4),), -0.2, 0.2)), 1.5, 4.0)
    return {"dual_weights": dual_weights, "direction": direction, "residual_dual": residual_dual, "obs_var": obs_var, "obs_route": obs_route, "obs_cell": obs_cell, "obs_interp": obs_interp, "wind_x": wind_x, "wind_y": wind_y, "coupling": coupling, "cov_scale": cov_scale}


diffusion = 0.05
vertical = 0.05
coupling_step = 0.05


def neighbour(grid_field, axis_no, offset):
    extent = grid_field.shape[axis_no]
    widths = [(1, 1) if dim_no == axis_no else (0, 0) for dim_no in range(grid_field.ndim)]
    padded = jnp.pad(grid_field, widths)
    return lax.slice_in_dim(padded, 1 + offset, 1 + offset + extent, axis=axis_no)


def coefficients(wind_east, wind_north):
    west_weight = jnp.maximum(wind_east, 0.0) + diffusion
    east_weight = jnp.maximum(-wind_east, 0.0) + diffusion
    south_weight = jnp.maximum(wind_north, 0.0) + diffusion
    north_weight = jnp.maximum(-wind_north, 0.0) + diffusion
    centre = 1.0 - jnp.abs(wind_east) - jnp.abs(wind_north) - 4.0 * diffusion - 2.0 * vertical
    return centre, west_weight, east_weight, south_weight, north_weight


def forward_step(model_state, weights_tuple, coupling):
    centre, west_weight, east_weight, south_weight, north_weight = weights_tuple
    result = centre * model_state + west_weight * neighbour(model_state, 2, -1) + east_weight * neighbour(model_state, 2, 1)
    result = result + south_weight * neighbour(model_state, 3, -1) + north_weight * neighbour(model_state, 3, 1)
    result = result + vertical * (neighbour(model_state, 1, -1) + neighbour(model_state, 1, 1))
    return result + coupling_step * jnp.einsum("vw,wlxy->vlxy", coupling, model_state, precision=lax.Precision.HIGHEST)


def adjoint_step(model_state, weights_tuple, coupling):
    centre, west_weight, east_weight, south_weight, north_weight = weights_tuple
    result = centre * model_state + neighbour(west_weight * model_state, 2, 1) + neighbour(east_weight * model_state, 2, -1)
    result = result + neighbour(south_weight * model_state, 3, 1) + neighbour(north_weight * model_state, 3, -1)
    result = result + vertical * (neighbour(model_state, 1, -1) + neighbour(model_state, 1, 1))
    return result + coupling_step * jnp.einsum("wv,wlxy->vlxy", coupling, model_state, precision=lax.Precision.HIGHEST)


def smooth(grid_field, axis_no):
    return 0.5 * grid_field + 0.25 * (neighbour(grid_field, axis_no, -1) + neighbour(grid_field, axis_no, 1))


def covariance(adjoint, scale_table):
    scales = scale_table[:, :, None, None]
    scaled = scales * adjoint
    scaled = smooth(smooth(scaled, 2), 2)
    scaled = smooth(smooth(scaled, 3), 3)
    return scales * scaled


def reference(dual_weights, direction, residual_dual, obs_var, obs_route, obs_cell, obs_interp, wind_x, wind_y, coupling, cov_scale):
    targets = obs_route[:, 0]
    obs_group = targets // N_SPACE
    tile_index = targets % N_SPACE
    y_corner = obs_cell % NY
    rest_part = obs_cell // NY
    x_corner = rest_part % CX
    upper_part = rest_part // CX
    base_cell = (upper_part * NX + tile_index * CX + x_corner) * NY + y_corner
    corner_index = jnp.concatenate([base_cell, base_cell + NY, base_cell + 1, base_cell + NY + 1]).astype(jnp.int32)
    corner_weight = obs_interp.reshape(-1)
    corner_group = jnp.concatenate([obs_group, obs_group, obs_group, obs_group])
    spread_direction = jnp.concatenate([direction, direction, direction, direction])
    cell_count = STEPS * NV * LEV * NX * NY
    adjoint = jnp.zeros((NV, LEV, NX, NY), jnp.float32)
    starts = [None] * GROUPS
    for section_index in reversed(range(GROUPS)):
        weights_tuple = coefficients(wind_x[section_index], wind_y[section_index])
        contrib = jnp.where(corner_group == section_index, corner_weight * spread_direction, 0.0)
        forcing = jnp.zeros((cell_count,), jnp.float32).at[corner_index].add(contrib)
        forcing = forcing.reshape(STEPS, NV, LEV, NX, NY)
        for step_index in reversed(range(STEPS)):
            adjoint = adjoint_step(adjoint + forcing[step_index], weights_tuple, coupling)
        starts[section_index] = adjoint
    model_state = jnp.zeros((NV, LEV, NX, NY), jnp.float32)
    mapped = jnp.zeros((OBS,), jnp.float32)
    for section_index in range(GROUPS):
        weights_tuple = coefficients(wind_x[section_index], wind_y[section_index])
        model_state = model_state + covariance(starts[section_index], cov_scale[section_index])
        trail = []
        for step_index in range(STEPS):
            model_state = forward_step(model_state, weights_tuple, coupling)
            trail.append(model_state)
        flat_states = jnp.stack(trail).reshape(-1)
        sampled = flat_states[corner_index].reshape(4, OBS)
        mapped_group = jnp.sum(obs_interp * sampled, axis=0)
        mapped = mapped + jnp.where(obs_group == section_index, mapped_group, 0.0)
    image = mapped + obs_var * direction
    norm_now = jnp.sum(residual_dual * residual_dual)
    curvature = jnp.sum(direction * image)
    step_size = norm_now / curvature
    dual_next = dual_weights + step_size * direction
    residual_next = residual_dual - step_size * image
    norm_next = jnp.sum(residual_next * residual_next)
    direction_next = residual_next + (norm_next / norm_now) * direction
    return dual_next, residual_next, direction_next
```

```python
import functools

import jax
import jax.numpy as jnp
from jax import lax
from jax.experimental import pallas as pl
from jax.experimental.pallas import tpu as pltpu
from jax.sharding import PartitionSpec as P

STEPS = 4
NV = 4
LEV = 16
CX = 8
NY = 256
CAP = 128
ROWS = LEV * CX
BUCKETS = STEPS * NV
SORT_ROWS = 160
CHUNK = 1024
SUB = 256
DELAY = 3
diffusion = 0.05
vertical = 0.05
coupling_step = 0.05
MESH = pl.DeviceIdType.MESH
F32 = jnp.float32
BF16 = jnp.bfloat16
VMEM = pl.BlockSpec(memory_space=pltpu.VMEM)
SMEM = pl.BlockSpec(memory_space=pltpu.SMEM)


def params(mib, **kw):
    return pltpu.CompilerParams(vmem_limit_bytes=mib * 1024 * 1024, **kw)


def iota(shape, dim):
    return lax.broadcasted_iota(jnp.int32, shape, dim)


def parts_of(value, count):
    out = []
    for _ in range(count - 1):
        head = value.astype(BF16)
        out.append(head)
        value = value - head.astype(F32)
    out.append(value.astype(BF16))
    return out


def nt(a, b):
    return lax.dot_general(a, b, (((1,), (1,)), ((), ())), preferred_element_type=F32)


def nn(a, b):
    return jnp.dot(a, b, preferred_element_type=F32)


def one_hot(mask):
    return jnp.where(mask, 1.0, 0.0).astype(BF16)


def running_rank(hot, hot_mask, carry, upper):
    keys = hot.shape[0]
    pieces = CHUNK // SUB
    stacked = jnp.concatenate([hot[:, i * SUB : (i + 1) * SUB] for i in range(pieces)], axis=0)
    counted = nn(stacked, upper)
    rows = []
    for i in range(pieces):
        mask = hot_mask[:, i * SUB : (i + 1) * SUB]
        part = counted[i * keys : (i + 1) * keys] + carry
        rows.append(jnp.sum(jnp.where(mask, part, 0.0), axis=0, keepdims=True))
        carry = carry + jnp.sum(jnp.where(mask, 1.0, 0.0), axis=1, keepdims=True)
    return jnp.concatenate(rows, axis=1), carry


def upper_strict():
    return one_hot(iota((SUB, SUB), 0) < iota((SUB, SUB), 1))


PACK_PARTS = (3, 2, 2, 2, 2, 2, 2, 2)


def pack_kernel(route_ref, field_ref, out_ref, rank_ref, acc_ref):
    devices = out_ref.shape[0]
    upper = upper_strict()
    acc_ref[...] = jnp.zeros_like(acc_ref)

    def body(c, carry):
        lanes = pl.ds(pl.multiple_of(c * CHUNK, CHUNK), CHUNK)
        dest = route_ref[:, lanes]
        mask = iota((devices, CHUNK), 0) == dest
        hot = one_hot(mask)
        rank, carry = running_rank(hot, mask, carry, upper)
        rank = rank.astype(jnp.int32)
        rank_ref[:, lanes] = rank
        slot = one_hot(iota((CAP, CHUNK), 0) == rank)
        fields = field_ref[:, lanes]
        pieces = []
        for f, count in enumerate(PACK_PARTS):
            for part in parts_of(fields[f : f + 1], count):
                pieces.append(slot * part)
        acc_ref[...] += nt(hot, jnp.concatenate(pieces, axis=0))
        return carry

    lax.fori_loop(0, route_ref.shape[1] // CHUNK, body, jnp.zeros((devices, 1), F32))
    at = 0
    for f, count in enumerate(PACK_PARTS):
        total = acc_ref[:, at * CAP : (at + 1) * CAP]
        for i in range(1, count):
            total = total + acc_ref[:, (at + i) * CAP : (at + i + 1) * CAP]
        at += count
        out_ref[:, f, :] = total


def row_of(ref, field, c):
    per = CHUNK // CAP
    base = c * per
    return jnp.concatenate([ref[base + i, field : field + 1, :] for i in range(per)], axis=1)


SORT_PARTS = 12


def sort_scatter_kernel(recv_ref, forcing_ref, sorted_ref, pos_ref, start_ref, rank_ref, acc_ref):
    chunks = recv_ref.shape[0] * CAP // CHUNK
    upper = upper_strict()

    def bucket_of(c):
        cell = row_of(recv_ref, 0, c).astype(jnp.int32) - 1
        bucket = jnp.where(cell < 0, -1, cell // (ROWS * NY))
        return cell, iota((BUCKETS, CHUNK), 0) == bucket

    def count_body(c, carry):
        _, mask = bucket_of(c)
        rank, carry = running_rank(one_hot(mask), mask, carry, upper)
        rank_ref[pl.ds(c, 1), :] = rank
        return carry

    totals = lax.fori_loop(0, chunks, count_body, jnp.zeros((BUCKETS, 1), F32))
    tiles = jnp.floor((totals + (SUB - 1.0)) * (1.0 / SUB))
    before = jnp.zeros((BUCKETS, 1), F32)
    ids = iota((BUCKETS, 1), 0)
    for b in range(BUCKETS):
        here = jnp.sum(jnp.where(ids == b, tiles, 0.0))
        before = before + jnp.where(ids > b, here, 0.0)
    for b in range(BUCKETS):
        start_ref[0, b] = jnp.sum(jnp.where(ids == b, before, 0.0)).astype(jnp.int32)
    start_ref[0, BUCKETS] = jnp.sum(tiles).astype(jnp.int32)
    offsets = before * float(SUB)

    acc_ref[...] = jnp.zeros_like(acc_ref)

    def sort_body(c, carry):
        cell, mask = bucket_of(c)
        offset = jnp.sum(jnp.where(mask, offsets, 0.0), axis=0, keepdims=True)
        pos = (offset + rank_ref[pl.ds(c, 1), :]).astype(jnp.int32)
        pos = jnp.where(cell < 0, -1, pos)
        pos_ref[pl.ds(c, 1), :] = pos
        high = one_hot(iota((SORT_ROWS, CHUNK), 0) == (pos >> 7))
        low = one_hot(iota((CAP, CHUNK), 0) == (pos & 127))
        inside = (cell & (ROWS * NY - 1)).astype(F32)
        pieces = []
        for value in [inside] + [row_of(recv_ref, f, c) for f in range(1, 6)]:
            for part in parts_of(value, 2):
                pieces.append(low * part)
        acc_ref[...] += nt(high, jnp.concatenate(pieces, axis=0))
        return carry

    lax.fori_loop(0, chunks, sort_body, 0)
    for f in range(SORT_PARTS // 2):
        sorted_ref[f] = (
            acc_ref[:, 2 * f * CAP : (2 * f + 1) * CAP]
            + acc_ref[:, (2 * f + 1) * CAP : (2 * f + 2) * CAP]
        )

    def bucket_body(b, carry):
        def tile_body(t, total):
            def row(f):
                return jnp.concatenate(
                    [sorted_ref[f, pl.ds(2 * t, 1), :], sorted_ref[f, pl.ds(2 * t + 1, 1), :]],
                    axis=1,
                )

            cell = row(0).astype(jnp.int32)
            hot = one_hot(iota((ROWS, SUB), 0) == (cell >> 8))
            y = cell & (NY - 1)
            spots = iota((NY, SUB), 0)
            here = one_hot(spots == y)
            above = one_hot(spots == y + 1)
            d = row(5)
            w = [parts_of(row(1 + i) * d, 2) for i in range(4)]
            stacked = jnp.concatenate(
                [
                    jnp.concatenate([here * w[0][p] + above * w[2][p] for p in range(2)], axis=1),
                    jnp.concatenate([here * w[1][p] + above * w[3][p] for p in range(2)], axis=1),
                ],
                axis=0,
            )
            return total + nt(jnp.concatenate([hot, hot], axis=1), stacked)

        total = lax.fori_loop(
            start_ref[0, b], start_ref[0, b + 1], tile_body, jnp.zeros((ROWS, 2 * NY), F32)
        )
        forcing_ref[b] = total[:, :NY] + pltpu.roll(total[:, NY:], 1, 0)
        return carry

    lax.fori_loop(0, BUCKETS, bucket_body, 0)


def gather_kernel(
    start_ref, state_ref, sorted_ref, pos_ref, recv_ref, own_ref, out_ref, value_ref
):
    devices = recv_ref.shape[0]
    chunks = devices * CAP // CHUNK
    value_ref[...] = jnp.zeros_like(value_ref)

    def bucket_body(b, carry):
        turned = state_ref[b].T
        shifted = pltpu.roll(turned, ROWS - 1, 1)
        table = jnp.concatenate(
            [
                jnp.concatenate(parts_of(turned, 2), axis=1),
                jnp.concatenate(parts_of(shifted, 2), axis=1),
            ],
            axis=0,
        )

        def tile_body(t, carry):
            def row(f):
                return jnp.concatenate(
                    [sorted_ref[f, pl.ds(2 * t, 1), :], sorted_ref[f, pl.ds(2 * t + 1, 1), :]],
                    axis=1,
                )

            cell = row(0).astype(jnp.int32)
            hot = one_hot(iota((ROWS, SUB), 0) == (cell >> 8))
            y = cell & (NY - 1)
            spots = iota((NY, SUB), 0)
            here = spots == y
            above = spots == y + 1
            got = nn(table, jnp.concatenate([hot, hot], axis=0))
            first = jnp.where(here, row(1), jnp.where(above, row(3), 0.0))
            second = jnp.where(here, row(2), jnp.where(above, row(4), 0.0))
            value = jnp.sum(first * got[:NY] + second * got[NY:], axis=0, keepdims=True)
            value_ref[pl.ds(2 * t, 1), :] = value[:, :CAP]
            value_ref[pl.ds(2 * t + 1, 1), :] = value[:, CAP:]
            return carry

        return lax.fori_loop(start_ref[0, b], start_ref[0, b + 1], tile_body, carry)

    lax.fori_loop(0, BUCKETS, bucket_body, 0)
    table = jnp.concatenate(parts_of(value_ref[...].T, 2), axis=1)
    depth = value_ref.shape[0]

    def unsort_body(c, carry):
        pos = pos_ref[pl.ds(c, 1), :]
        high = one_hot(iota((depth, CHUNK), 0) == (pos >> 7))
        got = nn(table, jnp.concatenate([high, high], axis=0))
        low = iota((CAP, CHUNK), 0) == (pos & 127)
        row = jnp.sum(jnp.where(low, got, 0.0), axis=0, keepdims=True)
        per = CHUNK // CAP
        block = jnp.concatenate([row[:, i * CAP : (i + 1) * CAP] for i in range(per)], axis=0)
        out_ref[pl.ds(pl.multiple_of(c * per, per), per), :CAP] = block
        return carry

    lax.fori_loop(0, chunks, unsort_body, 0)
    d = recv_ref[:, 5, :]
    r = recv_ref[:, 6, :]
    image = out_ref[:, :CAP] + recv_ref[:, 7, :] * d
    out_ref[:, :CAP] = image
    own = own_ref[...]
    lane = iota((1, CAP), 1)
    sums = jnp.where(lane == 0, jnp.sum(own * own), 0.0)
    sums = jnp.where(lane == 1, jnp.sum(d * image), sums)
    sums = jnp.where(lane == 2, jnp.sum(r * image), sums)
    sums = jnp.where(lane == 3, jnp.sum(image * image), sums)
    out_ref[:, CAP:] = jnp.broadcast_to(sums, (devices, CAP))


def final_kernel(
    back_ref, route_ref, rank_ref, dual_ref, d_ref, r_ref, dual_out, res_out, dir_out
):
    devices = back_ref.shape[0]
    sums = jnp.sum(back_ref[:, CAP:], axis=0, keepdims=True)
    lane = iota((1, CAP), 1)
    norm_now, curvature, cross, square = [
        jnp.sum(jnp.where(lane == i, sums, 0.0), axis=1, keepdims=True) for i in range(4)
    ]
    step = norm_now / curvature
    norm_next = norm_now - 2.0 * step * cross + step * step * square
    ratio = norm_next / norm_now
    table = jnp.concatenate(parts_of(back_ref[:, :CAP].T, 2), axis=1)
    for c in range(route_ref.shape[0]):
        hot = one_hot(iota((devices, CHUNK), 0) == route_ref[c : c + 1, :])
        got = nn(table, jnp.concatenate([hot, hot], axis=0))
        mask = iota((CAP, CHUNK), 0) == rank_ref[c : c + 1, :]
        image = jnp.sum(jnp.where(mask, got, 0.0), axis=0, keepdims=True)
        d = d_ref[c : c + 1, :]
        res = r_ref[c : c + 1, :] - step * image
        dual_out[c : c + 1, :] = dual_ref[c : c + 1, :] + step * d
        res_out[c : c + 1, :] = res
        dir_out[c : c + 1, :] = res + ratio * d


EXT = CX + 8


def pack_four(dst, value, lo):
    for v in range(NV):
        dst[v // 2, (v % 2) * 4 : (v % 2) * 4 + 4, :] = value[v][lo : lo + 4]


def pack_two(dst, value, lo):
    for v in range(NV):
        dst[2 * v : 2 * v + 2, :] = value[v][lo : lo + 2]


def sweep_kernel(
    forcing_ref,
    wind_ref,
    coupling_ref,
    scale_ref,
    state_ref,
    wind_in,
    coef,
    hop_a,
    hop_x,
    fin_a,
    fin_x,
    halo_out,
    halo_in,
    cov_out,
    cov_in,
    fwd_out,
    fwd_in,
    fext,
    u0,
    u1,
    u2,
    u3,
    inc,
    wind_sem,
    hop_sem,
    halo_sem,
    cov_sem,
    fwd_sem,
):
    g = lax.axis_index("tm")
    t = lax.axis_index("space")
    groups = lax.axis_size("tm")
    strips = lax.axis_size("space")
    left = (g, lax.rem(t + strips - 1, strips))
    right = (g, lax.rem(t + 1, strips))
    later = (lax.rem(g + 1, groups), t)
    earlier = (lax.rem(g + groups - 1, groups), t)
    sides = (left, right)
    first_strip = t == 0
    last_strip = t == strips - 1
    last_group = g == groups - 1
    first_group = g == 0

    barrier = pltpu.get_barrier_semaphore()
    for other in (left, right, later, earlier):
        pl.semaphore_signal(barrier, inc=1, device_id=other, device_id_type=MESH)
    pl.semaphore_wait(barrier, 4)

    def to_side(src, dst, sems, side, *idx):
        return pltpu.make_async_remote_copy(
            src_ref=src,
            dst_ref=dst,
            send_sem=sems.at[(0, side) + idx],
            recv_sem=sems.at[(1, 1 - side) + idx],
            device_id=sides[side],
            device_id_type=MESH,
        )

    def wait_side(dst, sems, slot, *idx):
        pltpu.make_async_remote_copy(
            src_ref=dst,
            dst_ref=dst,
            send_sem=sems.at[(0, slot) + idx],
            recv_sem=sems.at[(1, slot) + idx],
            device_id=sides[slot],
            device_id_type=MESH,
        ).wait_recv()

    def hop(src, dst, way, level, device):
        return pltpu.make_async_remote_copy(
            src_ref=src.at[level],
            dst_ref=dst.at[level],
            send_sem=hop_sem.at[way, 0, level],
            recv_sem=hop_sem.at[way, 1, level],
            device_id=device,
            device_id_type=MESH,
        )

    for side in range(2):
        to_side(wind_ref, wind_in.at[1 - side], wind_sem, side).start()

    edge = jnp.zeros((NV, EXT, NY), F32)
    for u in (u0, u1, u2, u3):
        u[0] = edge
        u[LEV + 1] = edge

    @pl.when(last_group)
    def _():
        hop_a[...] = jnp.zeros_like(hop_a)

    @pl.when(first_group)
    def _():
        hop_x[...] = jnp.zeros_like(hop_x)

    for slot in range(2):
        wait_side(wind_in.at[slot], wind_sem, slot)

    column = iota((EXT, NY), 0)
    lane = iota((EXT, NY), 1)
    low_x = jnp.where(first_strip, 4, 0)
    high_x = jnp.where(last_strip, 11, 15)
    inside = (column >= low_x) & (column <= high_x)
    west_ok = inside & ((column > 4) | jnp.logical_not(first_strip))
    east_ok = inside & ((column < 11) | jnp.logical_not(last_strip))
    south_ok = inside & (lane > 0)
    north_ok = inside & (lane < NY - 1)

    def coef_body(l, carry):
        winds = []
        for i in range(2):
            winds.append(
                jnp.concatenate(
                    [wind_in[0, i, l, 4:8], wind_ref[i, l], wind_in[1, i, l, 0:4]], axis=0
                )
            )
        wx, wy = winds
        coef[0, l] = jnp.where(
            inside, 1.0 - jnp.abs(wx) - jnp.abs(wy) - 4.0 * diffusion - 2.0 * vertical, 0.0
        )
        coef[1, l] = jnp.where(west_ok, jnp.maximum(wx, 0.0) + diffusion, 0.0)
        coef[2, l] = jnp.where(east_ok, jnp.maximum(-wx, 0.0) + diffusion, 0.0)
        coef[3, l] = jnp.where(south_ok, jnp.maximum(wy, 0.0) + diffusion, 0.0)
        coef[4, l] = jnp.where(north_ok, jnp.maximum(-wy, 0.0) + diffusion, 0.0)
        return carry

    lax.fori_loop(0, LEV, coef_body, 0)

    mix = [[coupling_step * coupling_ref[v, w] for w in range(NV)] for v in range(NV)]

    def adjoint_level(u, l):
        c, w, e, s, n = [coef[i, l] for i in range(5)]
        now = [u[l + 1, v] for v in range(NV)]
        out = []
        for v in range(NV):
            a = now[v]
            res = c * a + pltpu.roll(w * a, EXT - 1, 0) + pltpu.roll(e * a, 1, 0)
            res = res + pltpu.roll(s * a, NY - 1, 1) + pltpu.roll(n * a, 1, 1)
            res = res + vertical * (u[l, v] + u[l + 2, v])
            for k in range(NV):
                res = res + mix[k][v] * now[k]
            out.append(res)
        return out

    def forward_level(u, l):
        c, w, e, s, n = [coef[i, l] for i in range(5)]
        now = [u[l + 1, v] for v in range(NV)]
        out = []
        for v in range(NV):
            a = now[v]
            res = c * a + w * pltpu.roll(a, 1, 0) + e * pltpu.roll(a, EXT - 1, 0)
            res = res + s * pltpu.roll(a, 1, 1) + n * pltpu.roll(a, NY - 1, 1)
            res = res + vertical * (u[l, v] + u[l + 2, v])
            for k in range(NV):
                res = res + mix[v][k] * now[k]
            out.append(res)
        return out

    def in_range(l):
        return (l >= 0) & (l < LEV)

    def adjoint_tick(k, carry):
        @pl.when(k < LEV)
        def _():
            @pl.when(jnp.logical_not(last_group))
            def _():
                hop(hop_a, hop_a, 0, k, later).wait_recv()

            value = [hop_a[k, v] + forcing_ref[3, v, k] for v in range(NV)]
            for v in range(NV):
                u0[k + 1, v, 4 : 4 + CX] = value[v]
            for side in range(2):
                lo = 4 * side
                buf = halo_out.at[side, k]
                pack_four(buf.at[0:2], value, lo)
                pack_four(buf.at[2:4], [forcing_ref[2, v, k] for v in range(NV)], lo)
                lo = 6 * side
                pack_two(buf.at[4], [forcing_ref[1, v, k] for v in range(NV)], lo)
                pack_two(buf.at[5], [forcing_ref[0, v, k] for v in range(NV)], lo)
                to_side(buf, halo_in.at[1 - side, k], halo_sem, side, k).start()

        m = k - DELAY

        @pl.when(in_range(m))
        def _():
            for slot in range(2):
                wait_side(halo_in.at[slot, m], halo_sem, slot, m)
            for v in range(NV):
                rows = slice((v % 2) * 4, (v % 2) * 4 + 4)
                pair = slice(2 * v, 2 * v + 2)
                u0[m + 1, v, 0:4] = halo_in[0, m, v // 2, rows]
                u0[m + 1, v, 12:16] = halo_in[1, m, v // 2, rows]
                fext[2, m, v, 0:4] = halo_in[0, m, 2 + v // 2, rows]
                fext[2, m, v, 12:16] = halo_in[1, m, 2 + v // 2, rows]
                fext[2, m, v, 4:12] = forcing_ref[2, v, m]
                for i, tile in ((1, 4), (0, 5)):
                    fext[i, m, v, 0:2] = jnp.zeros((2, NY), F32)
                    fext[i, m, v, 14:16] = jnp.zeros((2, NY), F32)
                    fext[i, m, v, 2:4] = halo_in[0, m, tile, pair]
                    fext[i, m, v, 12:14] = halo_in[1, m, tile, pair]
                    fext[i, m, v, 4:12] = forcing_ref[i, v, m]

        for i, (src, dst) in enumerate(((u0, u1), (u1, u2), (u2, u3))):
            level = m - 1 - i

            @pl.when(in_range(level))
            def _():
                res = adjoint_level(src, level)
                for v in range(NV):
                    dst[level + 1, v] = res[v] + fext[2 - i, level, v]

        level = m - 4

        @pl.when(in_range(level))
        def _():
            res = [r[4 : 4 + CX] for r in adjoint_level(u3, level)]
            for v in range(NV):
                fin_a[level, v] = res[v]

            @pl.when(jnp.logical_not(first_group))
            def _():
                hop(fin_a, hop_a, 0, level, earlier).start()

            for side in range(2):
                pack_two(cov_out.at[side, level], res, 6 * side)
                to_side(
                    cov_out.at[side, level], cov_in.at[1 - side, level], cov_sem, side, level
                ).start()

        return carry

    lax.fori_loop(0, LEV + DELAY + 4, adjoint_tick, 0)

    lane_low = jnp.where(iota((CX, NY), 1) > 0, 1.0, 0.0)
    lane_high = jnp.where(iota((CX, NY), 1) < NY - 1, 1.0, 0.0)
    keep = jnp.where(inside, 1.0, 0.0)

    def cov_level(l, carry):
        for slot in range(2):
            wait_side(cov_in.at[slot, l], cov_sem, slot, l)
        zero = jnp.zeros((2, NY), F32)
        for v in range(NV):
            pair = slice(2 * v, 2 * v + 2)
            scale = scale_ref[v, l]
            ext = jnp.concatenate(
                [zero, cov_in[0, l, pair], fin_a[l, v], cov_in[1, l, pair], zero], axis=0
            )
            ext = ext * (keep * scale)
            ext = 0.5 * ext + 0.25 * (pltpu.roll(ext, 1, 0) + pltpu.roll(ext, EXT - 1, 0))
            ext = ext * keep
            ext = 0.5 * ext + 0.25 * (pltpu.roll(ext, 1, 0) + pltpu.roll(ext, EXT - 1, 0))
            own = ext[4 : 4 + CX]
            for _ in range(2):
                own = 0.5 * own + 0.25 * (
                    lane_low * pltpu.roll(own, 1, 1) + lane_high * pltpu.roll(own, NY - 1, 1)
                )
            inc[l, v] = own * scale
        return carry

    lax.fori_loop(0, LEV, cov_level, 0)

    def forward_tick(k, carry):
        @pl.when(k < LEV)
        def _():
            @pl.when(jnp.logical_not(first_group))
            def _():
                hop(hop_x, hop_x, 1, k, earlier).wait_recv()

            value = [hop_x[k, v] + inc[k, v] for v in range(NV)]
            for v in range(NV):
                u0[k + 1, v, 4 : 4 + CX] = value[v]
            for side in range(2):
                buf = fwd_out.at[side, k]
                pack_four(buf, value, 4 * side)
                to_side(buf, fwd_in.at[1 - side, k], fwd_sem, side, k).start()

        m = k - DELAY

        @pl.when(in_range(m))
        def _():
            for slot in range(2):
                wait_side(fwd_in.at[slot, m], fwd_sem, slot, m)
            for v in range(NV):
                rows = slice((v % 2) * 4, (v % 2) * 4 + 4)
                u0[m + 1, v, 0:4] = fwd_in[0, m, v // 2, rows]
                u0[m + 1, v, 12:16] = fwd_in[1, m, v // 2, rows]

        for i, (src, dst) in enumerate(((u0, u1), (u1, u2), (u2, u3))):
            level = m - 1 - i

            @pl.when(in_range(level))
            def _():
                res = forward_level(src, level)
                for v in range(NV):
                    dst[level + 1, v] = res[v]
                    state_ref[i, v, level] = res[v][4 : 4 + CX]

        level = m - 4

        @pl.when(in_range(level))
        def _():
            res = [r[4 : 4 + CX] for r in forward_level(u3, level)]
            for v in range(NV):
                state_ref[3, v, level] = res[v]
                fin_x[level, v] = res[v]

            @pl.when(jnp.logical_not(last_group))
            def _():
                hop(fin_x, hop_x, 1, level, later).start()

        return carry

    lax.fori_loop(0, LEV + DELAY + 4, forward_tick, 0)

    for side in range(2):
        to_side(wind_ref, wind_in.at[1 - side], wind_sem, side).wait_send()

    def drain(l, carry):
        for side in range(2):
            to_side(halo_out.at[side, l], halo_in.at[1 - side, l], halo_sem, side, l).wait_send()
            to_side(cov_out.at[side, l], cov_in.at[1 - side, l], cov_sem, side, l).wait_send()
            to_side(fwd_out.at[side, l], fwd_in.at[1 - side, l], fwd_sem, side, l).wait_send()

        @pl.when(jnp.logical_not(first_group))
        def _():
            hop(fin_a, hop_a, 0, l, earlier).wait_send()

        @pl.when(jnp.logical_not(last_group))
        def _():
            hop(fin_x, hop_x, 1, l, later).wait_send()

        return carry

    lax.fori_loop(0, LEV, drain, 0)


def sweeps(forcing, winds, coupling, scale):
    state = (LEV, NV, CX, NY)
    padded = (LEV + 2, NV, EXT, NY)
    dma = pltpu.SemaphoreType.DMA
    return pl.pallas_call(
        sweep_kernel,
        out_shape=jax.ShapeDtypeStruct((STEPS, NV, LEV, CX, NY), F32),
        in_specs=[VMEM, VMEM, SMEM, SMEM],
        out_specs=VMEM,
        scratch_shapes=[
            pltpu.VMEM((2, 2, LEV, CX, NY), F32),
            pltpu.VMEM((5, LEV, EXT, NY), F32),
            pltpu.VMEM(state, F32),
            pltpu.VMEM(state, F32),
            pltpu.VMEM(state, F32),
            pltpu.VMEM(state, F32),
            pltpu.VMEM((2, LEV, 6, 8, NY), F32),
            pltpu.VMEM((2, LEV, 6, 8, NY), F32),
            pltpu.VMEM((2, LEV, 8, NY), F32),
            pltpu.VMEM((2, LEV, 8, NY), F32),
            pltpu.VMEM((2, LEV, 2, 8, NY), F32),
            pltpu.VMEM((2, LEV, 2, 8, NY), F32),
            pltpu.VMEM((3, LEV, NV, EXT, NY), F32),
            pltpu.VMEM(padded, F32),
            pltpu.VMEM(padded, F32),
            pltpu.VMEM(padded, F32),
            pltpu.VMEM(padded, F32),
            pltpu.VMEM(state, F32),
            dma((2, 2)),
            dma((2, 2, LEV)),
            dma((2, 2, LEV)),
            dma((2, 2, LEV)),
            dma((2, 2, LEV)),
        ],
        compiler_params=params(48, collective_id=1, has_side_effects=True),
        name="sweeps",
    )(forcing, winds, coupling, scale)


def per_device(
    dual_weights,
    direction,
    residual_dual,
    obs_var,
    obs_route,
    obs_cell,
    obs_interp,
    wind_x,
    wind_y,
    coupling,
    cov_scale,
):
    devices = lax.axis_size("tm") * lax.axis_size("space")
    rows = direction.shape[0]
    wide = (rows // CHUNK, CHUNK)
    route = obs_route.reshape(1, rows)
    fields = jnp.concatenate(
        [
            (obs_cell + 1).astype(F32)[None],
            obs_interp,
            direction[None],
            residual_dual[None],
            obs_var[None],
        ],
        axis=0,
    )
    outgoing, rank = pl.pallas_call(
        pack_kernel,
        out_shape=(
            jax.ShapeDtypeStruct((devices, 8, CAP), F32),
            jax.ShapeDtypeStruct((1, rows), jnp.int32),
        ),
        in_specs=[VMEM, VMEM],
        out_specs=(VMEM, VMEM),
        scratch_shapes=[pltpu.VMEM((devices, sum(PACK_PARTS) * CAP), F32)],
        compiler_params=params(48),
        name="pack",
    )(route, fields)
    arrived = lax.all_to_all(outgoing, ("tm", "space"), split_axis=0, concat_axis=0, tiled=True)
    slots = devices * CAP
    forcing, ordered, position, starts = pl.pallas_call(
        sort_scatter_kernel,
        out_shape=(
            jax.ShapeDtypeStruct((BUCKETS, ROWS, NY), F32),
            jax.ShapeDtypeStruct((SORT_PARTS // 2, SORT_ROWS, CAP), F32),
            jax.ShapeDtypeStruct((slots // CHUNK, CHUNK), jnp.int32),
            jax.ShapeDtypeStruct((1, BUCKETS + 1), jnp.int32),
        ),
        in_specs=[VMEM],
        out_specs=(VMEM, VMEM, VMEM, SMEM),
        scratch_shapes=[
            pltpu.VMEM((slots // CHUNK, CHUNK), F32),
            pltpu.VMEM((SORT_ROWS, SORT_PARTS * CAP), F32),
        ],
        compiler_params=params(48),
        name="sort_scatter",
    )(arrived)
    winds = jnp.concatenate([wind_x, wind_y], axis=0)
    states = sweeps(
        forcing.reshape(STEPS, NV, LEV, CX, NY), winds, coupling, cov_scale[0]
    )
    returning = pl.pallas_call(
        gather_kernel,
        out_shape=jax.ShapeDtypeStruct((devices, 2 * CAP), F32),
        in_specs=[SMEM, VMEM, VMEM, VMEM, VMEM, VMEM],
        out_specs=VMEM,
        scratch_shapes=[pltpu.VMEM((256, CAP), F32)],
        compiler_params=params(48),
        name="gather",
    )(
        starts,
        states.reshape(BUCKETS, ROWS, NY),
        ordered,
        position,
        arrived,
        residual_dual.reshape(wide),
    )
    back = lax.all_to_all(returning, ("tm", "space"), split_axis=0, concat_axis=0, tiled=True)
    out = jax.ShapeDtypeStruct(wide, F32)
    results = pl.pallas_call(
        final_kernel,
        out_shape=(out, out, out),
        in_specs=[VMEM] * 6,
        out_specs=(VMEM, VMEM, VMEM),
        compiler_params=params(48),
        name="final",
    )(
        back,
        route.reshape(wide),
        rank.reshape(wide),
        dual_weights.reshape(wide),
        direction.reshape(wide),
        residual_dual.reshape(wide),
    )
    return tuple(r.reshape(rows) for r in results)


def solution(mesh):
    return jax.shard_map(
        per_device,
        mesh=mesh,
        in_specs=(
            P(("tm", "space")),
            P(("tm", "space")),
            P(("tm", "space")),
            P(("tm", "space")),
            P(("tm", "space"), None),
            P(("tm", "space")),
            P(None, ("tm", "space")),
            P("tm", None, "space", None),
            P("tm", None, "space", None),
            P(),
            P("tm", None, None),
        ),
        out_specs=(P(("tm", "space")), P(("tm", "space")), P(("tm", "space"))),
        check_vma=False,
    )
```

```python
import functools

import jax
import jax.numpy as jnp
from jax import lax
from jax.experimental import pallas as pl
from jax.experimental.pallas import tpu as pltpu
from jax.sharding import PartitionSpec as P

STEPS = 4
NV = 4
LEV = 16
CX = 8
NY = 256
CAP = 128
ROWS = LEV * CX
BUCKETS = STEPS * NV
SORT_ROWS = 160
CHUNK = 1024
SUB = 256
HALF = NY // 2
EXT = 2 * CX
ADJ_DELAY = 5
COV_DELAY = 5
FWD_DELAY = 5
FIRST_DELAY = 5
diffusion = 0.05
vertical = 0.05
coupling_step = 0.05
MESH = pl.DeviceIdType.MESH
F32 = jnp.float32
BF16 = jnp.bfloat16
VMEM = pl.BlockSpec(memory_space=pltpu.VMEM)
SMEM = pl.BlockSpec(memory_space=pltpu.SMEM)


def params(mib, **kw):
    return pltpu.CompilerParams(vmem_limit_bytes=mib * 1024 * 1024, **kw)


def iota(shape, dim):
    return lax.broadcasted_iota(jnp.int32, shape, dim)


def parts_of(value, count):
    out = []
    for _ in range(count - 1):
        head = value.astype(BF16)
        out.append(head)
        value = value - head.astype(F32)
    out.append(value.astype(BF16))
    return out


def nt(a, b):
    return lax.dot_general(a, b, (((1,), (1,)), ((), ())), preferred_element_type=F32)


def nn(a, b):
    return jnp.dot(a, b, preferred_element_type=F32)


def one_hot(mask):
    return jnp.where(mask, 1.0, 0.0).astype(BF16)


def running_rank(hot, hot_mask, carry, upper):
    keys = hot.shape[0]
    pieces = CHUNK // SUB
    stacked = jnp.concatenate([hot[:, i * SUB : (i + 1) * SUB] for i in range(pieces)], axis=0)
    counted = nn(stacked, upper)
    rows = []
    for i in range(pieces):
        mask = hot_mask[:, i * SUB : (i + 1) * SUB]
        part = counted[i * keys : (i + 1) * keys] + carry
        rows.append(jnp.sum(jnp.where(mask, part, 0.0), axis=0, keepdims=True))
        carry = carry + jnp.sum(jnp.where(mask, 1.0, 0.0), axis=1, keepdims=True)
    return jnp.concatenate(rows, axis=1), carry


def lane_of(y):
    return (y >> 1) + (y & 1) * HALF


def upper_strict():
    return one_hot(iota((SUB, SUB), 0) < iota((SUB, SUB), 1))


PACK_PARTS = (3, 2, 2, 2, 2, 2, 2, 2)


def everyone(me, act):
    g = lax.axis_index("tm")
    t = lax.axis_index("space")
    groups = lax.axis_size("tm")
    strips = lax.axis_size("space")
    for step in range(groups):
        group = g + step
        group = jnp.where(group >= groups, group - groups, group)

        def body(i, carry):
            strip = t + i
            strip = jnp.where(strip >= strips, strip - strips, strip)
            act(group * strips + strip, (group, strip))
            return carry

        lax.fori_loop(0 if step else 1, strips, body, 0, unroll=True)


def greet_all(me):
    barrier = pltpu.get_barrier_semaphore()
    everyone(
        me,
        lambda peer, device: pl.semaphore_signal(
            barrier, inc=1, device_id=device, device_id_type=MESH
        ),
    )


def await_all():
    devices = lax.axis_size("tm") * lax.axis_size("space")
    pl.semaphore_wait(pltpu.get_barrier_semaphore(), devices - 1)


def send_all(me, out, arrived, send_sem, recv_sem):
    def start(peer, device):
        pltpu.make_async_remote_copy(
            src_ref=out.at[peer],
            dst_ref=arrived.at[me],
            send_sem=send_sem,
            recv_sem=recv_sem,
            device_id=device,
            device_id_type=MESH,
        ).start()

    pltpu.make_async_copy(out.at[me], arrived.at[me], recv_sem).start()
    everyone(me, start)


def receive_all(arrived, recv_sem):
    pltpu.make_async_copy(arrived, arrived, recv_sem).wait()


def finish_sends(out, send_sem):
    rest = out.at[pl.ds(0, out.shape[0] - 1)]
    pltpu.make_async_copy(rest, rest, send_sem).wait()


def my_index():
    return lax.axis_index("tm") * lax.axis_size("space") + lax.axis_index("space")


def route_kernel(
    route_ref,
    field_ref,
    wind_ref,
    arrived_ref,
    rank_ref,
    coef,
    out_ref,
    landing,
    acc_ref,
    wind_own,
    wind_in,
    send_sem,
    recv_sem,
    wind_sem,
):
    me = my_index()
    g = lax.axis_index("tm")
    t = lax.axis_index("space")
    strips = lax.axis_size("space")
    sides = ((g, lax.rem(t + strips - 1, strips)), (g, lax.rem(t + 1, strips)))
    first_strip = t == 0
    last_strip = t == strips - 1
    greet_all(me)

    order = iota((NY, NY), 1)
    order = one_hot(iota((NY, NY), 0) == (order % HALF) * 2 + order // HALF)
    rows = 2 * LEV * CX
    turned = parts_of(wind_ref[...].reshape(rows, NY), 3)
    wind_own[...] = (nn(turned[0], order) + nn(turned[1], order) + nn(turned[2], order)).reshape(
        2, LEV, CX, NY
    )

    devices = out_ref.shape[0]
    upper = upper_strict()
    acc_ref[...] = jnp.zeros_like(acc_ref)

    def body(c, carry):
        lanes = pl.ds(pl.multiple_of(c * CHUNK, CHUNK), CHUNK)
        dest = route_ref[:, lanes]
        mask = iota((devices, CHUNK), 0) == dest
        hot = one_hot(mask)
        rank, carry = running_rank(hot, mask, carry, upper)
        rank = rank.astype(jnp.int32)
        rank_ref[:, lanes] = rank
        slot = one_hot(iota((CAP, CHUNK), 0) == rank)
        fields = field_ref[:, lanes]
        pieces = []
        for f, count in enumerate(PACK_PARTS):
            for part in parts_of(fields[f : f + 1], count):
                pieces.append(slot * part)
        acc_ref[...] += nt(hot, jnp.concatenate(pieces, axis=0))
        return carry

    lax.fori_loop(0, route_ref.shape[1] // CHUNK, body, jnp.zeros((devices, 1), F32))
    at = 0
    for f, count in enumerate(PACK_PARTS):
        total = acc_ref[:, at * CAP : (at + 1) * CAP]
        for i in range(1, count):
            total = total + acc_ref[:, (at + i) * CAP : (at + i + 1) * CAP]
        at += count
        out_ref[:, f, :] = total

    await_all()

    def to_side(side):
        return pltpu.make_async_remote_copy(
            src_ref=wind_own,
            dst_ref=wind_in.at[1 - side],
            send_sem=wind_sem.at[0, side],
            recv_sem=wind_sem.at[1, 1 - side],
            device_id=sides[side],
            device_id_type=MESH,
        )

    send_all(me, out_ref, landing, send_sem, recv_sem)
    for side in range(2):
        to_side(side).start()
    for side in range(2):
        to_side(side).wait_recv()

    column = iota((EXT, NY), 0)
    lane = iota((EXT, NY), 1)
    west_ok = jnp.logical_not(first_strip & (column == 0))
    east_ok = jnp.logical_not(last_strip & (column == CX - 1))
    inside = inside_grid(first_strip, last_strip)
    west_ok = inside & west_ok
    east_ok = inside & east_ok
    south_ok = inside & (lane > 0)
    north_ok = inside & (lane < NY - 1)
    from_right = iota((CX, NY), 0) < 4

    def coef_body(l, carry):
        wx, wy = [
            jnp.concatenate(
                [wind_own[i, l], jnp.where(from_right, wind_in[1, i, l], wind_in[0, i, l])], axis=0
            )
            for i in range(2)
        ]
        coef[0, l] = jnp.where(
            inside, 1.0 - jnp.abs(wx) - jnp.abs(wy) - 4.0 * diffusion - 2.0 * vertical, 0.0
        )
        coef[1, l] = jnp.where(west_ok, jnp.maximum(wx, 0.0) + diffusion, 0.0)
        coef[2, l] = jnp.where(east_ok, jnp.maximum(-wx, 0.0) + diffusion, 0.0)
        coef[3, l] = jnp.where(south_ok, jnp.maximum(wy, 0.0) + diffusion, 0.0)
        coef[4, l] = jnp.where(north_ok, jnp.maximum(-wy, 0.0) + diffusion, 0.0)
        return carry

    lax.fori_loop(0, LEV, coef_body, 0)
    receive_all(landing, recv_sem)
    arrived_ref[...] = landing[...]
    for side in range(2):
        to_side(side).wait_send()
    finish_sends(out_ref, send_sem)


def inside_grid(first_strip, last_strip):
    column = iota((EXT, NY), 0)
    return jnp.logical_not(
        (first_strip & (column >= 12)) | (last_strip & (column >= 8) & (column < 12))
    )


def row_of(ref, field, c):
    per = CHUNK // CAP
    base = c * per
    return jnp.concatenate([ref[base + i, field : field + 1, :] for i in range(per)], axis=1)


SORT_PARTS = 12


def sort_scatter_kernel(recv_ref, forcing_ref, sorted_ref, pos_ref, start_ref, rank_ref, acc_ref):
    chunks = recv_ref.shape[0] * CAP // CHUNK
    upper = upper_strict()

    def bucket_of(c):
        cell = row_of(recv_ref, 0, c).astype(jnp.int32) - 1
        bucket = jnp.where(cell < 0, -1, cell // (ROWS * NY))
        return cell, iota((BUCKETS, CHUNK), 0) == bucket

    def count_body(c, carry):
        _, mask = bucket_of(c)
        rank, carry = running_rank(one_hot(mask), mask, carry, upper)
        rank_ref[pl.ds(c, 1), :] = rank
        return carry

    totals = lax.fori_loop(0, chunks, count_body, jnp.zeros((BUCKETS, 1), F32))
    tiles = jnp.floor((totals + (SUB - 1.0)) * (1.0 / SUB))
    before = jnp.zeros((BUCKETS, 1), F32)
    ids = iota((BUCKETS, 1), 0)
    for b in range(BUCKETS):
        here = jnp.sum(jnp.where(ids == b, tiles, 0.0))
        before = before + jnp.where(ids > b, here, 0.0)
    for b in range(BUCKETS):
        start_ref[0, b] = jnp.sum(jnp.where(ids == b, before, 0.0)).astype(jnp.int32)
    start_ref[0, BUCKETS] = jnp.sum(tiles).astype(jnp.int32)
    offsets = before * float(SUB)

    acc_ref[...] = jnp.zeros_like(acc_ref)

    def sort_body(c, carry):
        cell, mask = bucket_of(c)
        offset = jnp.sum(jnp.where(mask, offsets, 0.0), axis=0, keepdims=True)
        pos = (offset + rank_ref[pl.ds(c, 1), :]).astype(jnp.int32)
        pos = jnp.where(cell < 0, -1, pos)
        pos_ref[pl.ds(c, 1), :] = pos
        high = one_hot(iota((SORT_ROWS, CHUNK), 0) == (pos >> 7))
        low = one_hot(iota((CAP, CHUNK), 0) == (pos & 127))
        inside = (cell & (ROWS * NY - 1)).astype(F32)
        pieces = []
        for value in [inside] + [row_of(recv_ref, f, c) for f in range(1, 6)]:
            for part in parts_of(value, 2):
                pieces.append(low * part)
        acc_ref[...] += nt(high, jnp.concatenate(pieces, axis=0))
        return carry

    lax.fori_loop(0, chunks, sort_body, 0)
    for f in range(SORT_PARTS // 2):
        sorted_ref[f] = (
            acc_ref[:, 2 * f * CAP : (2 * f + 1) * CAP]
            + acc_ref[:, (2 * f + 1) * CAP : (2 * f + 2) * CAP]
        )

    def bucket_body(b, carry):
        def tile_body(t, total):
            def row(f):
                return jnp.concatenate(
                    [sorted_ref[f, pl.ds(2 * t, 1), :], sorted_ref[f, pl.ds(2 * t + 1, 1), :]],
                    axis=1,
                )

            cell = row(0).astype(jnp.int32)
            hot = one_hot(iota((ROWS, SUB), 0) == (cell >> 8))
            y = cell & (NY - 1)
            spots = iota((NY, SUB), 0)
            here = one_hot(spots == lane_of(y))
            above = one_hot(spots == lane_of(y + 1))
            d = row(5)
            w = [parts_of(row(1 + i) * d, 2) for i in range(4)]
            stacked = jnp.concatenate(
                [
                    jnp.concatenate([here * w[0][p] + above * w[2][p] for p in range(2)], axis=1),
                    jnp.concatenate([here * w[1][p] + above * w[3][p] for p in range(2)], axis=1),
                ],
                axis=0,
            )
            return total + nt(jnp.concatenate([hot, hot], axis=1), stacked)

        total = lax.fori_loop(
            start_ref[0, b], start_ref[0, b + 1], tile_body, jnp.zeros((ROWS, 2 * NY), F32)
        )
        forcing_ref[b] = total[:, :NY] + pltpu.roll(total[:, NY:], 1, 0)
        return carry

    lax.fori_loop(0, BUCKETS, bucket_body, 0)


def gather_kernel(
    start_ref, state_ref, sorted_ref, pos_ref, recv_ref, own_ref, out_ref, value_ref
):
    devices = recv_ref.shape[0]
    chunks = devices * CAP // CHUNK
    value_ref[...] = jnp.zeros_like(value_ref)

    def bucket_body(b, carry):
        turned = state_ref[b].T
        shifted = pltpu.roll(turned, ROWS - 1, 1)
        table = jnp.concatenate(
            [
                jnp.concatenate(parts_of(turned, 2), axis=1),
                jnp.concatenate(parts_of(shifted, 2), axis=1),
            ],
            axis=0,
        )

        def tile_body(t, carry):
            def row(f):
                return jnp.concatenate(
                    [sorted_ref[f, pl.ds(2 * t, 1), :], sorted_ref[f, pl.ds(2 * t + 1, 1), :]],
                    axis=1,
                )

            cell = row(0).astype(jnp.int32)
            hot = one_hot(iota((ROWS, SUB), 0) == (cell >> 8))
            y = cell & (NY - 1)
            spots = iota((NY, SUB), 0)
            here = spots == lane_of(y)
            above = spots == lane_of(y + 1)
            got = nn(table, jnp.concatenate([hot, hot], axis=0))
            first = jnp.where(here, row(1), jnp.where(above, row(3), 0.0))
            second = jnp.where(here, row(2), jnp.where(above, row(4), 0.0))
            value = jnp.sum(first * got[:NY] + second * got[NY:], axis=0, keepdims=True)
            value_ref[pl.ds(2 * t, 1), :] = value[:, :CAP]
            value_ref[pl.ds(2 * t + 1, 1), :] = value[:, CAP:]
            return carry

        return lax.fori_loop(start_ref[0, b], start_ref[0, b + 1], tile_body, carry)

    lax.fori_loop(0, BUCKETS, bucket_body, 0)
    table = jnp.concatenate(parts_of(value_ref[...].T, 2), axis=1)
    depth = value_ref.shape[0]

    def unsort_body(c, carry):
        pos = pos_ref[pl.ds(c, 1), :]
        high = one_hot(iota((depth, CHUNK), 0) == (pos >> 7))
        got = nn(table, jnp.concatenate([high, high], axis=0))
        low = iota((CAP, CHUNK), 0) == (pos & 127)
        row = jnp.sum(jnp.where(low, got, 0.0), axis=0, keepdims=True)
        per = CHUNK // CAP
        block = jnp.concatenate([row[:, i * CAP : (i + 1) * CAP] for i in range(per)], axis=0)
        out_ref[pl.ds(pl.multiple_of(c * per, per), per), :CAP] = block
        return carry

    lax.fori_loop(0, chunks, unsort_body, 0)
    d = recv_ref[:, 5, :]
    r = recv_ref[:, 6, :]
    image = out_ref[:, :CAP] + recv_ref[:, 7, :] * d
    out_ref[:, :CAP] = image
    own = own_ref[...]
    lane = iota((1, CAP), 1)
    sums = jnp.where(lane == 0, jnp.sum(own * own), 0.0)
    sums = jnp.where(lane == 1, jnp.sum(d * image), sums)
    sums = jnp.where(lane == 2, jnp.sum(r * image), sums)
    sums = jnp.where(lane == 3, jnp.sum(image * image), sums)
    out_ref[:, CAP:] = jnp.broadcast_to(sums, (devices, CAP))


def final_kernel(
    out_ref,
    route_ref,
    rank_ref,
    dual_ref,
    d_ref,
    r_ref,
    dual_out,
    res_out,
    dir_out,
    landing,
    send_sem,
    recv_sem,
):
    devices = out_ref.shape[0]
    me = my_index()
    greet_all(me)
    await_all()
    send_all(me, out_ref, landing, send_sem, recv_sem)
    receive_all(landing, recv_sem)
    returned = landing[...].reshape(devices, 2 * CAP)
    sums = jnp.sum(returned[:, CAP:], axis=0, keepdims=True)
    lane = iota((1, CAP), 1)
    norm_now, curvature, cross, square = [
        jnp.sum(jnp.where(lane == i, sums, 0.0), axis=1, keepdims=True) for i in range(4)
    ]
    step = norm_now / curvature
    norm_next = norm_now - 2.0 * step * cross + step * step * square
    ratio = norm_next / norm_now
    table = jnp.concatenate(parts_of(returned[:, :CAP].T, 2), axis=1)
    for c in range(route_ref.shape[0]):
        hot = one_hot(iota((devices, CHUNK), 0) == route_ref[c : c + 1, :])
        got = nn(table, jnp.concatenate([hot, hot], axis=0))
        mask = iota((CAP, CHUNK), 0) == rank_ref[c : c + 1, :]
        image = jnp.sum(jnp.where(mask, got, 0.0), axis=0, keepdims=True)
        d = d_ref[c : c + 1, :]
        res = r_ref[c : c + 1, :] - step * image
        dual_out[c : c + 1, :] = dual_ref[c : c + 1, :] + step * d
        res_out[c : c + 1, :] = res
        dir_out[c : c + 1, :] = res + ratio * d
    finish_sends(out_ref, send_sem)


def back(x):
    return jnp.concatenate([pltpu.roll(x[:, HALF:], 1, 1), x[:, :HALF]], axis=1)


def ahead(x):
    return jnp.concatenate([x[:, HALF:], pltpu.roll(x[:, :HALF], HALF - 1, 1)], axis=1)


def sweep_kernel(
    forcing_ref,
    coef,
    coupling_ref,
    scale_ref,
    state_ref,
    hop_a,
    hop_x,
    fin_a,
    fin_x,
    adj_out,
    adj_in,
    force_out,
    force_in,
    cov_out,
    cov_in,
    fwd_out,
    fwd_in,
    fext,
    u0,
    u1,
    u2,
    u3,
    v0,
    v1,
    v2,
    v3,
    inc,
    hop_sem,
    adj_sem,
    force_sem,
    cov_sem,
    fwd_sem,
):
    g = lax.axis_index("tm")
    t = lax.axis_index("space")
    groups = lax.axis_size("tm")
    strips = lax.axis_size("space")
    left = (g, lax.rem(t + strips - 1, strips))
    right = (g, lax.rem(t + 1, strips))
    later = (lax.rem(g + 1, groups), t)
    earlier = (lax.rem(g + groups - 1, groups), t)
    sides = (left, right)
    first_strip = t == 0
    last_strip = t == strips - 1
    last_group = g == groups - 1
    first_group = g == 0

    barrier = pltpu.get_barrier_semaphore()
    for other in (left, right, later, earlier):
        pl.semaphore_signal(barrier, inc=1, device_id=other, device_id_type=MESH)

    pl.semaphore_wait(barrier, 4)

    def to_side(src, dst, sems, side, *idx):
        return pltpu.make_async_remote_copy(
            src_ref=src,
            dst_ref=dst,
            send_sem=sems.at[(0, side) + idx],
            recv_sem=sems.at[(1, 1 - side) + idx],
            device_id=sides[side],
            device_id_type=MESH,
        )

    def wait_side(dst, sems, slot, *idx):
        pltpu.make_async_remote_copy(
            src_ref=dst,
            dst_ref=dst,
            send_sem=sems.at[(0, slot) + idx],
            recv_sem=sems.at[(1, slot) + idx],
            device_id=sides[slot],
            device_id_type=MESH,
        ).wait_recv()

    def hop(src, dst, way, level, device):
        return pltpu.make_async_remote_copy(
            src_ref=src.at[level],
            dst_ref=dst.at[level],
            send_sem=hop_sem.at[way, 0, level],
            recv_sem=hop_sem.at[way, 1, level],
            device_id=device,
            device_id_type=MESH,
        )

    upper = iota((CX, NY), 0) < 4

    def pack(out, level, first, value):
        for j in range(NV // 2):
            one = value[2 * j]
            two = pltpu.roll(value[2 * j + 1], 4, 0)
            out[0, level, first + j] = jnp.where(upper, one, two)
            out[1, level, first + j] = jnp.where(upper, two, one)

    def join(arrived, level, first):
        tiles = []
        for j in range(NV // 2):
            from_left = arrived[0, level, first + j]
            from_right = arrived[1, level, first + j]
            tiles.append(jnp.where(upper, from_right, from_left))
            tiles.append(pltpu.roll(jnp.where(upper, from_left, from_right), 4, 0))
        return tiles

    def exchange(out, arrived, sems, level):
        for side in range(2):
            to_side(
                out.at[side, level], arrived.at[1 - side, level], sems, side, level
            ).start()

    def await_sides(arrived, sems, level):
        for slot in range(2):
            wait_side(arrived.at[slot, level], sems, slot, level)

    def send_forcing(l):
        for i in range(3):
            pack(force_out, l, 2 * i, [forcing_ref[i, v, l] for v in range(NV)])
        exchange(force_out, force_in, force_sem, l)

    edge = jnp.zeros((NV, EXT, NY), F32)
    for u in (u0, u1, u2, u3, v0, v1, v2, v3):
        u[0] = edge
        u[LEV + 1] = edge

    @pl.when(last_group)
    def _():
        hop_a[...] = jnp.zeros_like(hop_a)

    @pl.when(first_group)
    def _():
        hop_x[...] = jnp.zeros_like(hop_x)

    @pl.when(jnp.logical_not(last_group))
    def _():
        def early(l, carry):
            send_forcing(l)
            return carry

        lax.fori_loop(0, LEV, early, 0)

    inside = inside_grid(first_strip, last_strip)
    mix = [[coupling_step * coupling_ref[v, w] for w in range(NV)] for v in range(NV)]

    def adjoint_level(u, l, rows):
        c, w, e, s, n = [coef[i, l] for i in range(5)]
        now = [u[l + 1, v] for v in range(NV)]
        out = []
        for v in range(NV):
            a = now[v]
            res = c[:rows] * a[:rows]
            res = res + pltpu.roll(w * a, EXT - 1, 0)[:rows] + pltpu.roll(e * a, 1, 0)[:rows]
            res = res + ahead(s[:rows] * a[:rows]) + back(n[:rows] * a[:rows])
            res = res + vertical * (u[l, v, :rows] + u[l + 2, v, :rows])
            for k in range(NV):
                res = res + mix[k][v] * now[k][:rows]
            out.append(res)
        return out

    def forward_level(u, l, rows):
        c, w, e, s, n = [coef[i, l][:rows] for i in range(5)]
        now = [u[l + 1, v] for v in range(NV)]
        out = []
        for v in range(NV):
            a = now[v]
            res = c * a[:rows]
            res = res + w * pltpu.roll(a, 1, 0)[:rows] + e * pltpu.roll(a, EXT - 1, 0)[:rows]
            res = res + s * back(a[:rows]) + n * ahead(a[:rows])
            res = res + vertical * (u[l, v, :rows] + u[l + 2, v, :rows])
            for k in range(NV):
                res = res + mix[v][k] * now[k][:rows]
            out.append(res)
        return out

    def in_range(l):
        return (l >= 0) & (l < LEV)

    def adjoint_tick(k):
        @pl.when(in_range(k))
        def _():
            @pl.when(jnp.logical_not(last_group))
            def _():
                hop(hop_a, hop_a, 0, k, later).wait_recv()

            value = [hop_a[k, v] + forcing_ref[3, v, k] for v in range(NV)]
            pack(adj_out, k, 0, value)
            exchange(adj_out, adj_in, adj_sem, k)

            @pl.when(last_group)
            def _():
                send_forcing(k)

            for v in range(NV):
                u0[k + 1, v, :CX] = value[v]

        m = k - ADJ_DELAY

        @pl.when(in_range(m))
        def _():
            await_sides(adj_in, adj_sem, m)
            await_sides(force_in, force_sem, m)
            for v, tile in enumerate(join(adj_in, m, 0)):
                u0[m + 1, v, CX:] = tile
            for i in range(3):
                for v, tile in enumerate(join(force_in, m, 2 * i)):
                    fext[i, m, v] = tile

        for i, (src, dst) in enumerate(((u0, u1), (u1, u2), (u2, u3))):
            level = m - 1 - i

            @pl.when(in_range(level))
            def _():
                res = adjoint_level(src, level, EXT)
                for v in range(NV):
                    dst[level + 1, v, :CX] = res[v][:CX] + forcing_ref[2 - i, v, level]
                    dst[level + 1, v, CX:] = res[v][CX:] + fext[2 - i, level, v]

        level = m - 4

        @pl.when(in_range(level))
        def _():
            res = adjoint_level(u3, level, CX)
            for v in range(NV):
                fin_a[level, v] = res[v]

            @pl.when(jnp.logical_not(first_group))
            def _():
                hop(fin_a, hop_a, 0, level, earlier).start()

            pack(cov_out, level, 0, res)
            exchange(cov_out, cov_in, cov_sem, level)

    lane_low = jnp.where(iota((CX, NY), 1) > 0, 1.0, 0.0)
    lane_high = jnp.where(iota((CX, NY), 1) < NY - 1, 1.0, 0.0)
    keep = jnp.where(inside, 1.0, 0.0)

    def cov_tick(l):
        @pl.when(in_range(l))
        def _():
            await_sides(cov_in, cov_sem, l)
            for v, tile in enumerate(join(cov_in, l, 0)):
                scale = scale_ref[v, l]
                ext = jnp.concatenate([fin_a[l, v], tile], axis=0) * (keep * scale)
                ext = 0.5 * ext + 0.25 * (pltpu.roll(ext, 1, 0) + pltpu.roll(ext, EXT - 1, 0))
                ext = ext * keep
                ext = 0.5 * ext + 0.25 * (pltpu.roll(ext, 1, 0) + pltpu.roll(ext, EXT - 1, 0))
                own = ext[:CX]
                for _ in range(2):
                    own = 0.5 * own + 0.25 * (lane_low * back(own) + lane_high * ahead(own))
                inc[l, v] = own * scale

    fwd_delay = jnp.where(first_group, FIRST_DELAY, FWD_DELAY)

    def forward_tick(k):
        @pl.when(in_range(k))
        def _():
            @pl.when(jnp.logical_not(first_group))
            def _():
                hop(hop_x, hop_x, 1, k, earlier).wait_recv()

            value = [hop_x[k, v] + inc[k, v] for v in range(NV)]
            pack(fwd_out, k, 0, value)
            exchange(fwd_out, fwd_in, fwd_sem, k)
            for v in range(NV):
                v0[k + 1, v, :CX] = value[v]

        m = k - fwd_delay

        @pl.when(in_range(m))
        def _():
            await_sides(fwd_in, fwd_sem, m)
            for v, tile in enumerate(join(fwd_in, m, 0)):
                v0[m + 1, v, CX:] = tile

        for i, (src, dst) in enumerate(((v0, v1), (v1, v2), (v2, v3))):
            level = m - 1 - i

            @pl.when(in_range(level))
            def _():
                res = forward_level(src, level, EXT)
                for v in range(NV):
                    dst[level + 1, v] = res[v]
                    state_ref[i, v, level] = res[v][:CX]

        level = m - 4

        @pl.when(in_range(level))
        def _():
            res = forward_level(v3, level, CX)
            for v in range(NV):
                state_ref[3, v, level] = res[v]
                fin_x[level, v] = res[v]

            @pl.when(jnp.logical_not(last_group))
            def _():
                hop(fin_x, hop_x, 1, level, later).start()

    adjoint_ticks = LEV + ADJ_DELAY + 4
    behind = jnp.where(first_group, ADJ_DELAY + 4 + COV_DELAY, adjoint_ticks)

    def tick(k, carry):
        adjoint_tick(k)
        cov_tick(k - (ADJ_DELAY + 4 + COV_DELAY))
        forward_tick(k - behind)
        return carry

    lax.fori_loop(0, behind + LEV + fwd_delay + 4, tick, 0)

    def drain(l, carry):
        for out, arrived, sems in (
            (adj_out, adj_in, adj_sem),
            (force_out, force_in, force_sem),
            (cov_out, cov_in, cov_sem),
            (fwd_out, fwd_in, fwd_sem),
        ):
            for side in range(2):
                to_side(
                    out.at[side, l], arrived.at[1 - side, l], sems, side, l
                ).wait_send()

        @pl.when(jnp.logical_not(first_group))
        def _():
            hop(fin_a, hop_a, 0, l, earlier).wait_send()

        @pl.when(jnp.logical_not(last_group))
        def _():
            hop(fin_x, hop_x, 1, l, later).wait_send()

        return carry

    lax.fori_loop(0, LEV, drain, 0)


def sweeps(forcing, coef, coupling, scale):
    state = pltpu.VMEM((LEV, NV, CX, NY), F32)
    padded = pltpu.VMEM((LEV + 2, NV, EXT, NY), F32)
    edges = pltpu.VMEM((2, LEV, 2, CX, NY), F32)
    wide_edges = pltpu.VMEM((2, LEV, 6, CX, NY), F32)
    levels = pltpu.SemaphoreType.DMA((2, 2, LEV))
    return pl.pallas_call(
        sweep_kernel,
        out_shape=jax.ShapeDtypeStruct((STEPS, NV, LEV, CX, NY), F32),
        in_specs=[VMEM, VMEM, SMEM, SMEM],
        out_specs=VMEM,
        scratch_shapes=[state] * 4
        + [edges] * 2
        + [wide_edges] * 2
        + [edges] * 4
        + [pltpu.VMEM((3, LEV, NV, CX, NY), F32)]
        + [padded] * 8
        + [state]
        + [levels] * 5,
        compiler_params=params(34, collective_id=1, has_side_effects=True),
        name="sweeps",
    )(forcing, coef, coupling, scale)


def per_device(
    dual_weights,
    direction,
    residual_dual,
    obs_var,
    obs_route,
    obs_cell,
    obs_interp,
    wind_x,
    wind_y,
    coupling,
    cov_scale,
):
    devices = lax.axis_size("tm") * lax.axis_size("space")
    rows = direction.shape[0]
    wide = (rows // CHUNK, CHUNK)
    route = obs_route.reshape(1, rows)
    fields = jnp.concatenate(
        [
            (obs_cell + 1).astype(F32)[None],
            obs_interp,
            direction[None],
            residual_dual[None],
            obs_var[None],
        ],
        axis=0,
    )
    winds = jnp.concatenate([wind_x, wind_y], axis=0)
    tiles = pltpu.VMEM((devices, 8, CAP), F32)
    arrived, rank, coef = pl.pallas_call(
        route_kernel,
        out_shape=(
            jax.ShapeDtypeStruct((devices, 8, CAP), F32),
            jax.ShapeDtypeStruct((1, rows), jnp.int32),
            jax.ShapeDtypeStruct((5, LEV, EXT, NY), F32),
        ),
        in_specs=[VMEM, VMEM, VMEM],
        out_specs=(VMEM, VMEM, VMEM),
        scratch_shapes=[
            tiles,
            tiles,
            pltpu.VMEM((devices, sum(PACK_PARTS) * CAP), F32),
            pltpu.VMEM((2, LEV, CX, NY), F32),
            pltpu.VMEM((2, 2, LEV, CX, NY), F32),
            pltpu.SemaphoreType.DMA,
            pltpu.SemaphoreType.DMA,
            pltpu.SemaphoreType.DMA((2, 2)),
        ],
        compiler_params=params(20, collective_id=2, has_side_effects=True),
        name="route",
    )(route, fields, winds)
    slots = devices * CAP
    forcing, ordered, position, starts = pl.pallas_call(
        sort_scatter_kernel,
        out_shape=(
            jax.ShapeDtypeStruct((BUCKETS, ROWS, NY), F32),
            jax.ShapeDtypeStruct((SORT_PARTS // 2, SORT_ROWS, CAP), F32),
            jax.ShapeDtypeStruct((slots // CHUNK, CHUNK), jnp.int32),
            jax.ShapeDtypeStruct((1, BUCKETS + 1), jnp.int32),
        ),
        in_specs=[VMEM],
        out_specs=(VMEM, VMEM, VMEM, SMEM),
        scratch_shapes=[
            pltpu.VMEM((slots // CHUNK, CHUNK), F32),
            pltpu.VMEM((SORT_ROWS, SORT_PARTS * CAP), F32),
        ],
        compiler_params=params(20),
        name="sort_scatter",
    )(arrived)
    states = sweeps(forcing.reshape(STEPS, NV, LEV, CX, NY), coef, coupling, cov_scale[0])
    returning = pl.pallas_call(
        gather_kernel,
        out_shape=jax.ShapeDtypeStruct((devices, 2 * CAP), F32),
        in_specs=[SMEM, VMEM, VMEM, VMEM, VMEM, VMEM],
        out_specs=VMEM,
        scratch_shapes=[pltpu.VMEM((256, CAP), F32)],
        compiler_params=params(20),
        name="gather",
    )(
        starts,
        states.reshape(BUCKETS, ROWS, NY),
        ordered,
        position,
        arrived,
        residual_dual.reshape(wide),
    )
    out = jax.ShapeDtypeStruct(wide, F32)
    results = pl.pallas_call(
        final_kernel,
        out_shape=(out, out, out),
        in_specs=[VMEM] * 6,
        out_specs=(VMEM, VMEM, VMEM),
        scratch_shapes=[
            pltpu.VMEM((devices, 1, 2 * CAP), F32),
            pltpu.SemaphoreType.DMA,
            pltpu.SemaphoreType.DMA,
        ],
        compiler_params=params(12, collective_id=3, has_side_effects=True),
        name="final",
    )(
        returning.reshape(devices, 1, 2 * CAP),
        route.reshape(wide),
        rank.reshape(wide),
        dual_weights.reshape(wide),
        direction.reshape(wide),
        residual_dual.reshape(wide),
    )
    return tuple(r.reshape(rows) for r in results)


def solution(mesh):
    return jax.shard_map(
        per_device,
        mesh=mesh,
        in_specs=(
            P(("tm", "space")),
            P(("tm", "space")),
            P(("tm", "space")),
            P(("tm", "space")),
            P(("tm", "space"), None),
            P(("tm", "space")),
            P(None, ("tm", "space")),
            P("tm", None, "space", None),
            P("tm", None, "space", None),
            P(),
            P("tm", None, None),
        ),
        out_specs=(P(("tm", "space")), P(("tm", "space")), P(("tm", "space"))),
        check_vma=False,
    )
```

```python
import functools

import jax
import jax.numpy as jnp
from jax import lax
from jax.experimental import pallas as pl
from jax.experimental.pallas import tpu as pltpu
from jax.sharding import PartitionSpec as P

STEPS = 4
NV = 4
LEV = 16
CX = 8
NY = 256
CAP = 128
ROWS = LEV * CX
BUCKETS = STEPS * NV
SORT_ROWS = 160
CHUNK = 1024
SUB = 256
HALF = NY // 2
EXT = 2 * CX
ADJ_DELAY = 4
COV_DELAY = 4
FWD_DELAY = 4
FIRST_DELAY = 4
diffusion = 0.05
vertical = 0.05
coupling_step = 0.05
MESH = pl.DeviceIdType.MESH
F32 = jnp.float32
BF16 = jnp.bfloat16
VMEM = pl.BlockSpec(memory_space=pltpu.VMEM)
SMEM = pl.BlockSpec(memory_space=pltpu.SMEM)
ANY = pl.BlockSpec(memory_space=pltpu.HBM)


def params(mib, **kw):
    return pltpu.CompilerParams(vmem_limit_bytes=mib * 1024 * 1024, **kw)


def iota(shape, dim):
    return lax.broadcasted_iota(jnp.int32, shape, dim)


def parts_of(value, count):
    out = []
    for _ in range(count - 1):
        head = value.astype(BF16)
        out.append(head)
        value = value - head.astype(F32)
    out.append(value.astype(BF16))
    return out


def nt(a, b):
    return lax.dot_general(a, b, (((1,), (1,)), ((), ())), preferred_element_type=F32)


def nn(a, b):
    return jnp.dot(a, b, preferred_element_type=F32)


def one_hot(mask):
    return jnp.where(mask, 1.0, 0.0).astype(BF16)


def short_hot(ids, row):
    same = ids.astype(jnp.int16) == row.astype(jnp.int16)
    return jnp.where(same, jnp.ones((), BF16), jnp.zeros((), BF16))


def running_rank(hot, hot_mask, carry, upper):
    keys = hot.shape[0]
    pieces = CHUNK // SUB
    stacked = jnp.concatenate([hot[:, i * SUB : (i + 1) * SUB] for i in range(pieces)], axis=0)
    counted = nn(stacked, upper)
    rows = []
    for i in range(pieces):
        mask = hot_mask[:, i * SUB : (i + 1) * SUB]
        part = counted[i * keys : (i + 1) * keys] + carry
        rows.append(jnp.sum(jnp.where(mask, part, 0.0), axis=0, keepdims=True))
        carry = carry + jnp.sum(jnp.where(mask, 1.0, 0.0), axis=1, keepdims=True)
    return jnp.concatenate(rows, axis=1), carry


def lane_of(y):
    return (y >> 1) + (y & 1) * HALF


def upper_strict():
    return one_hot(iota((SUB, SUB), 0) < iota((SUB, SUB), 1))


PACK_PARTS = (3, 2, 2, 2, 2, 2, 2)


ROW_STRIPS = 8


def backwards(within):
    return ROW_STRIPS - 2 - within + 2 * (within % 2)


def strip_of(t):
    row = t // ROW_STRIPS
    within = t % ROW_STRIPS
    return row * ROW_STRIPS + jnp.where(row % 2 == 1, backwards(within), within)


def around(start, step, size):
    index = start + step
    return jnp.where(index >= size, index - size, index)


def everyone(act):
    g = lax.axis_index("tm")
    t = lax.axis_index("space")
    groups = lax.axis_size("tm")
    rows = lax.axis_size("space") // ROW_STRIPS
    ways = []
    for step in range(ROW_STRIPS):
        within = around(t % ROW_STRIPS, step, ROW_STRIPS)
        ways.append((within, backwards(within)))
    for group_step in range(groups):
        group = around(g, group_step, groups)
        for row_step in range(rows):
            row = around(t // ROW_STRIPS, row_step, rows)
            first = row * ROW_STRIPS
            odd = row % 2 == 1
            for step, (within, turned) in enumerate(ways):
                if group_step or row_step or step:
                    act(group, first + within, first + jnp.where(odd, turned, within))


def greet_all():
    barrier = pltpu.get_barrier_semaphore()
    everyone(
        lambda group, place, strip: pl.semaphore_signal(
            barrier, inc=1, device_id=(group, place), device_id_type=MESH
        )
    )


def await_all():
    devices = lax.axis_size("tm") * lax.axis_size("space")
    pl.semaphore_wait(pltpu.get_barrier_semaphore(), devices - 1)


def send_all(me, out, arrived, send_sem, recv_sem):
    strips = lax.axis_size("space")

    def start(group, place, strip):
        pltpu.make_async_remote_copy(
            src_ref=out.at[group * strips + strip],
            dst_ref=arrived.at[me],
            send_sem=send_sem,
            recv_sem=recv_sem,
            device_id=(group, place),
            device_id_type=MESH,
        ).start()

    own = lax.axis_index("tm") * strips + strip_of(lax.axis_index("space"))
    pltpu.make_async_copy(out.at[own], arrived.at[me], recv_sem).start()
    everyone(start)


def receive_all(arrived, recv_sem):
    pltpu.make_async_copy(arrived, arrived, recv_sem).wait()


def finish_sends(out, send_sem):
    rest = out.at[pl.ds(0, out.shape[0] - 1)]
    pltpu.make_async_copy(rest, rest, send_sem).wait()


def my_index():
    return lax.axis_index("tm") * lax.axis_size("space") + lax.axis_index("space")


def route_kernel(
    route_hbm,
    cell_hbm,
    interp_hbm,
    d_hbm,
    r_hbm,
    var_hbm,
    wind_x_hbm,
    wind_y_hbm,
    arrived_ref,
    rank_ref,
    coef,
    out_ref,
    landing,
    acc_ref,
    wind_own,
    wind_in,
    route_ref,
    cell_ref,
    interp_ref,
    d_ref,
    r_ref,
    var_ref,
    wind_x_ref,
    wind_y_ref,
    send_sem,
    recv_sem,
    wind_sem,
    fetch_sem,
):
    fetches = [
        pltpu.make_async_copy(src, dst, fetch_sem.at[i])
        for i, (src, dst) in enumerate(
            (
                (wind_x_hbm, wind_x_ref),
                (wind_y_hbm, wind_y_ref),
                (route_hbm, route_ref),
                (cell_hbm, cell_ref),
                (interp_hbm, interp_ref),
                (d_hbm, d_ref),
                (r_hbm, r_ref),
                (var_hbm, var_ref),
            )
        )
    ]
    for fetch in fetches:
        fetch.start()
    me = my_index()
    g = lax.axis_index("tm")
    t = lax.axis_index("space")
    strips = lax.axis_size("space")
    strip = strip_of(t)
    stays = strip == t
    first_strip = strip == 0
    last_strip = strip == strips - 1
    greet_all()
    for fetch in fetches:
        fetch.wait()

    order = iota((NY, NY), 1)
    order = one_hot(iota((NY, NY), 0) == (order % HALF) * 2 + order // HALF)
    for i, wind in enumerate((wind_x_ref, wind_y_ref)):
        turned = parts_of(wind[...].reshape(LEV * CX, NY), 3)
        turned = nn(turned[0], order) + nn(turned[1], order) + nn(turned[2], order)
        wind_own[i] = turned.reshape(LEV, CX, NY)

    devices = out_ref.shape[0]
    upper = upper_strict()
    acc_ref[...] = jnp.zeros_like(acc_ref)

    def body(c, carry):
        lanes = pl.ds(pl.multiple_of(c * CHUNK, CHUNK), CHUNK)
        dest = route_ref[:, lanes]
        mask = iota((devices, CHUNK), 0) == dest
        hot = one_hot(mask)
        rank, carry = running_rank(hot, mask, carry, upper)
        rank = rank.astype(jnp.int32)
        rank_ref[:, lanes] = rank
        slot = one_hot(iota((CAP, CHUNK), 0) == rank)
        fields = [(cell_ref[:, lanes] + 1).astype(F32)]
        fields += [interp_ref[f : f + 1, lanes] for f in range(3)]
        fields += [d_ref[:, lanes], r_ref[:, lanes], var_ref[:, lanes]]
        pieces = []
        for field, count in zip(fields, PACK_PARTS):
            for part in parts_of(field, count):
                pieces.append(slot * part)
        acc_ref[...] += nt(hot, jnp.concatenate(pieces, axis=0))
        return carry

    chunks = route_ref.shape[1] // CHUNK
    carry = jnp.zeros((devices, 1), F32)
    carry = lax.fori_loop(0, chunks // 2, body, carry, unroll=2)
    await_all()

    def to_strip(slot):
        other = lax.rem(t + strips + 1 - slot, strips)
        return pltpu.make_async_remote_copy(
            src_ref=wind_own,
            dst_ref=wind_in.at[slot],
            send_sem=wind_sem.at[0, slot],
            recv_sem=wind_sem.at[1, slot],
            device_id=(g, strip_of(other)),
            device_id_type=MESH,
        )

    to_strip(0).start()
    to_strip(2).start()

    @pl.when(stays)
    def _():
        pltpu.make_async_copy(wind_own, wind_in.at[1], wind_sem.at[1, 1]).start()

    @pl.when(jnp.logical_not(stays))
    def _():
        to_strip(1).start()

    lax.fori_loop(chunks // 2, chunks, body, carry, unroll=2)
    at = 0
    for f, count in enumerate(PACK_PARTS):
        total = acc_ref[:, at * CAP : (at + 1) * CAP]
        for i in range(1, count):
            total = total + acc_ref[:, (at + i) * CAP : (at + i + 1) * CAP]
        at += count
        out_ref[:, f, :] = total
    out_ref[:, 7, :] = jnp.zeros_like(out_ref[:, 7, :])
    send_all(me, out_ref, landing, send_sem, recv_sem)
    for slot in range(3):
        pltpu.make_async_copy(wind_in.at[slot], wind_in.at[slot], wind_sem.at[1, slot]).wait()

    column = iota((EXT, NY), 0)
    lane = iota((EXT, NY), 1)
    west_ok = jnp.logical_not(first_strip & (column == 0))
    east_ok = jnp.logical_not(last_strip & (column == CX - 1))
    inside = inside_grid(first_strip, last_strip)
    west_ok = inside & west_ok
    east_ok = inside & east_ok
    south_ok = inside & (lane > 0)
    north_ok = inside & (lane < NY - 1)
    from_right = iota((CX, NY), 0) < 4

    def coef_body(l, carry):
        wx, wy = [
            jnp.concatenate(
                [wind_in[1, i, l], jnp.where(from_right, wind_in[2, i, l], wind_in[0, i, l])], axis=0
            )
            for i in range(2)
        ]
        coef[0, l] = jnp.where(
            inside, 1.0 - jnp.abs(wx) - jnp.abs(wy) - 4.0 * diffusion - 2.0 * vertical, 0.0
        )
        coef[1, l] = jnp.where(west_ok, jnp.maximum(wx, 0.0) + diffusion, 0.0)
        coef[2, l] = jnp.where(east_ok, jnp.maximum(-wx, 0.0) + diffusion, 0.0)
        coef[3, l] = jnp.where(south_ok, jnp.maximum(wy, 0.0) + diffusion, 0.0)
        coef[4, l] = jnp.where(north_ok, jnp.maximum(-wy, 0.0) + diffusion, 0.0)
        return carry

    lax.fori_loop(0, LEV, coef_body, 0)
    receive_all(landing, recv_sem)
    arrived_ref[...] = landing[...]
    to_strip(0).wait_send()
    to_strip(2).wait_send()

    @pl.when(jnp.logical_not(stays))
    def _():
        to_strip(1).wait_send()

    finish_sends(out_ref, send_sem)


def inside_grid(first_strip, last_strip):
    column = iota((EXT, NY), 0)
    return jnp.logical_not(
        (first_strip & (column >= 12)) | (last_strip & (column >= 8) & (column < 12))
    )


def row_of(ref, field, c):
    per = CHUNK // CAP
    base = c * per
    return jnp.concatenate([ref[base + i, field : field + 1, :] for i in range(per)], axis=1)


SORT_PARTS = 10


def sort_scatter_kernel(recv_ref, forcing_ref, sorted_ref, pos_ref, bucket_ref, rank_ref, acc_ref):
    chunks = recv_ref.shape[0] * CAP // CHUNK
    upper = upper_strict()

    def bucket_of(c):
        cell = row_of(recv_ref, 0, c).astype(jnp.int32) - 1
        bucket = jnp.where(cell < 0, -1, cell // (ROWS * NY))
        return cell, iota((BUCKETS, CHUNK), 0) == bucket

    def count_body(c, carry):
        _, mask = bucket_of(c)
        rank, carry = running_rank(one_hot(mask), mask, carry, upper)
        rank_ref[pl.ds(c, 1), :] = rank
        return carry

    totals = lax.fori_loop(0, chunks, count_body, jnp.zeros((BUCKETS, 1), F32), unroll=4)
    tiles = jnp.floor((totals + (SUB - 1.0)) * (1.0 / SUB))
    before = jnp.zeros((BUCKETS, 1), F32)
    ids = iota((BUCKETS, 1), 0)
    for b in range(BUCKETS):
        here = jnp.sum(jnp.where(ids == b, tiles, 0.0))
        before = before + jnp.where(ids > b, here, 0.0)
    tile_ids = iota((BUCKETS, CAP), 1).astype(F32)
    of_tile = jnp.sum(jnp.where(tile_ids >= before + tiles, 1.0, 0.0), axis=0, keepdims=True)
    used = jnp.sum(tiles)
    of_tile = jnp.where(
        iota((1, CAP), 1) == CAP - 1, used, jnp.minimum(of_tile, BUCKETS - 1.0)
    )
    bucket_ref[...] = of_tile.astype(jnp.int32)
    used = used.astype(jnp.int32)
    offsets = before * float(SUB)

    acc_ref[...] = jnp.zeros_like(acc_ref)

    def sort_body(c, carry):
        cell, mask = bucket_of(c)
        offset = jnp.sum(jnp.where(mask, offsets, 0.0), axis=0, keepdims=True)
        pos = (offset + rank_ref[pl.ds(c, 1), :]).astype(jnp.int32)
        pos = jnp.where(cell < 0, -1, pos)
        pos_ref[pl.ds(c, 1), :] = pos
        high = one_hot(iota((SORT_ROWS, CHUNK), 0) == (pos >> 7))
        low = one_hot(iota((CAP, CHUNK), 0) == (pos & 127))
        inside = (cell & (ROWS * NY - 1)).astype(F32)
        pieces = []
        for value in [inside] + [row_of(recv_ref, f, c) for f in range(1, 5)]:
            for part in parts_of(value, 2):
                pieces.append(low * part)
        acc_ref[...] += nt(high, jnp.concatenate(pieces, axis=0))
        return carry

    lax.fori_loop(0, chunks, sort_body, 0, unroll=2)
    for f in range(SORT_PARTS // 2):
        sorted_ref[f] = (
            acc_ref[:, 2 * f * CAP : (2 * f + 1) * CAP]
            + acc_ref[:, (2 * f + 1) * CAP : (2 * f + 2) * CAP]
        )

    bucket_rows = bucket_ref[...].astype(F32)
    tile_lane = iota((1, CAP), 1)
    forcing_ref[...] = jnp.zeros_like(forcing_ref)

    def tile_body(i, carry):
        for t in range(4):
            t = 4 * i + t
            cell, y, w, d = tile_rows(sorted_ref, t)
            level_x = iota((ROWS, SUB), 0)
            hot = short_hot(level_x, cell >> 8)
            next_hot = short_hot(level_x, (cell >> 8) + 1)
            spots = iota((NY, SUB), 0)
            here = short_hot(spots, lane_of(y))
            above = short_hot(spots, lane_of(y + 1))
            w = [parts_of(x * d, 2) for x in w]
            stacked = [here * w[0][p] + above * w[2][p] for p in range(2)]
            stacked += [here * w[1][p] + above * w[3][p] for p in range(2)]
            added = nt(
                jnp.concatenate([hot, hot, next_hot, next_hot], axis=1),
                jnp.concatenate(stacked, axis=1),
            )
            bucket = jnp.sum(jnp.where(tile_lane == t, bucket_rows, 0.0)).astype(jnp.int32)
            forcing_ref[bucket] += added
        return carry

    lax.fori_loop(0, (used + 3) // 4, tile_body, 0)


def tile_rows(sorted_ref, t):
    def row(f):
        return jnp.concatenate(
            [sorted_ref[f, pl.ds(2 * t, 1), :], sorted_ref[f, pl.ds(2 * t + 1, 1), :]], axis=1
        )

    cell = row(0).astype(jnp.int32)
    w = [row(1), row(2), row(3)]
    w.append(1.0 - w[0] - w[1] - w[2])
    return cell, cell & (NY - 1), w, row(4)


def gather_kernel(
    bucket_ref, state_ref, sorted_ref, pos_ref, recv_ref, own_ref, out_ref, value_ref, table_ref
):
    devices = recv_ref.shape[0]
    chunks = devices * CAP // CHUNK
    value_ref[...] = jnp.zeros_like(value_ref)

    def table_body(b, carry):
        turned = state_ref[b].T
        shifted = pltpu.roll(turned, ROWS - 1, 1)
        table_ref[b] = jnp.concatenate(
            [
                jnp.concatenate(parts_of(turned, 2), axis=1),
                jnp.concatenate(parts_of(shifted, 2), axis=1),
            ],
            axis=0,
        )
        return carry

    lax.fori_loop(0, BUCKETS, table_body, 0)

    def tile_body(i, carry):
        for t in range(4):
            t = 4 * i + t
            cell, y, w, _ = tile_rows(sorted_ref, t)
            hot = one_hot(iota((ROWS, SUB), 0) == (cell >> 8))
            spots = iota((NY, SUB), 0)
            here = spots == lane_of(y)
            above = spots == lane_of(y + 1)
            got = nn(table_ref[bucket_ref[0, t]], jnp.concatenate([hot, hot], axis=0))
            first = jnp.where(here, w[0], jnp.where(above, w[2], 0.0))
            second = jnp.where(here, w[1], jnp.where(above, w[3], 0.0))
            value_ref[pl.ds(t, 1), :] = jnp.sum(
                first * got[:NY] + second * got[NY:], axis=0, keepdims=True
            )
        return carry

    lax.fori_loop(0, (bucket_ref[0, CAP - 1] + 3) // 4, tile_body, 0)
    table = jnp.concatenate(parts_of(value_ref[...].T, 2), axis=1)
    depth = value_ref.shape[0]

    def unsort_body(c, carry):
        pos = pos_ref[pl.ds(c, 1), :]
        high = one_hot(iota((depth, CHUNK), 0) == (pos >> 8))
        got = nn(table, jnp.concatenate([high, high], axis=0))
        low = iota((SUB, CHUNK), 0) == (pos & (SUB - 1))
        row = jnp.sum(jnp.where(low, got, 0.0), axis=0, keepdims=True)
        per = CHUNK // CAP
        block = jnp.concatenate([row[:, i * CAP : (i + 1) * CAP] for i in range(per)], axis=0)
        out_ref[pl.ds(pl.multiple_of(c * per, per), per), :CAP] = block
        return carry

    lax.fori_loop(0, chunks, unsort_body, 0, unroll=2)
    d = recv_ref[:, 4, :]
    r = recv_ref[:, 5, :]
    image = out_ref[:, :CAP] + recv_ref[:, 6, :] * d
    out_ref[:, :CAP] = image
    own = own_ref[...]
    lane = iota((1, CAP), 1)
    sums = jnp.where(lane == 0, jnp.sum(own * own), 0.0)
    sums = jnp.where(lane == 1, jnp.sum(d * image), sums)
    sums = jnp.where(lane == 2, jnp.sum(r * image), sums)
    sums = jnp.where(lane == 3, jnp.sum(image * image), sums)
    out_ref[:, CAP:] = jnp.broadcast_to(sums, (devices, CAP))


def final_kernel(
    out_ref,
    route_ref,
    rank_ref,
    dual_ref,
    d_ref,
    r_ref,
    dual_out,
    res_out,
    dir_out,
    halfway,
    landing,
    send_sem,
    recv_sem,
):
    g = lax.axis_index("tm")
    t = lax.axis_index("space")
    groups = lax.axis_size("tm")
    strips = lax.axis_size("space")
    devices = groups * strips

    barrier = pltpu.get_barrier_semaphore()
    for step in range(1, groups):
        pl.semaphore_signal(
            barrier, inc=1, device_id=(around(g, step, groups), t), device_id_type=MESH
        )

    def greet(i, carry):
        other = (g, around(t, i, strips))
        pl.semaphore_signal(barrier, inc=1, device_id=other, device_id_type=MESH)
        return carry

    lax.fori_loop(1, strips, greet, 0, unroll=True)
    pl.semaphore_wait(barrier, groups + strips - 2)

    def along_space(i, carry):
        strip = around(t, i, strips)
        pltpu.make_async_remote_copy(
            src_ref=out_ref.at[:, strip],
            dst_ref=halfway.at[:, strip_of(t)],
            send_sem=send_sem.at[0],
            recv_sem=recv_sem.at[0],
            device_id=(g, strip),
            device_id_type=MESH,
        ).start()
        return carry

    lax.fori_loop(1, strips, along_space, 0, unroll=True)
    pltpu.make_async_copy(out_ref.at[:, t], halfway.at[:, strip_of(t)], recv_sem.at[0]).start()
    pltpu.make_async_copy(halfway, halfway, recv_sem.at[0]).wait()
    for step in range(1, groups):
        group = around(g, step, groups)
        pltpu.make_async_remote_copy(
            src_ref=halfway.at[group],
            dst_ref=landing.at[g],
            send_sem=send_sem.at[1],
            recv_sem=recv_sem.at[1],
            device_id=(group, t),
            device_id_type=MESH,
        ).start()
    pltpu.make_async_copy(halfway.at[g], landing.at[g], recv_sem.at[1]).start()
    pltpu.make_async_copy(landing, landing, recv_sem.at[1]).wait()
    returned = landing[...].reshape(devices, 2 * CAP)
    sums = jnp.sum(returned[:, CAP:], axis=0, keepdims=True)
    lane = iota((1, CAP), 1)
    norm_now, curvature, cross, square = [
        jnp.sum(jnp.where(lane == i, sums, 0.0), axis=1, keepdims=True) for i in range(4)
    ]
    step = norm_now / curvature
    norm_next = norm_now - 2.0 * step * cross + step * step * square
    ratio = norm_next / norm_now
    table = jnp.concatenate(parts_of(returned[:, :CAP].T, 2), axis=1)
    for c in range(route_ref.shape[1] // CHUNK):
        lanes = slice(c * CHUNK, (c + 1) * CHUNK)
        hot = one_hot(iota((devices, CHUNK), 0) == route_ref[:, lanes])
        got = nn(table, jnp.concatenate([hot, hot], axis=0))
        mask = iota((CAP, CHUNK), 0) == rank_ref[:, lanes]
        image = jnp.sum(jnp.where(mask, got, 0.0), axis=0, keepdims=True)
        d = d_ref[:, lanes]
        res = r_ref[:, lanes] - step * image
        dual_out[:, lanes] = dual_ref[:, lanes] + step * d
        res_out[:, lanes] = res
        dir_out[:, lanes] = res + ratio * d
    rest = out_ref.at[:, pl.ds(0, strips - 1)]
    pltpu.make_async_copy(rest, rest, send_sem.at[0]).wait()
    rest = halfway.at[pl.ds(0, groups - 1)]
    pltpu.make_async_copy(rest, rest, send_sem.at[1]).wait()


def back(x):
    return jnp.concatenate([pltpu.roll(x[:, HALF:], 1, 1), x[:, :HALF]], axis=1)


def ahead(x):
    return jnp.concatenate([x[:, HALF:], pltpu.roll(x[:, :HALF], HALF - 1, 1)], axis=1)


def sweep_kernel(
    forcing_ref,
    coef,
    coupling_hbm,
    scale_hbm,
    state_ref,
    coupling_ref,
    scale_ref,
    scalar_sem,
    hop_a,
    hop_x,
    fin_a,
    fin_x,
    adj_out,
    adj_in,
    force_out,
    force_in,
    cov_out,
    cov_in,
    fwd_out,
    fwd_in,
    fext,
    u0,
    u1,
    u2,
    u3,
    v0,
    v1,
    v2,
    v3,
    inc,
    hop_sem,
    adj_sem,
    force_sem,
    cov_sem,
    fwd_sem,
):
    g = lax.axis_index("tm")
    t = lax.axis_index("space")
    groups = lax.axis_size("tm")
    strips = lax.axis_size("space")
    strip = strip_of(t)
    left = (g, strip_of(lax.rem(strip + strips - 1, strips)))
    right = (g, strip_of(lax.rem(strip + 1, strips)))
    later = (lax.rem(g + 1, groups), t)
    earlier = (lax.rem(g + groups - 1, groups), t)
    sides = (left, right)
    first_strip = strip == 0
    last_strip = strip == strips - 1
    last_group = g == groups - 1
    first_group = g == 0

    barrier = pltpu.get_barrier_semaphore()
    for other in (left, right, later, earlier):
        pl.semaphore_signal(barrier, inc=1, device_id=other, device_id_type=MESH)

    coupling_fetch = pltpu.make_async_copy(coupling_hbm, coupling_ref, scalar_sem.at[0])
    scale_fetch = pltpu.make_async_copy(scale_hbm, scale_ref, scalar_sem.at[1])
    coupling_fetch.start()
    scale_fetch.start()
    pl.semaphore_wait(barrier, 4)

    def to_side(src, dst, sems, side, *idx):
        return pltpu.make_async_remote_copy(
            src_ref=src,
            dst_ref=dst,
            send_sem=sems.at[(0, side) + idx],
            recv_sem=sems.at[(1, 1 - side) + idx],
            device_id=sides[side],
            device_id_type=MESH,
        )

    def wait_side(dst, sems, slot, *idx):
        pltpu.make_async_remote_copy(
            src_ref=dst,
            dst_ref=dst,
            send_sem=sems.at[(0, slot) + idx],
            recv_sem=sems.at[(1, slot) + idx],
            device_id=sides[slot],
            device_id_type=MESH,
        ).wait_recv()

    def hop(src, dst, way, level, device):
        return pltpu.make_async_remote_copy(
            src_ref=src.at[level],
            dst_ref=dst.at[level],
            send_sem=hop_sem.at[way, 0, level],
            recv_sem=hop_sem.at[way, 1, level],
            device_id=device,
            device_id_type=MESH,
        )

    upper = iota((CX, NY), 0) < 4

    def pack(out, level, first, value):
        for j in range(NV // 2):
            one = value[2 * j]
            two = pltpu.roll(value[2 * j + 1], 4, 0)
            out[0, level, first + j] = jnp.where(upper, one, two)
            out[1, level, first + j] = jnp.where(upper, two, one)

    def join(arrived, level, first):
        tiles = []
        for j in range(NV // 2):
            from_left = arrived[0, level, first + j]
            from_right = arrived[1, level, first + j]
            tiles.append(jnp.where(upper, from_right, from_left))
            tiles.append(pltpu.roll(jnp.where(upper, from_left, from_right), 4, 0))
        return tiles

    def exchange(out, arrived, sems, level):
        for side in range(2):
            to_side(
                out.at[side, level], arrived.at[1 - side, level], sems, side, level
            ).start()

    def await_sides(arrived, sems, level):
        for slot in range(2):
            wait_side(arrived.at[slot, level], sems, slot, level)

    def send_forcing(l):
        for i in range(3):
            pack(force_out, l, 2 * i, [forcing_ref[i, v, l] for v in range(NV)])
        exchange(force_out, force_in, force_sem, l)

    edge = jnp.zeros((NV, EXT, NY), F32)
    for u in (u0, u1, u2, u3, v0, v1, v2, v3):
        u[0] = edge
        u[LEV + 1] = edge

    @pl.when(last_group)
    def _():
        hop_a[...] = jnp.zeros_like(hop_a)

    @pl.when(first_group)
    def _():
        hop_x[...] = jnp.zeros_like(hop_x)

    @pl.when(jnp.logical_not(last_group))
    def _():
        def early(l, carry):
            send_forcing(l)
            return carry

        lax.fori_loop(0, LEV, early, 0)

    inside = inside_grid(first_strip, last_strip)
    coupling_fetch.wait()
    scale_fetch.wait()
    mix = [[coupling_step * coupling_ref[v, w] for w in range(NV)] for v in range(NV)]

    def adjoint_level(u, l, rows):
        c, w, e, s, n = [coef[i, l] for i in range(5)]
        now = [u[l + 1, v] for v in range(NV)]
        out = []
        for v in range(NV):
            a = now[v]
            res = c[:rows] * a[:rows]
            res = res + pltpu.roll(w * a, EXT - 1, 0)[:rows] + pltpu.roll(e * a, 1, 0)[:rows]
            res = res + ahead(s[:rows] * a[:rows]) + back(n[:rows] * a[:rows])
            res = res + vertical * (u[l, v, :rows] + u[l + 2, v, :rows])
            for k in range(NV):
                res = res + mix[k][v] * now[k][:rows]
            out.append(res)
        return out

    def forward_level(u, l, rows):
        c, w, e, s, n = [coef[i, l][:rows] for i in range(5)]
        now = [u[l + 1, v] for v in range(NV)]
        out = []
        for v in range(NV):
            a = now[v]
            res = c * a[:rows]
            res = res + w * pltpu.roll(a, 1, 0)[:rows] + e * pltpu.roll(a, EXT - 1, 0)[:rows]
            res = res + s * back(a[:rows]) + n * ahead(a[:rows])
            res = res + vertical * (u[l, v, :rows] + u[l + 2, v, :rows])
            for k in range(NV):
                res = res + mix[v][k] * now[k][:rows]
            out.append(res)
        return out

    def in_range(l):
        return (l >= 0) & (l < LEV)

    def adjoint_tick(k):
        @pl.when(in_range(k))
        def _():
            @pl.when(jnp.logical_not(last_group))
            def _():
                hop(hop_a, hop_a, 0, k, later).wait_recv()

            value = [hop_a[k, v] + forcing_ref[3, v, k] for v in range(NV)]
            pack(adj_out, k, 0, value)
            exchange(adj_out, adj_in, adj_sem, k)

            @pl.when(last_group)
            def _():
                send_forcing(k)

            for v in range(NV):
                u0[k + 1, v, :CX] = value[v]

        m = k - ADJ_DELAY

        @pl.when(in_range(m))
        def _():
            await_sides(adj_in, adj_sem, m)
            await_sides(force_in, force_sem, m)
            for v, tile in enumerate(join(adj_in, m, 0)):
                u0[m + 1, v, CX:] = tile
            for i in range(3):
                for v, tile in enumerate(join(force_in, m, 2 * i)):
                    fext[i, m, v] = tile

        for i, (src, dst) in enumerate(((u0, u1), (u1, u2), (u2, u3))):
            level = m - 1 - i

            @pl.when(in_range(level))
            def _():
                res = adjoint_level(src, level, EXT)
                for v in range(NV):
                    dst[level + 1, v, :CX] = res[v][:CX] + forcing_ref[2 - i, v, level]
                    dst[level + 1, v, CX:] = res[v][CX:] + fext[2 - i, level, v]

        level = m - 4

        @pl.when(in_range(level))
        def _():
            res = adjoint_level(u3, level, CX)
            for v in range(NV):
                fin_a[level, v] = res[v]

            @pl.when(jnp.logical_not(first_group))
            def _():
                hop(fin_a, hop_a, 0, level, earlier).start()

            pack(cov_out, level, 0, res)
            exchange(cov_out, cov_in, cov_sem, level)

    lane_low = jnp.where(iota((CX, NY), 1) > 0, 1.0, 0.0)
    lane_high = jnp.where(iota((CX, NY), 1) < NY - 1, 1.0, 0.0)
    keep = jnp.where(inside, 1.0, 0.0)

    def cov_tick(l):
        @pl.when(in_range(l))
        def _():
            await_sides(cov_in, cov_sem, l)
            for v, tile in enumerate(join(cov_in, l, 0)):
                scale = scale_ref[0, v, l]
                ext = jnp.concatenate([fin_a[l, v], tile], axis=0) * (keep * scale)
                ext = 0.5 * ext + 0.25 * (pltpu.roll(ext, 1, 0) + pltpu.roll(ext, EXT - 1, 0))
                ext = ext * keep
                ext = 0.5 * ext + 0.25 * (pltpu.roll(ext, 1, 0) + pltpu.roll(ext, EXT - 1, 0))
                own = ext[:CX]
                for _ in range(2):
                    own = 0.5 * own + 0.25 * (lane_low * back(own) + lane_high * ahead(own))
                inc[l, v] = own * scale

    fwd_delay = jnp.where(first_group, FIRST_DELAY, FWD_DELAY)

    def forward_tick(k):
        @pl.when(in_range(k))
        def _():
            @pl.when(jnp.logical_not(first_group))
            def _():
                hop(hop_x, hop_x, 1, k, earlier).wait_recv()

            value = [hop_x[k, v] + inc[k, v] for v in range(NV)]
            pack(fwd_out, k, 0, value)
            exchange(fwd_out, fwd_in, fwd_sem, k)
            for v in range(NV):
                v0[k + 1, v, :CX] = value[v]

        m = k - fwd_delay

        @pl.when(in_range(m))
        def _():
            await_sides(fwd_in, fwd_sem, m)
            for v, tile in enumerate(join(fwd_in, m, 0)):
                v0[m + 1, v, CX:] = tile

        for i, (src, dst) in enumerate(((v0, v1), (v1, v2), (v2, v3))):
            level = m - 1 - i

            @pl.when(in_range(level))
            def _():
                res = forward_level(src, level, EXT)
                for v in range(NV):
                    dst[level + 1, v] = res[v]
                    state_ref[i, v, level] = res[v][:CX]

        level = m - 4

        @pl.when(in_range(level))
        def _():
            res = forward_level(v3, level, CX)
            for v in range(NV):
                state_ref[3, v, level] = res[v]
                fin_x[level, v] = res[v]

            @pl.when(jnp.logical_not(last_group))
            def _():
                hop(fin_x, hop_x, 1, level, later).start()

    adjoint_ticks = LEV + ADJ_DELAY + 4
    behind = jnp.where(first_group, ADJ_DELAY + 4 + COV_DELAY, adjoint_ticks)

    def tick(k, carry):
        adjoint_tick(k)
        cov_tick(k - (ADJ_DELAY + 4 + COV_DELAY))
        forward_tick(k - behind)
        return carry

    lax.fori_loop(0, behind + LEV + fwd_delay + 4, tick, 0)

    def drain(l, carry):
        for out, arrived, sems in (
            (adj_out, adj_in, adj_sem),
            (force_out, force_in, force_sem),
            (cov_out, cov_in, cov_sem),
            (fwd_out, fwd_in, fwd_sem),
        ):
            for side in range(2):
                to_side(
                    out.at[side, l], arrived.at[1 - side, l], sems, side, l
                ).wait_send()

        @pl.when(jnp.logical_not(first_group))
        def _():
            hop(fin_a, hop_a, 0, l, earlier).wait_send()

        @pl.when(jnp.logical_not(last_group))
        def _():
            hop(fin_x, hop_x, 1, l, later).wait_send()

        return carry

    lax.fori_loop(0, LEV, drain, 0)


def sweeps(forcing, coef, coupling, scale):
    state = pltpu.VMEM((LEV, NV, CX, NY), F32)
    padded = pltpu.VMEM((LEV + 2, NV, EXT, NY), F32)
    edges = pltpu.VMEM((2, LEV, 2, CX, NY), F32)
    wide_edges = pltpu.VMEM((2, LEV, 6, CX, NY), F32)
    levels = pltpu.SemaphoreType.DMA((2, 2, LEV))
    return pl.pallas_call(
        sweep_kernel,
        out_shape=jax.ShapeDtypeStruct((STEPS, NV, LEV, CX, NY), F32),
        in_specs=[VMEM, VMEM, ANY, ANY],
        out_specs=VMEM,
        scratch_shapes=[
            pltpu.SMEM((NV, NV), F32),
            pltpu.SMEM((1, NV, LEV), F32),
            pltpu.SemaphoreType.DMA((2,)),
        ]
        + [state] * 4
        + [edges] * 2
        + [wide_edges] * 2
        + [edges] * 4
        + [pltpu.VMEM((3, LEV, NV, CX, NY), F32)]
        + [padded] * 8
        + [state]
        + [levels] * 5,
        compiler_params=params(34, collective_id=1, has_side_effects=True),
        name="sweeps",
    )(forcing, coef, coupling, scale)


def per_device(
    dual_weights,
    direction,
    residual_dual,
    obs_var,
    obs_route,
    obs_cell,
    obs_interp,
    wind_x,
    wind_y,
    coupling,
    cov_scale,
):
    grid = (lax.axis_size("tm"), lax.axis_size("space"))
    devices = grid[0] * grid[1]
    rows = direction.shape[0]
    wide = (1, rows)
    route = obs_route.reshape(1, rows)
    tiles = pltpu.VMEM((devices, 8, CAP), F32)
    arrived, rank, coef = pl.pallas_call(
        route_kernel,
        out_shape=(
            jax.ShapeDtypeStruct((devices, 8, CAP), F32),
            jax.ShapeDtypeStruct((1, rows), jnp.int32),
            jax.ShapeDtypeStruct((5, LEV, EXT, NY), F32),
        ),
        in_specs=[ANY] * 8,
        out_specs=(VMEM, VMEM, VMEM),
        scratch_shapes=[
            tiles,
            tiles,
            pltpu.VMEM((devices, sum(PACK_PARTS) * CAP), F32),
            pltpu.VMEM((2, LEV, CX, NY), F32),
            pltpu.VMEM((3, 2, LEV, CX, NY), F32),
            pltpu.VMEM((1, rows), jnp.int32),
            pltpu.VMEM((1, rows), jnp.int32),
            pltpu.VMEM((4, rows), F32),
            pltpu.VMEM((1, rows), F32),
            pltpu.VMEM((1, rows), F32),
            pltpu.VMEM((1, rows), F32),
            pltpu.VMEM((1, LEV, CX, NY), F32),
            pltpu.VMEM((1, LEV, CX, NY), F32),
            pltpu.SemaphoreType.DMA,
            pltpu.SemaphoreType.DMA,
            pltpu.SemaphoreType.DMA((2, 3)),
            pltpu.SemaphoreType.DMA((8,)),
        ],
        compiler_params=params(58, collective_id=2, has_side_effects=True),
        name="route",
    )(
        route,
        obs_cell.reshape(1, rows),
        obs_interp,
        direction.reshape(1, rows),
        residual_dual.reshape(1, rows),
        obs_var.reshape(1, rows),
        wind_x,
        wind_y,
    )
    slots = devices * CAP
    forcing, ordered, position, starts = pl.pallas_call(
        sort_scatter_kernel,
        out_shape=(
            jax.ShapeDtypeStruct((BUCKETS, ROWS, NY), F32),
            jax.ShapeDtypeStruct((SORT_PARTS // 2, SORT_ROWS, CAP), F32),
            jax.ShapeDtypeStruct((slots // CHUNK, CHUNK), jnp.int32),
            jax.ShapeDtypeStruct((1, CAP), jnp.int32),
        ),
        in_specs=[VMEM],
        out_specs=(VMEM, VMEM, VMEM, VMEM),
        scratch_shapes=[
            pltpu.VMEM((slots // CHUNK, CHUNK), F32),
            pltpu.VMEM((SORT_ROWS, SORT_PARTS * CAP), F32),
        ],
        compiler_params=params(20),
        name="sort_scatter",
    )(arrived)
    states = sweeps(forcing.reshape(STEPS, NV, LEV, CX, NY), coef, coupling, cov_scale)
    returning = pl.pallas_call(
        gather_kernel,
        out_shape=jax.ShapeDtypeStruct((devices, 2 * CAP), F32),
        in_specs=[SMEM, VMEM, VMEM, VMEM, VMEM, VMEM],
        out_specs=VMEM,
        scratch_shapes=[
            pltpu.VMEM((CAP, SUB), F32),
            pltpu.VMEM((BUCKETS, 2 * NY, 2 * ROWS), BF16),
        ],
        compiler_params=params(20),
        name="gather",
    )(
        starts,
        states.reshape(BUCKETS, ROWS, NY),
        ordered,
        position,
        arrived,
        residual_dual.reshape(wide),
    )
    out = jax.ShapeDtypeStruct(wide, F32)
    results = pl.pallas_call(
        final_kernel,
        out_shape=(out, out, out),
        in_specs=[VMEM] * 6,
        out_specs=(VMEM, VMEM, VMEM),
        scratch_shapes=[
            pltpu.VMEM(grid + (1, 2 * CAP), F32),
            pltpu.VMEM(grid + (1, 2 * CAP), F32),
            pltpu.SemaphoreType.DMA((2,)),
            pltpu.SemaphoreType.DMA((2,)),
        ],
        compiler_params=params(12, collective_id=3, has_side_effects=True),
        name="final",
    )(
        returning.reshape(grid + (1, 2 * CAP)),
        route.reshape(wide),
        rank.reshape(wide),
        dual_weights.reshape(wide),
        direction.reshape(wide),
        residual_dual.reshape(wide),
    )
    return tuple(r.reshape(rows) for r in results)


def solution(mesh):
    return jax.shard_map(
        per_device,
        mesh=mesh,
        in_specs=(
            P(("tm", "space")),
            P(("tm", "space")),
            P(("tm", "space")),
            P(("tm", "space")),
            P(("tm", "space"), None),
            P(("tm", "space")),
            P(None, ("tm", "space")),
            P("tm", None, "space", None),
            P("tm", None, "space", None),
            P(),
            P("tm", None, None),
        ),
        out_specs=(P(("tm", "space")), P(("tm", "space")), P(("tm", "space"))),
        check_vma=False,
    )
```

```python
import functools

import jax
import jax.numpy as jnp
from jax import lax
from jax.experimental import pallas as pl
from jax.experimental.pallas import tpu as pltpu
from jax.sharding import PartitionSpec as P

STEPS = 4
NV = 4
LEV = 16
CX = 8
NY = 256
CAP = 128
ROWS = LEV * CX
BUCKETS = STEPS * NV
SORT_ROWS = 160
CHUNK = 1024
SUB = 256
HALF = NY // 2
EXT = 2 * CX
ADJ_DELAY = 4
COV_DELAY = 4
FWD_DELAY = 4
FIRST_DELAY = 4
diffusion = 0.05
vertical = 0.05
coupling_step = 0.05
MESH = pl.DeviceIdType.MESH
F32 = jnp.float32
BF16 = jnp.bfloat16
VMEM = pl.BlockSpec(memory_space=pltpu.VMEM)
SMEM = pl.BlockSpec(memory_space=pltpu.SMEM)
ANY = pl.BlockSpec(memory_space=pltpu.HBM)


def params(mib, **kw):
    return pltpu.CompilerParams(vmem_limit_bytes=mib * 1024 * 1024, **kw)


def iota(shape, dim):
    return lax.broadcasted_iota(jnp.int32, shape, dim)


def parts_of(value, count):
    out = []
    for _ in range(count - 1):
        head = value.astype(BF16)
        out.append(head)
        value = value - head.astype(F32)
    out.append(value.astype(BF16))
    return out


def nt(a, b):
    return lax.dot_general(a, b, (((1,), (1,)), ((), ())), preferred_element_type=F32)


def nn(a, b):
    return jnp.dot(a, b, preferred_element_type=F32)


def one_hot(mask):
    return jnp.where(mask, 1.0, 0.0).astype(BF16)


def short_hot(ids, row):
    same = ids.astype(jnp.int16) == row.astype(jnp.int16)
    return jnp.where(same, jnp.ones((), BF16), jnp.zeros((), BF16))


def running_rank(hot, hot_mask, carry, upper):
    keys = hot.shape[0]
    pieces = CHUNK // SUB
    stacked = jnp.concatenate([hot[:, i * SUB : (i + 1) * SUB] for i in range(pieces)], axis=0)
    counted = nn(stacked, upper)
    rows = []
    for i in range(pieces):
        mask = hot_mask[:, i * SUB : (i + 1) * SUB]
        part = counted[i * keys : (i + 1) * keys] + carry
        rows.append(jnp.sum(jnp.where(mask, part, 0.0), axis=0, keepdims=True))
        carry = carry + jnp.sum(jnp.where(mask, 1.0, 0.0), axis=1, keepdims=True)
    return jnp.concatenate(rows, axis=1), carry


def lane_of(y):
    return (y >> 1) + (y & 1) * HALF


def upper_strict():
    return one_hot(iota((SUB, SUB), 0) < iota((SUB, SUB), 1))


PACK_PARTS = (3, 2, 2, 2, 2, 2, 2)


ROW_STRIPS = 8


def backwards(within):
    return ROW_STRIPS - 2 - within + 2 * (within % 2)


def strip_of(t):
    row = t // ROW_STRIPS
    within = t % ROW_STRIPS
    return row * ROW_STRIPS + jnp.where(row % 2 == 1, backwards(within), within)


def around(start, step, size):
    index = start + step
    return jnp.where(index >= size, index - size, index)


def everyone(act):
    g = lax.axis_index("tm")
    t = lax.axis_index("space")
    groups = lax.axis_size("tm")
    rows = lax.axis_size("space") // ROW_STRIPS
    ways = []
    for step in range(ROW_STRIPS):
        within = around(t % ROW_STRIPS, step, ROW_STRIPS)
        ways.append((within, backwards(within)))
    for group_step in range(groups):
        group = around(g, group_step, groups)
        for row_step in range(rows):
            row = around(t // ROW_STRIPS, row_step, rows)
            first = row * ROW_STRIPS
            odd = row % 2 == 1
            for step, (within, turned) in enumerate(ways):
                if group_step or row_step or step:
                    act(group, first + within, first + jnp.where(odd, turned, within))


def greet_all():
    barrier = pltpu.get_barrier_semaphore()
    everyone(
        lambda group, place, strip: pl.semaphore_signal(
            barrier, inc=1, device_id=(group, place), device_id_type=MESH
        )
    )


def await_all():
    devices = lax.axis_size("tm") * lax.axis_size("space")
    pl.semaphore_wait(pltpu.get_barrier_semaphore(), devices - 1)


def send_all(me, out, arrived, send_sem, recv_sem):
    strips = lax.axis_size("space")

    def start(group, place, strip):
        pltpu.make_async_remote_copy(
            src_ref=out.at[group * strips + strip],
            dst_ref=arrived.at[me],
            send_sem=send_sem,
            recv_sem=recv_sem,
            device_id=(group, place),
            device_id_type=MESH,
        ).start()

    own = lax.axis_index("tm") * strips + strip_of(lax.axis_index("space"))
    pltpu.make_async_copy(out.at[own], arrived.at[me], recv_sem).start()
    everyone(start)


def receive_all(arrived, recv_sem):
    pltpu.make_async_copy(arrived, arrived, recv_sem).wait()


def finish_sends(out, send_sem):
    rest = out.at[pl.ds(0, out.shape[0] - 1)]
    pltpu.make_async_copy(rest, rest, send_sem).wait()


def my_index():
    return lax.axis_index("tm") * lax.axis_size("space") + lax.axis_index("space")


def route_kernel(
    route_hbm,
    cell_hbm,
    interp_hbm,
    d_hbm,
    r_hbm,
    var_hbm,
    wind_x_hbm,
    wind_y_hbm,
    coupling_hbm,
    scale_hbm,
    arrived_ref,
    rank_ref,
    coef,
    out_ref,
    landing,
    acc_ref,
    wind_own,
    wind_in,
    route_ref,
    cell_ref,
    interp_ref,
    d_ref,
    r_ref,
    var_ref,
    wind_x_ref,
    wind_y_ref,
    coupling_ref,
    scale_ref,
    send_sem,
    recv_sem,
    wind_sem,
    fetch_sem,
):
    fetches = [
        pltpu.make_async_copy(src, dst, fetch_sem.at[i])
        for i, (src, dst) in enumerate(
            (
                (wind_x_hbm, wind_x_ref),
                (wind_y_hbm, wind_y_ref),
                (route_hbm, route_ref),
                (cell_hbm, cell_ref),
                (interp_hbm, interp_ref),
                (d_hbm, d_ref),
                (r_hbm, r_ref),
                (var_hbm, var_ref),
                (coupling_hbm, coupling_ref),
                (scale_hbm, scale_ref),
            )
        )
    ]
    for fetch in fetches:
        fetch.start()
    me = my_index()
    g = lax.axis_index("tm")
    t = lax.axis_index("space")
    strips = lax.axis_size("space")
    strip = strip_of(t)
    stays = strip == t
    first_strip = strip == 0
    last_strip = strip == strips - 1
    greet_all()
    for fetch in fetches:
        fetch.wait()

    order = iota((NY, NY), 1)
    order = one_hot(iota((NY, NY), 0) == (order % HALF) * 2 + order // HALF)
    for i, wind in enumerate((wind_x_ref, wind_y_ref)):
        turned = parts_of(wind[...].reshape(LEV * CX, NY), 3)
        turned = nn(turned[0], order) + nn(turned[1], order) + nn(turned[2], order)
        wind_own[i] = turned.reshape(LEV, CX, NY)

    devices = out_ref.shape[0]
    upper = upper_strict()
    acc_ref[...] = jnp.zeros_like(acc_ref)

    def body(c, carry):
        lanes = pl.ds(pl.multiple_of(c * CHUNK, CHUNK), CHUNK)
        dest = route_ref[:, lanes]
        mask = iota((devices, CHUNK), 0) == dest
        hot = one_hot(mask)
        rank, carry = running_rank(hot, mask, carry, upper)
        rank = rank.astype(jnp.int32)
        rank_ref[:, lanes] = rank
        slot = one_hot(iota((CAP, CHUNK), 0) == rank)
        fields = [(cell_ref[:, lanes] + 1).astype(F32)]
        fields += [interp_ref[f : f + 1, lanes] for f in range(3)]
        fields += [d_ref[:, lanes], r_ref[:, lanes], var_ref[:, lanes]]
        pieces = []
        for field, count in zip(fields, PACK_PARTS):
            for part in parts_of(field, count):
                pieces.append(slot * part)
        acc_ref[...] += nt(hot, jnp.concatenate(pieces, axis=0))
        return carry

    chunks = route_ref.shape[1] // CHUNK
    carry = jnp.zeros((devices, 1), F32)
    carry = lax.fori_loop(0, chunks // 2, body, carry, unroll=2)
    await_all()

    def to_strip(slot):
        other = lax.rem(t + strips + 1 - slot, strips)
        return pltpu.make_async_remote_copy(
            src_ref=wind_own,
            dst_ref=wind_in.at[slot],
            send_sem=wind_sem.at[0, slot],
            recv_sem=wind_sem.at[1, slot],
            device_id=(g, strip_of(other)),
            device_id_type=MESH,
        )

    to_strip(0).start()
    to_strip(2).start()

    @pl.when(stays)
    def _():
        pltpu.make_async_copy(wind_own, wind_in.at[1], wind_sem.at[1, 1]).start()

    @pl.when(jnp.logical_not(stays))
    def _():
        to_strip(1).start()

    lax.fori_loop(chunks // 2, chunks, body, carry, unroll=2)
    at = 0
    for f, count in enumerate(PACK_PARTS):
        total = acc_ref[:, at * CAP : (at + 1) * CAP]
        for i in range(1, count):
            total = total + acc_ref[:, (at + i) * CAP : (at + i + 1) * CAP]
        at += count
        out_ref[:, f, :] = total
    out_ref[:, 7, :] = jnp.zeros_like(out_ref[:, 7, :])
    send_all(me, out_ref, landing, send_sem, recv_sem)
    for slot in range(3):
        pltpu.make_async_copy(wind_in.at[slot], wind_in.at[slot], wind_sem.at[1, slot]).wait()

    column = iota((EXT, NY), 0)
    lane = iota((EXT, NY), 1)
    west_ok = jnp.logical_not(first_strip & (column == 0))
    east_ok = jnp.logical_not(last_strip & (column == CX - 1))
    inside = inside_grid(first_strip, last_strip)
    west_ok = inside & west_ok
    east_ok = inside & east_ok
    south_ok = inside & (lane > 0)
    north_ok = inside & (lane < NY - 1)
    from_right = iota((CX, NY), 0) < 4

    def coef_body(l, carry):
        wx, wy = [
            jnp.concatenate(
                [wind_in[1, i, l], jnp.where(from_right, wind_in[2, i, l], wind_in[0, i, l])], axis=0
            )
            for i in range(2)
        ]
        coef[l] = jnp.where(
            inside, 1.0 - jnp.abs(wx) - jnp.abs(wy) - 4.0 * diffusion - 2.0 * vertical, 0.0
        )
        coef[LEV + l] = jnp.where(west_ok, jnp.maximum(wx, 0.0) + diffusion, 0.0)
        coef[2 * LEV + l] = jnp.where(east_ok, jnp.maximum(-wx, 0.0) + diffusion, 0.0)
        coef[3 * LEV + l] = jnp.where(south_ok, jnp.maximum(wy, 0.0) + diffusion, 0.0)
        coef[4 * LEV + l] = jnp.where(north_ok, jnp.maximum(-wy, 0.0) + diffusion, 0.0)
        return carry

    lax.fori_loop(0, LEV, coef_body, 0)
    coef[5 * LEV] = jnp.zeros((EXT, NY), F32)
    coef[5 * LEV, :NV, :NV] = coupling_ref[...]
    coef[5 * LEV, CX : CX + NV, :LEV] = scale_ref[0]
    receive_all(landing, recv_sem)
    arrived_ref[...] = landing[...]
    to_strip(0).wait_send()
    to_strip(2).wait_send()

    @pl.when(jnp.logical_not(stays))
    def _():
        to_strip(1).wait_send()

    finish_sends(out_ref, send_sem)


def inside_grid(first_strip, last_strip):
    column = iota((EXT, NY), 0)
    return jnp.logical_not(
        (first_strip & (column >= 12)) | (last_strip & (column >= 8) & (column < 12))
    )


def row_of(ref, field, c):
    per = CHUNK // CAP
    base = c * per
    return jnp.concatenate([ref[base + i, field : field + 1, :] for i in range(per)], axis=1)


SORT_PARTS = 10


def sort_scatter_kernel(recv_ref, forcing_ref, sorted_ref, pos_ref, bucket_ref, rank_ref, acc_ref):
    chunks = recv_ref.shape[0] * CAP // CHUNK
    upper = upper_strict()

    def bucket_of(c):
        cell = row_of(recv_ref, 0, c).astype(jnp.int32) - 1
        bucket = jnp.where(cell < 0, -1, cell // (ROWS * NY))
        return cell, iota((BUCKETS, CHUNK), 0) == bucket

    def count_body(c, carry):
        _, mask = bucket_of(c)
        rank, carry = running_rank(one_hot(mask), mask, carry, upper)
        rank_ref[pl.ds(c, 1), :] = rank
        return carry

    totals = lax.fori_loop(0, chunks, count_body, jnp.zeros((BUCKETS, 1), F32), unroll=4)
    tiles = jnp.floor((totals + (SUB - 1.0)) * (1.0 / SUB))
    before = jnp.zeros((BUCKETS, 1), F32)
    ids = iota((BUCKETS, 1), 0)
    for b in range(BUCKETS):
        here = jnp.sum(jnp.where(ids == b, tiles, 0.0))
        before = before + jnp.where(ids > b, here, 0.0)
    tile_ids = iota((BUCKETS, CAP), 1).astype(F32)
    of_tile = jnp.sum(jnp.where(tile_ids >= before + tiles, 1.0, 0.0), axis=0, keepdims=True)
    used = jnp.sum(tiles)
    of_tile = jnp.where(
        iota((1, CAP), 1) == CAP - 1, used, jnp.minimum(of_tile, BUCKETS - 1.0)
    )
    bucket_ref[...] = of_tile.astype(jnp.int32)
    used = used.astype(jnp.int32)
    offsets = before * float(SUB)

    acc_ref[...] = jnp.zeros_like(acc_ref)

    def sort_body(c, carry):
        cell, mask = bucket_of(c)
        offset = jnp.sum(jnp.where(mask, offsets, 0.0), axis=0, keepdims=True)
        pos = (offset + rank_ref[pl.ds(c, 1), :]).astype(jnp.int32)
        pos = jnp.where(cell < 0, -1, pos)
        pos_ref[pl.ds(c, 1), :] = pos
        high = one_hot(iota((SORT_ROWS, CHUNK), 0) == (pos >> 7))
        low = one_hot(iota((CAP, CHUNK), 0) == (pos & 127))
        inside = (cell & (ROWS * NY - 1)).astype(F32)
        pieces = []
        for value in [inside] + [row_of(recv_ref, f, c) for f in range(1, 5)]:
            for part in parts_of(value, 2):
                pieces.append(low * part)
        acc_ref[...] += nt(high, jnp.concatenate(pieces, axis=0))
        return carry

    lax.fori_loop(0, chunks, sort_body, 0, unroll=2)
    for f in range(SORT_PARTS // 2):
        sorted_ref[f] = (
            acc_ref[:, 2 * f * CAP : (2 * f + 1) * CAP]
            + acc_ref[:, (2 * f + 1) * CAP : (2 * f + 2) * CAP]
        )

    bucket_rows = bucket_ref[...].astype(F32)
    tile_lane = iota((1, CAP), 1)
    forcing_ref[...] = jnp.zeros_like(forcing_ref)

    def tile_body(i, carry):
        for t in range(4):
            t = 4 * i + t
            cell, y, w, d = tile_rows(sorted_ref, t)
            level_x = iota((ROWS, SUB), 0)
            hot = short_hot(level_x, cell >> 8)
            next_hot = short_hot(level_x, (cell >> 8) + 1)
            spots = iota((NY, SUB), 0)
            here = short_hot(spots, lane_of(y))
            above = short_hot(spots, lane_of(y + 1))
            w = [parts_of(x * d, 2) for x in w]
            stacked = [here * w[0][p] + above * w[2][p] for p in range(2)]
            stacked += [here * w[1][p] + above * w[3][p] for p in range(2)]
            added = nt(
                jnp.concatenate([hot, hot, next_hot, next_hot], axis=1),
                jnp.concatenate(stacked, axis=1),
            )
            bucket = jnp.sum(jnp.where(tile_lane == t, bucket_rows, 0.0)).astype(jnp.int32)
            forcing_ref[bucket] += added
        return carry

    lax.fori_loop(0, (used + 3) // 4, tile_body, 0)


def tile_rows(sorted_ref, t):
    def row(f):
        return jnp.concatenate(
            [sorted_ref[f, pl.ds(2 * t, 1), :], sorted_ref[f, pl.ds(2 * t + 1, 1), :]], axis=1
        )

    cell = row(0).astype(jnp.int32)
    w = [row(1), row(2), row(3)]
    w.append(1.0 - w[0] - w[1] - w[2])
    return cell, cell & (NY - 1), w, row(4)


def gather_kernel(
    bucket_ref, state_ref, sorted_ref, pos_ref, recv_ref, own_ref, out_ref, value_ref, table_ref
):
    devices = recv_ref.shape[0]
    chunks = devices * CAP // CHUNK
    value_ref[...] = jnp.zeros_like(value_ref)

    def table_body(b, carry):
        turned = state_ref[b].T
        shifted = pltpu.roll(turned, ROWS - 1, 1)
        table_ref[b] = jnp.concatenate(
            [
                jnp.concatenate(parts_of(turned, 2), axis=1),
                jnp.concatenate(parts_of(shifted, 2), axis=1),
            ],
            axis=0,
        )
        return carry

    lax.fori_loop(0, BUCKETS, table_body, 0)

    def tile_body(i, carry):
        for t in range(4):
            t = 4 * i + t
            cell, y, w, _ = tile_rows(sorted_ref, t)
            hot = one_hot(iota((ROWS, SUB), 0) == (cell >> 8))
            spots = iota((NY, SUB), 0)
            here = spots == lane_of(y)
            above = spots == lane_of(y + 1)
            got = nn(table_ref[bucket_ref[0, t]], jnp.concatenate([hot, hot], axis=0))
            first = jnp.where(here, w[0], jnp.where(above, w[2], 0.0))
            second = jnp.where(here, w[1], jnp.where(above, w[3], 0.0))
            value_ref[pl.ds(t, 1), :] = jnp.sum(
                first * got[:NY] + second * got[NY:], axis=0, keepdims=True
            )
        return carry

    lax.fori_loop(0, (bucket_ref[0, CAP - 1] + 3) // 4, tile_body, 0)
    table = jnp.concatenate(parts_of(value_ref[...].T, 2), axis=1)
    depth = value_ref.shape[0]

    def unsort_body(c, carry):
        pos = pos_ref[pl.ds(c, 1), :]
        high = one_hot(iota((depth, CHUNK), 0) == (pos >> 8))
        got = nn(table, jnp.concatenate([high, high], axis=0))
        low = iota((SUB, CHUNK), 0) == (pos & (SUB - 1))
        row = jnp.sum(jnp.where(low, got, 0.0), axis=0, keepdims=True)
        per = CHUNK // CAP
        block = jnp.concatenate([row[:, i * CAP : (i + 1) * CAP] for i in range(per)], axis=0)
        out_ref[pl.ds(pl.multiple_of(c * per, per), per), :CAP] = block
        return carry

    lax.fori_loop(0, chunks, unsort_body, 0, unroll=2)
    d = recv_ref[:, 4, :]
    r = recv_ref[:, 5, :]
    image = out_ref[:, :CAP] + recv_ref[:, 6, :] * d
    out_ref[:, :CAP] = image
    own = own_ref[...]
    lane = iota((1, CAP), 1)
    sums = jnp.where(lane == 0, jnp.sum(own * own), 0.0)
    sums = jnp.where(lane == 1, jnp.sum(d * image), sums)
    sums = jnp.where(lane == 2, jnp.sum(r * image), sums)
    sums = jnp.where(lane == 3, jnp.sum(image * image), sums)
    out_ref[:, CAP:] = jnp.broadcast_to(sums, (devices, CAP))


def final_kernel(
    out_ref,
    route_ref,
    rank_ref,
    dual_ref,
    d_ref,
    r_ref,
    dual_out,
    res_out,
    dir_out,
    halfway,
    landing,
    hot_ref,
    send_sem,
    recv_sem,
):
    g = lax.axis_index("tm")
    t = lax.axis_index("space")
    groups = lax.axis_size("tm")
    strips = lax.axis_size("space")
    devices = groups * strips

    barrier = pltpu.get_barrier_semaphore()
    for step in range(1, groups):
        pl.semaphore_signal(
            barrier, inc=1, device_id=(around(g, step, groups), t), device_id_type=MESH
        )

    def greet(i, carry):
        other = (g, around(t, i, strips))
        pl.semaphore_signal(barrier, inc=1, device_id=other, device_id_type=MESH)
        return carry

    lax.fori_loop(1, strips, greet, 0, unroll=True)
    pl.semaphore_wait(barrier, groups + strips - 2)

    def along_space(i, carry):
        strip = around(t, i, strips)
        pltpu.make_async_remote_copy(
            src_ref=out_ref.at[:, strip],
            dst_ref=halfway.at[:, strip_of(t)],
            send_sem=send_sem.at[0],
            recv_sem=recv_sem.at[0],
            device_id=(g, strip),
            device_id_type=MESH,
        ).start()
        return carry

    lax.fori_loop(1, strips, along_space, 0, unroll=True)
    pltpu.make_async_copy(out_ref.at[:, t], halfway.at[:, strip_of(t)], recv_sem.at[0]).start()
    chunks = route_ref.shape[1] // CHUNK
    for c in range(chunks):
        lanes = slice(c * CHUNK, (c + 1) * CHUNK)
        hot_ref[c] = one_hot(iota((devices, CHUNK), 0) == route_ref[:, lanes])
    pltpu.make_async_copy(halfway, halfway, recv_sem.at[0]).wait()
    for step in range(1, groups):
        group = around(g, step, groups)
        pltpu.make_async_remote_copy(
            src_ref=halfway.at[group],
            dst_ref=landing.at[g],
            send_sem=send_sem.at[1],
            recv_sem=recv_sem.at[1],
            device_id=(group, t),
            device_id_type=MESH,
        ).start()
    pltpu.make_async_copy(halfway.at[g], landing.at[g], recv_sem.at[1]).start()
    pltpu.make_async_copy(landing, landing, recv_sem.at[1]).wait()
    returned = landing[...].reshape(devices, 2 * CAP)
    sums = jnp.sum(returned[:, CAP:], axis=0, keepdims=True)
    lane = iota((1, CAP), 1)
    norm_now, curvature, cross, square = [
        jnp.sum(jnp.where(lane == i, sums, 0.0), axis=1, keepdims=True) for i in range(4)
    ]
    step = norm_now / curvature
    norm_next = norm_now - 2.0 * step * cross + step * step * square
    ratio = norm_next / norm_now
    table = jnp.concatenate(parts_of(returned[:, :CAP].T, 2), axis=1)
    for c in range(chunks):
        lanes = slice(c * CHUNK, (c + 1) * CHUNK)
        hot = hot_ref[c]
        got = nn(table, jnp.concatenate([hot, hot], axis=0))
        mask = iota((CAP, CHUNK), 0) == rank_ref[:, lanes]
        image = jnp.sum(jnp.where(mask, got, 0.0), axis=0, keepdims=True)
        d = d_ref[:, lanes]
        res = r_ref[:, lanes] - step * image
        dual_out[:, lanes] = dual_ref[:, lanes] + step * d
        res_out[:, lanes] = res
        dir_out[:, lanes] = res + ratio * d
    rest = out_ref.at[:, pl.ds(0, strips - 1)]
    pltpu.make_async_copy(rest, rest, send_sem.at[0]).wait()
    rest = halfway.at[pl.ds(0, groups - 1)]
    pltpu.make_async_copy(rest, rest, send_sem.at[1]).wait()


def back(x):
    return jnp.concatenate([pltpu.roll(x[:, HALF:], 1, 1), x[:, :HALF]], axis=1)


def ahead(x):
    return jnp.concatenate([x[:, HALF:], pltpu.roll(x[:, :HALF], HALF - 1, 1)], axis=1)


def sweep_kernel(
    forcing_ref,
    coef,
    state_ref,
    scalars,
    scalar_sem,
    hop_a,
    hop_x,
    fin_a,
    fin_x,
    adj_out,
    adj_in,
    force_out,
    force_in,
    cov_out,
    cov_in,
    fwd_out,
    fwd_in,
    fext,
    u0,
    u1,
    u2,
    u3,
    v0,
    v1,
    v2,
    v3,
    inc,
    hop_sem,
    adj_sem,
    force_sem,
    cov_sem,
    fwd_sem,
):
    g = lax.axis_index("tm")
    t = lax.axis_index("space")
    groups = lax.axis_size("tm")
    strips = lax.axis_size("space")
    strip = strip_of(t)
    left = (g, strip_of(lax.rem(strip + strips - 1, strips)))
    right = (g, strip_of(lax.rem(strip + 1, strips)))
    later = (lax.rem(g + 1, groups), t)
    earlier = (lax.rem(g + groups - 1, groups), t)
    sides = (left, right)
    first_strip = strip == 0
    last_strip = strip == strips - 1
    last_group = g == groups - 1
    first_group = g == 0

    barrier = pltpu.get_barrier_semaphore()
    for other in (left, right, later, earlier):
        pl.semaphore_signal(barrier, inc=1, device_id=other, device_id_type=MESH)

    fetch = pltpu.make_async_copy(coef.at[5 * LEV, :, pl.ds(0, CAP)], scalars, scalar_sem)
    fetch.start()
    pl.semaphore_wait(barrier, 4)

    def to_side(src, dst, sems, side, *idx):
        return pltpu.make_async_remote_copy(
            src_ref=src,
            dst_ref=dst,
            send_sem=sems.at[(0, side) + idx],
            recv_sem=sems.at[(1, 1 - side) + idx],
            device_id=sides[side],
            device_id_type=MESH,
        )

    def wait_side(dst, sems, slot, *idx):
        pltpu.make_async_remote_copy(
            src_ref=dst,
            dst_ref=dst,
            send_sem=sems.at[(0, slot) + idx],
            recv_sem=sems.at[(1, slot) + idx],
            device_id=sides[slot],
            device_id_type=MESH,
        ).wait_recv()

    def hop(src, dst, way, level, device):
        return pltpu.make_async_remote_copy(
            src_ref=src.at[level],
            dst_ref=dst.at[level],
            send_sem=hop_sem.at[way, 0, level],
            recv_sem=hop_sem.at[way, 1, level],
            device_id=device,
            device_id_type=MESH,
        )

    upper = iota((CX, NY), 0) < 4

    def pack(out, level, first, value):
        for j in range(NV // 2):
            one = value[2 * j]
            two = pltpu.roll(value[2 * j + 1], 4, 0)
            out[0, level, first + j] = jnp.where(upper, one, two)
            out[1, level, first + j] = jnp.where(upper, two, one)

    def join(arrived, level, first):
        tiles = []
        for j in range(NV // 2):
            from_left = arrived[0, level, first + j]
            from_right = arrived[1, level, first + j]
            tiles.append(jnp.where(upper, from_right, from_left))
            tiles.append(pltpu.roll(jnp.where(upper, from_left, from_right), 4, 0))
        return tiles

    def exchange(out, arrived, sems, level):
        for side in range(2):
            to_side(
                out.at[side, level], arrived.at[1 - side, level], sems, side, level
            ).start()

    def await_sides(arrived, sems, level):
        for slot in range(2):
            wait_side(arrived.at[slot, level], sems, slot, level)

    def send_forcing(l):
        for i in range(3):
            pack(force_out, l, 2 * i, [forcing_ref[i, v, l] for v in range(NV)])
        exchange(force_out, force_in, force_sem, l)

    edge = jnp.zeros((NV, EXT, NY), F32)
    for u in (u0, u1, u2, u3, v0, v1, v2, v3):
        u[0] = edge
        u[LEV + 1] = edge

    @pl.when(last_group)
    def _():
        hop_a[...] = jnp.zeros_like(hop_a)

    @pl.when(first_group)
    def _():
        hop_x[...] = jnp.zeros_like(hop_x)

    @pl.when(jnp.logical_not(last_group))
    def _():
        def early(l, carry):
            send_forcing(l)
            return carry

        lax.fori_loop(0, LEV, early, 0)

    inside = inside_grid(first_strip, last_strip)
    fetch.wait()
    mix = [[coupling_step * scalars[v, w] for w in range(NV)] for v in range(NV)]

    def adjoint_level(u, l, rows):
        c, w, e, s, n = [coef[i * LEV + l] for i in range(5)]
        now = [u[l + 1, v] for v in range(NV)]
        out = []
        for v in range(NV):
            a = now[v]
            res = c[:rows] * a[:rows]
            res = res + pltpu.roll(w * a, EXT - 1, 0)[:rows] + pltpu.roll(e * a, 1, 0)[:rows]
            res = res + ahead(s[:rows] * a[:rows]) + back(n[:rows] * a[:rows])
            res = res + vertical * (u[l, v, :rows] + u[l + 2, v, :rows])
            for k in range(NV):
                res = res + mix[k][v] * now[k][:rows]
            out.append(res)
        return out

    def forward_level(u, l, rows):
        c, w, e, s, n = [coef[i * LEV + l][:rows] for i in range(5)]
        now = [u[l + 1, v] for v in range(NV)]
        out = []
        for v in range(NV):
            a = now[v]
            res = c * a[:rows]
            res = res + w * pltpu.roll(a, 1, 0)[:rows] + e * pltpu.roll(a, EXT - 1, 0)[:rows]
            res = res + s * back(a[:rows]) + n * ahead(a[:rows])
            res = res + vertical * (u[l, v, :rows] + u[l + 2, v, :rows])
            for k in range(NV):
                res = res + mix[v][k] * now[k][:rows]
            out.append(res)
        return out

    def in_range(l):
        return (l >= 0) & (l < LEV)

    def adjoint_tick(k):
        @pl.when(in_range(k))
        def _():
            @pl.when(jnp.logical_not(last_group))
            def _():
                hop(hop_a, hop_a, 0, k, later).wait_recv()

            value = [hop_a[k, v] + forcing_ref[3, v, k] for v in range(NV)]
            pack(adj_out, k, 0, value)
            exchange(adj_out, adj_in, adj_sem, k)

            @pl.when(last_group)
            def _():
                send_forcing(k)

            for v in range(NV):
                u0[k + 1, v, :CX] = value[v]

        m = k - ADJ_DELAY

        @pl.when(in_range(m))
        def _():
            await_sides(adj_in, adj_sem, m)
            await_sides(force_in, force_sem, m)
            for v, tile in enumerate(join(adj_in, m, 0)):
                u0[m + 1, v, CX:] = tile
            for i in range(3):
                for v, tile in enumerate(join(force_in, m, 2 * i)):
                    fext[i, m, v] = tile

        for i, (src, dst) in enumerate(((u0, u1), (u1, u2), (u2, u3))):
            level = m - 1 - i

            @pl.when(in_range(level))
            def _():
                res = adjoint_level(src, level, EXT)
                for v in range(NV):
                    dst[level + 1, v, :CX] = res[v][:CX] + forcing_ref[2 - i, v, level]
                    dst[level + 1, v, CX:] = res[v][CX:] + fext[2 - i, level, v]

        level = m - 4

        @pl.when(in_range(level))
        def _():
            res = adjoint_level(u3, level, CX)
            for v in range(NV):
                fin_a[level, v] = res[v]

            @pl.when(jnp.logical_not(first_group))
            def _():
                hop(fin_a, hop_a, 0, level, earlier).start()

            pack(cov_out, level, 0, res)
            exchange(cov_out, cov_in, cov_sem, level)

    lane_low = jnp.where(iota((CX, NY), 1) > 0, 1.0, 0.0)
    lane_high = jnp.where(iota((CX, NY), 1) < NY - 1, 1.0, 0.0)
    keep = jnp.where(inside, 1.0, 0.0)

    def cov_tick(l):
        @pl.when(in_range(l))
        def _():
            await_sides(cov_in, cov_sem, l)
            for v, tile in enumerate(join(cov_in, l, 0)):
                scale = scalars[CX + v, l]
                ext = jnp.concatenate([fin_a[l, v], tile], axis=0) * (keep * scale)
                ext = 0.5 * ext + 0.25 * (pltpu.roll(ext, 1, 0) + pltpu.roll(ext, EXT - 1, 0))
                ext = ext * keep
                ext = 0.5 * ext + 0.25 * (pltpu.roll(ext, 1, 0) + pltpu.roll(ext, EXT - 1, 0))
                own = ext[:CX]
                for _ in range(2):
                    own = 0.5 * own + 0.25 * (lane_low * back(own) + lane_high * ahead(own))
                inc[l, v] = own * scale

    fwd_delay = jnp.where(first_group, FIRST_DELAY, FWD_DELAY)

    def forward_tick(k):
        @pl.when(in_range(k))
        def _():
            @pl.when(jnp.logical_not(first_group))
            def _():
                hop(hop_x, hop_x, 1, k, earlier).wait_recv()

            value = [hop_x[k, v] + inc[k, v] for v in range(NV)]
            pack(fwd_out, k, 0, value)
            exchange(fwd_out, fwd_in, fwd_sem, k)
            for v in range(NV):
                v0[k + 1, v, :CX] = value[v]

        m = k - fwd_delay

        @pl.when(in_range(m))
        def _():
            await_sides(fwd_in, fwd_sem, m)
            for v, tile in enumerate(join(fwd_in, m, 0)):
                v0[m + 1, v, CX:] = tile

        for i, (src, dst) in enumerate(((v0, v1), (v1, v2), (v2, v3))):
            level = m - 1 - i

            @pl.when(in_range(level))
            def _():
                res = forward_level(src, level, EXT)
                for v in range(NV):
                    dst[level + 1, v] = res[v]
                    state_ref[i, v, level] = res[v][:CX]

        level = m - 4

        @pl.when(in_range(level))
        def _():
            res = forward_level(v3, level, CX)
            for v in range(NV):
                state_ref[3, v, level] = res[v]
                fin_x[level, v] = res[v]

            @pl.when(jnp.logical_not(last_group))
            def _():
                hop(fin_x, hop_x, 1, level, later).start()

    adjoint_ticks = LEV + ADJ_DELAY + 4
    behind = jnp.where(first_group, ADJ_DELAY + 4 + COV_DELAY, adjoint_ticks)

    def tick(k, carry):
        adjoint_tick(k)
        cov_tick(k - (ADJ_DELAY + 4 + COV_DELAY))
        forward_tick(k - behind)
        return carry

    lax.fori_loop(0, behind + LEV + fwd_delay + 4, tick, 0)

    def drain(l, carry):
        for out, arrived, sems in (
            (adj_out, adj_in, adj_sem),
            (force_out, force_in, force_sem),
            (cov_out, cov_in, cov_sem),
            (fwd_out, fwd_in, fwd_sem),
        ):
            for side in range(2):
                to_side(
                    out.at[side, l], arrived.at[1 - side, l], sems, side, l
                ).wait_send()

        @pl.when(jnp.logical_not(first_group))
        def _():
            hop(fin_a, hop_a, 0, l, earlier).wait_send()

        @pl.when(jnp.logical_not(last_group))
        def _():
            hop(fin_x, hop_x, 1, l, later).wait_send()

        return carry

    lax.fori_loop(0, LEV, drain, 0)


def sweeps(forcing, coef):
    state = pltpu.VMEM((LEV, NV, CX, NY), F32)
    padded = pltpu.VMEM((LEV + 2, NV, EXT, NY), F32)
    edges = pltpu.VMEM((2, LEV, 2, CX, NY), F32)
    wide_edges = pltpu.VMEM((2, LEV, 6, CX, NY), F32)
    levels = pltpu.SemaphoreType.DMA((2, 2, LEV))
    return pl.pallas_call(
        sweep_kernel,
        out_shape=jax.ShapeDtypeStruct((STEPS, NV, LEV, CX, NY), F32),
        in_specs=[VMEM, VMEM],
        out_specs=VMEM,
        scratch_shapes=[
            pltpu.SMEM((EXT, CAP), F32),
            pltpu.SemaphoreType.DMA,
        ]
        + [state] * 4
        + [edges] * 2
        + [wide_edges] * 2
        + [edges] * 4
        + [pltpu.VMEM((3, LEV, NV, CX, NY), F32)]
        + [padded] * 8
        + [state]
        + [levels] * 5,
        compiler_params=params(34, collective_id=1, has_side_effects=True),
        name="sweeps",
    )(forcing, coef)


def per_device(
    dual_weights,
    direction,
    residual_dual,
    obs_var,
    obs_route,
    obs_cell,
    obs_interp,
    wind_x,
    wind_y,
    coupling,
    cov_scale,
):
    grid = (lax.axis_size("tm"), lax.axis_size("space"))
    devices = grid[0] * grid[1]
    rows = direction.shape[0]
    wide = (1, rows)
    route = obs_route.reshape(1, rows)
    tiles = pltpu.VMEM((devices, 8, CAP), F32)
    arrived, rank, coef = pl.pallas_call(
        route_kernel,
        out_shape=(
            jax.ShapeDtypeStruct((devices, 8, CAP), F32),
            jax.ShapeDtypeStruct((1, rows), jnp.int32),
            jax.ShapeDtypeStruct((5 * LEV + 1, EXT, NY), F32),
        ),
        in_specs=[ANY] * 10,
        out_specs=(VMEM, VMEM, VMEM),
        scratch_shapes=[
            tiles,
            tiles,
            pltpu.VMEM((devices, sum(PACK_PARTS) * CAP), F32),
            pltpu.VMEM((2, LEV, CX, NY), F32),
            pltpu.VMEM((3, 2, LEV, CX, NY), F32),
            pltpu.VMEM((1, rows), jnp.int32),
            pltpu.VMEM((1, rows), jnp.int32),
            pltpu.VMEM((4, rows), F32),
            pltpu.VMEM((1, rows), F32),
            pltpu.VMEM((1, rows), F32),
            pltpu.VMEM((1, rows), F32),
            pltpu.VMEM((1, LEV, CX, NY), F32),
            pltpu.VMEM((1, LEV, CX, NY), F32),
            pltpu.VMEM((NV, NV), F32),
            pltpu.VMEM((1, NV, LEV), F32),
            pltpu.SemaphoreType.DMA,
            pltpu.SemaphoreType.DMA,
            pltpu.SemaphoreType.DMA((2, 3)),
            pltpu.SemaphoreType.DMA((10,)),
        ],
        compiler_params=params(58, collective_id=2, has_side_effects=True),
        name="route",
    )(
        route,
        obs_cell.reshape(1, rows),
        obs_interp,
        direction.reshape(1, rows),
        residual_dual.reshape(1, rows),
        obs_var.reshape(1, rows),
        wind_x,
        wind_y,
        coupling,
        cov_scale,
    )
    slots = devices * CAP
    forcing, ordered, position, starts = pl.pallas_call(
        sort_scatter_kernel,
        out_shape=(
            jax.ShapeDtypeStruct((BUCKETS, ROWS, NY), F32),
            jax.ShapeDtypeStruct((SORT_PARTS // 2, SORT_ROWS, CAP), F32),
            jax.ShapeDtypeStruct((slots // CHUNK, CHUNK), jnp.int32),
            jax.ShapeDtypeStruct((1, CAP), jnp.int32),
        ),
        in_specs=[VMEM],
        out_specs=(VMEM, VMEM, VMEM, VMEM),
        scratch_shapes=[
            pltpu.VMEM((slots // CHUNK, CHUNK), F32),
            pltpu.VMEM((SORT_ROWS, SORT_PARTS * CAP), F32),
        ],
        compiler_params=params(20),
        name="sort_scatter",
    )(arrived)
    states = sweeps(forcing.reshape(STEPS, NV, LEV, CX, NY), coef)
    returning = pl.pallas_call(
        gather_kernel,
        out_shape=jax.ShapeDtypeStruct((devices, 2 * CAP), F32),
        in_specs=[SMEM, VMEM, VMEM, VMEM, VMEM, VMEM],
        out_specs=VMEM,
        scratch_shapes=[
            pltpu.VMEM((CAP, SUB), F32),
            pltpu.VMEM((BUCKETS, 2 * NY, 2 * ROWS), BF16),
        ],
        compiler_params=params(20),
        name="gather",
    )(
        starts,
        states.reshape(BUCKETS, ROWS, NY),
        ordered,
        position,
        arrived,
        residual_dual.reshape(wide),
    )
    out = jax.ShapeDtypeStruct(wide, F32)
    results = pl.pallas_call(
        final_kernel,
        out_shape=(out, out, out),
        in_specs=[VMEM] * 6,
        out_specs=(VMEM, VMEM, VMEM),
        scratch_shapes=[
            pltpu.VMEM(grid + (1, 2 * CAP), F32),
            pltpu.VMEM(grid + (1, 2 * CAP), F32),
            pltpu.VMEM((rows // CHUNK, devices, CHUNK), BF16),
            pltpu.SemaphoreType.DMA((2,)),
            pltpu.SemaphoreType.DMA((2,)),
        ],
        compiler_params=params(12, collective_id=3, has_side_effects=True),
        name="final",
    )(
        returning.reshape(grid + (1, 2 * CAP)),
        route.reshape(wide),
        rank.reshape(wide),
        dual_weights.reshape(wide),
        direction.reshape(wide),
        residual_dual.reshape(wide),
    )
    return tuple(r.reshape(rows) for r in results)


def solution(mesh):
    return jax.shard_map(
        per_device,
        mesh=mesh,
        in_specs=(
            P(("tm", "space")),
            P(("tm", "space")),
            P(("tm", "space")),
            P(("tm", "space")),
            P(("tm", "space"), None),
            P(("tm", "space")),
            P(None, ("tm", "space")),
            P("tm", None, "space", None),
            P("tm", None, "space", None),
            P(),
            P("tm", None, None),
        ),
        out_specs=(P(("tm", "space")), P(("tm", "space")), P(("tm", "space"))),
        check_vma=False,
    )
```

```python
import functools

import jax
import jax.numpy as jnp
from jax import lax
from jax.experimental import pallas as pl
from jax.experimental.pallas import tpu as pltpu
from jax.sharding import PartitionSpec as P

STEPS = 4
NV = 4
LEV = 16
CX = 8
NY = 256
CAP = 128
ROWS = LEV * CX
BUCKETS = STEPS * NV
SORT_ROWS = 160
CHUNK = 1024
SUB = 256
HALF = NY // 2
EXT = 2 * CX
ADJ_DELAY = 4
COV_DELAY = 4
FWD_DELAY = 4
FIRST_DELAY = 4
diffusion = 0.05
vertical = 0.05
coupling_step = 0.05
MESH = pl.DeviceIdType.MESH
F32 = jnp.float32
BF16 = jnp.bfloat16
VMEM = pl.BlockSpec(memory_space=pltpu.VMEM)
SMEM = pl.BlockSpec(memory_space=pltpu.SMEM)
ANY = pl.BlockSpec(memory_space=pltpu.HBM)


def params(mib, **kw):
    return pltpu.CompilerParams(vmem_limit_bytes=mib * 1024 * 1024, **kw)


def iota(shape, dim):
    return lax.broadcasted_iota(jnp.int32, shape, dim)


def parts_of(value, count):
    out = []
    for _ in range(count - 1):
        head = value.astype(BF16)
        out.append(head)
        value = value - head.astype(F32)
    out.append(value.astype(BF16))
    return out


def nt(a, b):
    return lax.dot_general(a, b, (((1,), (1,)), ((), ())), preferred_element_type=F32)


def nn(a, b):
    return jnp.dot(a, b, preferred_element_type=F32)


def one_hot(mask):
    return jnp.where(mask, 1.0, 0.0).astype(BF16)


def short_hot(ids, row):
    same = ids.astype(jnp.int16) == row.astype(jnp.int16)
    return jnp.where(same, jnp.ones((), BF16), jnp.zeros((), BF16))


def running_rank(hot, hot_mask, carry, upper):
    keys = hot.shape[0]
    pieces = CHUNK // SUB
    stacked = jnp.concatenate([hot[:, i * SUB : (i + 1) * SUB] for i in range(pieces)], axis=0)
    counted = nn(stacked, upper)
    rows = []
    for i in range(pieces):
        mask = hot_mask[:, i * SUB : (i + 1) * SUB]
        part = counted[i * keys : (i + 1) * keys] + carry
        rows.append(jnp.sum(jnp.where(mask, part, 0.0), axis=0, keepdims=True))
        carry = carry + jnp.sum(jnp.where(mask, 1.0, 0.0), axis=1, keepdims=True)
    return jnp.concatenate(rows, axis=1), carry


def lane_of(y):
    return (y >> 1) + (y & 1) * HALF


def upper_strict():
    return one_hot(iota((SUB, SUB), 0) < iota((SUB, SUB), 1))


PACK_PARTS = (3, 2, 2, 2, 2, 2, 2)


ROW_STRIPS = 8


def backwards(within):
    return ROW_STRIPS - 2 - within + 2 * (within % 2)


def strip_of(t):
    row = t // ROW_STRIPS
    within = t % ROW_STRIPS
    return row * ROW_STRIPS + jnp.where(row % 2 == 1, backwards(within), within)


def around(start, step, size):
    index = start + step
    return jnp.where(index >= size, index - size, index)


def everyone(act):
    g = lax.axis_index("tm")
    t = lax.axis_index("space")
    groups = lax.axis_size("tm")
    rows = lax.axis_size("space") // ROW_STRIPS
    ways = []
    for step in range(ROW_STRIPS):
        within = around(t % ROW_STRIPS, step, ROW_STRIPS)
        ways.append((within, backwards(within)))
    for group_step in range(groups):
        group = around(g, group_step, groups)
        for row_step in range(rows):
            row = around(t // ROW_STRIPS, row_step, rows)
            first = row * ROW_STRIPS
            odd = row % 2 == 1
            for step, (within, turned) in enumerate(ways):
                if group_step or row_step or step:
                    act(group, first + within, first + jnp.where(odd, turned, within))


def greet_all():
    barrier = pltpu.get_barrier_semaphore()
    everyone(
        lambda group, place, strip: pl.semaphore_signal(
            barrier, inc=1, device_id=(group, place), device_id_type=MESH
        )
    )


def await_all():
    devices = lax.axis_size("tm") * lax.axis_size("space")
    pl.semaphore_wait(pltpu.get_barrier_semaphore(), devices - 1)


def send_all(me, out, arrived, send_sem, recv_sem):
    strips = lax.axis_size("space")

    def start(group, place, strip):
        pltpu.make_async_remote_copy(
            src_ref=out.at[group * strips + strip],
            dst_ref=arrived.at[me],
            send_sem=send_sem,
            recv_sem=recv_sem,
            device_id=(group, place),
            device_id_type=MESH,
        ).start()

    own = lax.axis_index("tm") * strips + strip_of(lax.axis_index("space"))
    pltpu.make_async_copy(out.at[own], arrived.at[me], recv_sem).start()
    everyone(start)


def receive_all(arrived, recv_sem):
    pltpu.make_async_copy(arrived, arrived, recv_sem).wait()


def finish_sends(out, send_sem):
    rest = out.at[pl.ds(0, out.shape[0] - 1)]
    pltpu.make_async_copy(rest, rest, send_sem).wait()


def my_index():
    return lax.axis_index("tm") * lax.axis_size("space") + lax.axis_index("space")


def route_kernel(
    route_hbm,
    cell_hbm,
    interp_hbm,
    d_hbm,
    r_hbm,
    var_hbm,
    wind_x_hbm,
    wind_y_hbm,
    coupling_hbm,
    scale_hbm,
    arrived_ref,
    rank_ref,
    coef,
    out_ref,
    landing,
    acc_ref,
    wind_own,
    wind_in,
    route_ref,
    cell_ref,
    interp_ref,
    d_ref,
    r_ref,
    var_ref,
    wind_x_ref,
    wind_y_ref,
    coupling_ref,
    scale_ref,
    send_sem,
    recv_sem,
    wind_sem,
    fetch_sem,
):
    fetches = [
        pltpu.make_async_copy(src, dst, fetch_sem.at[i])
        for i, (src, dst) in enumerate(
            (
                (wind_x_hbm, wind_x_ref),
                (wind_y_hbm, wind_y_ref),
                (route_hbm, route_ref),
                (cell_hbm, cell_ref),
                (interp_hbm, interp_ref),
                (d_hbm, d_ref),
                (r_hbm, r_ref),
                (var_hbm, var_ref),
                (coupling_hbm, coupling_ref),
                (scale_hbm, scale_ref),
            )
        )
    ]
    for fetch in fetches:
        fetch.start()
    me = my_index()
    g = lax.axis_index("tm")
    t = lax.axis_index("space")
    strips = lax.axis_size("space")
    strip = strip_of(t)
    stays = strip == t
    first_strip = strip == 0
    last_strip = strip == strips - 1
    greet_all()
    for fetch in fetches:
        fetch.wait()

    order = iota((NY, NY), 1)
    order = one_hot(iota((NY, NY), 0) == (order % HALF) * 2 + order // HALF)
    for i, wind in enumerate((wind_x_ref, wind_y_ref)):
        turned = parts_of(wind[...].reshape(LEV * CX, NY), 3)
        turned = nn(turned[0], order) + nn(turned[1], order) + nn(turned[2], order)
        wind_own[i] = turned.reshape(LEV, CX, NY)

    devices = out_ref.shape[0]
    upper = upper_strict()
    acc_ref[...] = jnp.zeros_like(acc_ref)

    def body(c, carry):
        lanes = pl.ds(pl.multiple_of(c * CHUNK, CHUNK), CHUNK)
        dest = route_ref[:, lanes]
        mask = iota((devices, CHUNK), 0) == dest
        hot = one_hot(mask)
        rank, carry = running_rank(hot, mask, carry, upper)
        rank = rank.astype(jnp.int32)
        rank_ref[:, lanes] = rank
        slot = one_hot(iota((CAP, CHUNK), 0) == rank)
        fields = [(cell_ref[:, lanes] + 1).astype(F32)]
        fields += [interp_ref[f : f + 1, lanes] for f in range(3)]
        fields += [d_ref[:, lanes], r_ref[:, lanes], var_ref[:, lanes]]
        pieces = []
        for field, count in zip(fields, PACK_PARTS):
            for part in parts_of(field, count):
                pieces.append(slot * part)
        acc_ref[...] += nt(hot, jnp.concatenate(pieces, axis=0))
        return carry

    chunks = route_ref.shape[1] // CHUNK
    carry = jnp.zeros((devices, 1), F32)
    carry = lax.fori_loop(0, chunks // 2, body, carry, unroll=2)
    await_all()

    def to_strip(slot):
        other = lax.rem(t + strips + 1 - slot, strips)
        return pltpu.make_async_remote_copy(
            src_ref=wind_own,
            dst_ref=wind_in.at[slot],
            send_sem=wind_sem.at[0, slot],
            recv_sem=wind_sem.at[1, slot],
            device_id=(g, strip_of(other)),
            device_id_type=MESH,
        )

    to_strip(0).start()
    to_strip(2).start()

    @pl.when(stays)
    def _():
        pltpu.make_async_copy(wind_own, wind_in.at[1], wind_sem.at[1, 1]).start()

    @pl.when(jnp.logical_not(stays))
    def _():
        to_strip(1).start()

    lax.fori_loop(chunks // 2, chunks, body, carry, unroll=2)
    at = 0
    for f, count in enumerate(PACK_PARTS):
        total = acc_ref[:, at * CAP : (at + 1) * CAP]
        for i in range(1, count):
            total = total + acc_ref[:, (at + i) * CAP : (at + i + 1) * CAP]
        at += count
        out_ref[:, f, :] = total
    out_ref[:, 7, :] = jnp.zeros_like(out_ref[:, 7, :])
    send_all(me, out_ref, landing, send_sem, recv_sem)
    for slot in range(3):
        pltpu.make_async_copy(wind_in.at[slot], wind_in.at[slot], wind_sem.at[1, slot]).wait()

    column = iota((EXT, NY), 0)
    lane = iota((EXT, NY), 1)
    west_ok = jnp.logical_not(first_strip & (column == 0))
    east_ok = jnp.logical_not(last_strip & (column == CX - 1))
    inside = inside_grid(first_strip, last_strip)
    west_ok = inside & west_ok
    east_ok = inside & east_ok
    south_ok = inside & (lane > 0)
    north_ok = inside & (lane < NY - 1)
    from_right = iota((CX, NY), 0) < 4

    def coef_body(l, carry):
        wx, wy = [
            jnp.concatenate(
                [wind_in[1, i, l], jnp.where(from_right, wind_in[2, i, l], wind_in[0, i, l])], axis=0
            )
            for i in range(2)
        ]
        coef[l] = jnp.where(
            inside, 1.0 - jnp.abs(wx) - jnp.abs(wy) - 4.0 * diffusion - 2.0 * vertical, 0.0
        )
        coef[LEV + l] = jnp.where(west_ok, jnp.maximum(wx, 0.0) + diffusion, 0.0)
        coef[2 * LEV + l] = jnp.where(east_ok, jnp.maximum(-wx, 0.0) + diffusion, 0.0)
        coef[3 * LEV + l] = jnp.where(south_ok, jnp.maximum(wy, 0.0) + diffusion, 0.0)
        coef[4 * LEV + l] = jnp.where(north_ok, jnp.maximum(-wy, 0.0) + diffusion, 0.0)
        return carry

    lax.fori_loop(0, LEV, coef_body, 0)
    coef[5 * LEV] = jnp.zeros((EXT, NY), F32)
    coef[5 * LEV, :NV, :NV] = coupling_ref[...]
    coef[5 * LEV, CX : CX + NV, :LEV] = scale_ref[0]
    receive_all(landing, recv_sem)
    arrived_ref[...] = landing[...]
    to_strip(0).wait_send()
    to_strip(2).wait_send()

    @pl.when(jnp.logical_not(stays))
    def _():
        to_strip(1).wait_send()

    finish_sends(out_ref, send_sem)


def inside_grid(first_strip, last_strip):
    column = iota((EXT, NY), 0)
    return jnp.logical_not(
        (first_strip & (column >= 12)) | (last_strip & (column >= 8) & (column < 12))
    )


def row_of(ref, field, c):
    per = CHUNK // CAP
    base = c * per
    return jnp.concatenate([ref[base + i, field : field + 1, :] for i in range(per)], axis=1)


SORT_PARTS = 10


def sort_scatter_kernel(recv_ref, forcing_ref, sorted_ref, pos_ref, bucket_ref, rank_ref, acc_ref):
    chunks = recv_ref.shape[0] * CAP // CHUNK
    upper = upper_strict()

    def bucket_of(c):
        cell = row_of(recv_ref, 0, c).astype(jnp.int32) - 1
        bucket = jnp.where(cell < 0, -1, cell // (ROWS * NY))
        return cell, iota((BUCKETS, CHUNK), 0) == bucket

    def count_body(c, carry):
        _, mask = bucket_of(c)
        rank, carry = running_rank(one_hot(mask), mask, carry, upper)
        rank_ref[pl.ds(c, 1), :] = rank
        return carry

    totals = lax.fori_loop(0, chunks, count_body, jnp.zeros((BUCKETS, 1), F32), unroll=4)
    tiles = jnp.floor((totals + (SUB - 1.0)) * (1.0 / SUB))
    before = jnp.zeros((BUCKETS, 1), F32)
    ids = iota((BUCKETS, 1), 0)
    for b in range(BUCKETS):
        here = jnp.sum(jnp.where(ids == b, tiles, 0.0))
        before = before + jnp.where(ids > b, here, 0.0)
    tile_ids = iota((BUCKETS, CAP), 1).astype(F32)
    of_tile = jnp.sum(jnp.where(tile_ids >= before + tiles, 1.0, 0.0), axis=0, keepdims=True)
    used = jnp.sum(tiles)
    of_tile = jnp.where(
        iota((1, CAP), 1) == CAP - 1, used, jnp.minimum(of_tile, BUCKETS - 1.0)
    )
    bucket_ref[...] = of_tile.astype(jnp.int32)
    used = used.astype(jnp.int32)
    offsets = before * float(SUB)

    acc_ref[...] = jnp.zeros_like(acc_ref)

    def sort_body(c, carry):
        cell, mask = bucket_of(c)
        offset = jnp.sum(jnp.where(mask, offsets, 0.0), axis=0, keepdims=True)
        pos = (offset + rank_ref[pl.ds(c, 1), :]).astype(jnp.int32)
        pos = jnp.where(cell < 0, -1, pos)
        pos_ref[pl.ds(c, 1), :] = pos
        high = short_hot(iota((SORT_ROWS, CHUNK), 0), pos >> 7)
        low = short_hot(iota((CAP, CHUNK), 0), pos & 127)
        inside = (cell & (ROWS * NY - 1)).astype(F32)
        pieces = []
        for value in [inside] + [row_of(recv_ref, f, c) for f in range(1, 5)]:
            for part in parts_of(value, 2):
                pieces.append(low * part)
        acc_ref[...] += nt(high, jnp.concatenate(pieces, axis=0))
        return carry

    lax.fori_loop(0, chunks, sort_body, 0, unroll=2)
    for f in range(SORT_PARTS // 2):
        sorted_ref[f] = (
            acc_ref[:, 2 * f * CAP : (2 * f + 1) * CAP]
            + acc_ref[:, (2 * f + 1) * CAP : (2 * f + 2) * CAP]
        )

    bucket_rows = bucket_ref[...].astype(F32)
    tile_lane = iota((1, CAP), 1)
    forcing_ref[...] = jnp.zeros_like(forcing_ref)

    def tile_body(i, carry):
        for t in range(4):
            t = 4 * i + t
            cell, y, w, d = tile_rows(sorted_ref, t)
            level_x = iota((ROWS, SUB), 0)
            hot = short_hot(level_x, cell >> 8)
            next_hot = short_hot(level_x, (cell >> 8) + 1)
            spots = iota((NY, SUB), 0)
            here = short_hot(spots, lane_of(y))
            above = short_hot(spots, lane_of(y + 1))
            w = [parts_of(x * d, 2) for x in w]
            stacked = [here * w[0][p] + above * w[2][p] for p in range(2)]
            stacked += [here * w[1][p] + above * w[3][p] for p in range(2)]
            added = nt(
                jnp.concatenate([hot, hot, next_hot, next_hot], axis=1),
                jnp.concatenate(stacked, axis=1),
            )
            bucket = jnp.sum(jnp.where(tile_lane == t, bucket_rows, 0.0)).astype(jnp.int32)
            forcing_ref[bucket] += added
        return carry

    lax.fori_loop(0, (used + 3) // 4, tile_body, 0)


def tile_rows(sorted_ref, t):
    def row(f):
        return jnp.concatenate(
            [sorted_ref[f, pl.ds(2 * t, 1), :], sorted_ref[f, pl.ds(2 * t + 1, 1), :]], axis=1
        )

    cell = row(0).astype(jnp.int32)
    w = [row(1), row(2), row(3)]
    w.append(1.0 - w[0] - w[1] - w[2])
    return cell, cell & (NY - 1), w, row(4)


def gather_kernel(
    bucket_ref, state_ref, sorted_ref, pos_ref, recv_ref, own_ref, out_ref, value_ref, table_ref
):
    devices = recv_ref.shape[0]
    chunks = devices * CAP // CHUNK
    value_ref[...] = jnp.zeros_like(value_ref)

    def table_body(b, carry):
        turned = state_ref[b].T
        shifted = pltpu.roll(turned, ROWS - 1, 1)
        table_ref[b] = jnp.concatenate(
            [
                jnp.concatenate(parts_of(turned, 2), axis=1),
                jnp.concatenate(parts_of(shifted, 2), axis=1),
            ],
            axis=0,
        )
        return carry

    lax.fori_loop(0, BUCKETS, table_body, 0)

    def tile_body(i, carry):
        for t in range(4):
            t = 4 * i + t
            cell, y, w, _ = tile_rows(sorted_ref, t)
            hot = short_hot(iota((ROWS, SUB), 0), cell >> 8)
            spots = iota((NY, SUB), 0)
            here = spots == lane_of(y)
            above = spots == lane_of(y + 1)
            got = nn(table_ref[bucket_ref[0, t]], jnp.concatenate([hot, hot], axis=0))
            first = jnp.where(here, w[0], jnp.where(above, w[2], 0.0))
            second = jnp.where(here, w[1], jnp.where(above, w[3], 0.0))
            value_ref[pl.ds(t, 1), :] = jnp.sum(
                first * got[:NY] + second * got[NY:], axis=0, keepdims=True
            )
        return carry

    lax.fori_loop(0, (bucket_ref[0, CAP - 1] + 3) // 4, tile_body, 0)
    table = jnp.concatenate(parts_of(value_ref[...].T, 2), axis=1)
    depth = value_ref.shape[0]

    def unsort_body(c, carry):
        pos = pos_ref[pl.ds(c, 1), :]
        high = short_hot(iota((depth, CHUNK), 0), pos >> 8)
        got = nn(table, jnp.concatenate([high, high], axis=0))
        low = iota((SUB, CHUNK), 0) == (pos & (SUB - 1))
        row = jnp.sum(jnp.where(low, got, 0.0), axis=0, keepdims=True)
        per = CHUNK // CAP
        block = jnp.concatenate([row[:, i * CAP : (i + 1) * CAP] for i in range(per)], axis=0)
        out_ref[pl.ds(pl.multiple_of(c * per, per), per), :CAP] = block
        return carry

    lax.fori_loop(0, chunks, unsort_body, 0, unroll=2)
    d = recv_ref[:, 4, :]
    r = recv_ref[:, 5, :]
    image = out_ref[:, :CAP] + recv_ref[:, 6, :] * d
    out_ref[:, :CAP] = image
    own = own_ref[...]
    lane = iota((1, CAP), 1)
    sums = jnp.where(lane == 0, jnp.sum(own * own), 0.0)
    sums = jnp.where(lane == 1, jnp.sum(d * image), sums)
    sums = jnp.where(lane == 2, jnp.sum(r * image), sums)
    sums = jnp.where(lane == 3, jnp.sum(image * image), sums)
    out_ref[:, CAP:] = jnp.broadcast_to(sums, (devices, CAP))


def final_kernel(
    out_ref,
    route_ref,
    rank_ref,
    dual_ref,
    d_ref,
    r_ref,
    dual_out,
    res_out,
    dir_out,
    halfway,
    landing,
    hot_ref,
    send_sem,
    recv_sem,
):
    g = lax.axis_index("tm")
    t = lax.axis_index("space")
    groups = lax.axis_size("tm")
    strips = lax.axis_size("space")
    devices = groups * strips

    barrier = pltpu.get_barrier_semaphore()
    for step in range(1, groups):
        pl.semaphore_signal(
            barrier, inc=1, device_id=(around(g, step, groups), t), device_id_type=MESH
        )

    def greet(i, carry):
        other = (g, around(t, i, strips))
        pl.semaphore_signal(barrier, inc=1, device_id=other, device_id_type=MESH)
        return carry

    lax.fori_loop(1, strips, greet, 0, unroll=True)
    pl.semaphore_wait(barrier, groups + strips - 2)

    def along_space(i, carry):
        strip = around(t, i, strips)
        pltpu.make_async_remote_copy(
            src_ref=out_ref.at[:, strip],
            dst_ref=halfway.at[:, strip_of(t)],
            send_sem=send_sem.at[0],
            recv_sem=recv_sem.at[0],
            device_id=(g, strip),
            device_id_type=MESH,
        ).start()
        return carry

    lax.fori_loop(1, strips, along_space, 0, unroll=True)
    pltpu.make_async_copy(out_ref.at[:, t], halfway.at[:, strip_of(t)], recv_sem.at[0]).start()
    chunks = route_ref.shape[1] // CHUNK
    for c in range(chunks):
        lanes = slice(c * CHUNK, (c + 1) * CHUNK)
        hot_ref[c] = one_hot(iota((devices, CHUNK), 0) == route_ref[:, lanes])
    pltpu.make_async_copy(halfway, halfway, recv_sem.at[0]).wait()
    for step in range(1, groups):
        group = around(g, step, groups)
        pltpu.make_async_remote_copy(
            src_ref=halfway.at[group],
            dst_ref=landing.at[g],
            send_sem=send_sem.at[1],
            recv_sem=recv_sem.at[1],
            device_id=(group, t),
            device_id_type=MESH,
        ).start()
    pltpu.make_async_copy(halfway.at[g], landing.at[g], recv_sem.at[1]).start()
    pltpu.make_async_copy(landing, landing, recv_sem.at[1]).wait()
    returned = landing[...].reshape(devices, 2 * CAP)
    sums = jnp.sum(returned[:, CAP:], axis=0, keepdims=True)
    lane = iota((1, CAP), 1)
    norm_now, curvature, cross, square = [
        jnp.sum(jnp.where(lane == i, sums, 0.0), axis=1, keepdims=True) for i in range(4)
    ]
    step = norm_now / curvature
    norm_next = norm_now - 2.0 * step * cross + step * step * square
    ratio = norm_next / norm_now
    table = jnp.concatenate(parts_of(returned[:, :CAP].T, 2), axis=1)
    for c in range(chunks):
        lanes = slice(c * CHUNK, (c + 1) * CHUNK)
        hot = hot_ref[c]
        got = nn(table, jnp.concatenate([hot, hot], axis=0))
        mask = iota((CAP, CHUNK), 0) == rank_ref[:, lanes]
        image = jnp.sum(jnp.where(mask, got, 0.0), axis=0, keepdims=True)
        d = d_ref[:, lanes]
        res = r_ref[:, lanes] - step * image
        dual_out[:, lanes] = dual_ref[:, lanes] + step * d
        res_out[:, lanes] = res
        dir_out[:, lanes] = res + ratio * d
    rest = out_ref.at[:, pl.ds(0, strips - 1)]
    pltpu.make_async_copy(rest, rest, send_sem.at[0]).wait()
    rest = halfway.at[pl.ds(0, groups - 1)]
    pltpu.make_async_copy(rest, rest, send_sem.at[1]).wait()


def back(x):
    return jnp.concatenate([pltpu.roll(x[:, HALF:], 1, 1), x[:, :HALF]], axis=1)


def ahead(x):
    return jnp.concatenate([x[:, HALF:], pltpu.roll(x[:, :HALF], HALF - 1, 1)], axis=1)


def sweep_kernel(
    forcing_ref,
    coef,
    state_ref,
    scalars,
    scalar_sem,
    hop_a,
    hop_x,
    fin_a,
    fin_x,
    adj_out,
    adj_in,
    force_out,
    force_in,
    cov_out,
    cov_in,
    fwd_out,
    fwd_in,
    fext,
    u0,
    u1,
    u2,
    u3,
    v0,
    v1,
    v2,
    v3,
    inc,
    hop_sem,
    adj_sem,
    force_sem,
    cov_sem,
    fwd_sem,
):
    g = lax.axis_index("tm")
    t = lax.axis_index("space")
    groups = lax.axis_size("tm")
    strips = lax.axis_size("space")
    strip = strip_of(t)
    left = (g, strip_of(lax.rem(strip + strips - 1, strips)))
    right = (g, strip_of(lax.rem(strip + 1, strips)))
    later = (lax.rem(g + 1, groups), t)
    earlier = (lax.rem(g + groups - 1, groups), t)
    sides = (left, right)
    first_strip = strip == 0
    last_strip = strip == strips - 1
    last_group = g == groups - 1
    first_group = g == 0

    barrier = pltpu.get_barrier_semaphore()
    for other in (left, right, later, earlier):
        pl.semaphore_signal(barrier, inc=1, device_id=other, device_id_type=MESH)

    fetch = pltpu.make_async_copy(coef.at[5 * LEV, :, pl.ds(0, CAP)], scalars, scalar_sem)
    fetch.start()
    pl.semaphore_wait(barrier, 4)

    def to_side(src, dst, sems, side, *idx):
        return pltpu.make_async_remote_copy(
            src_ref=src,
            dst_ref=dst,
            send_sem=sems.at[(0, side) + idx],
            recv_sem=sems.at[(1, 1 - side) + idx],
            device_id=sides[side],
            device_id_type=MESH,
        )

    def wait_side(dst, sems, slot, *idx):
        pltpu.make_async_remote_copy(
            src_ref=dst,
            dst_ref=dst,
            send_sem=sems.at[(0, slot) + idx],
            recv_sem=sems.at[(1, slot) + idx],
            device_id=sides[slot],
            device_id_type=MESH,
        ).wait_recv()

    def hop(src, dst, way, level, device):
        return pltpu.make_async_remote_copy(
            src_ref=src.at[level],
            dst_ref=dst.at[level],
            send_sem=hop_sem.at[way, 0, level],
            recv_sem=hop_sem.at[way, 1, level],
            device_id=device,
            device_id_type=MESH,
        )

    upper = iota((CX, NY), 0) < 4

    def pack(out, level, first, value):
        for j in range(NV // 2):
            one = value[2 * j]
            two = pltpu.roll(value[2 * j + 1], 4, 0)
            out[0, level, first + j] = jnp.where(upper, one, two)
            out[1, level, first + j] = jnp.where(upper, two, one)

    def join(arrived, level, first):
        tiles = []
        for j in range(NV // 2):
            from_left = arrived[0, level, first + j]
            from_right = arrived[1, level, first + j]
            tiles.append(jnp.where(upper, from_right, from_left))
            tiles.append(pltpu.roll(jnp.where(upper, from_left, from_right), 4, 0))
        return tiles

    def exchange(out, arrived, sems, level):
        for side in range(2):
            to_side(
                out.at[side, level], arrived.at[1 - side, level], sems, side, level
            ).start()

    def await_sides(arrived, sems, level):
        for slot in range(2):
            wait_side(arrived.at[slot, level], sems, slot, level)

    def send_forcing(l):
        for i in range(3):
            pack(force_out, l, 2 * i, [forcing_ref[i, v, l] for v in range(NV)])
        exchange(force_out, force_in, force_sem, l)

    edge = jnp.zeros((NV, EXT, NY), F32)
    for u in (u0, u1, u2, u3, v0, v1, v2, v3):
        u[0] = edge
        u[LEV + 1] = edge

    @pl.when(last_group)
    def _():
        hop_a[...] = jnp.zeros_like(hop_a)

    @pl.when(first_group)
    def _():
        hop_x[...] = jnp.zeros_like(hop_x)

    @pl.when(jnp.logical_not(last_group))
    def _():
        def early(l, carry):
            send_forcing(l)
            return carry

        lax.fori_loop(0, LEV, early, 0)

    inside = inside_grid(first_strip, last_strip)
    fetch.wait()
    mix = [[coupling_step * scalars[v, w] for w in range(NV)] for v in range(NV)]

    def adjoint_level(u, l, rows):
        c, w, e, s, n = [coef[i * LEV + l] for i in range(5)]
        now = [u[l + 1, v] for v in range(NV)]
        out = []
        for v in range(NV):
            a = now[v]
            res = c[:rows] * a[:rows]
            res = res + pltpu.roll(w * a, EXT - 1, 0)[:rows] + pltpu.roll(e * a, 1, 0)[:rows]
            res = res + ahead(s[:rows] * a[:rows]) + back(n[:rows] * a[:rows])
            res = res + vertical * (u[l, v, :rows] + u[l + 2, v, :rows])
            for k in range(NV):
                res = res + mix[k][v] * now[k][:rows]
            out.append(res)
        return out

    def forward_level(u, l, rows):
        c, w, e, s, n = [coef[i * LEV + l][:rows] for i in range(5)]
        now = [u[l + 1, v] for v in range(NV)]
        out = []
        for v in range(NV):
            a = now[v]
            res = c * a[:rows]
            res = res + w * pltpu.roll(a, 1, 0)[:rows] + e * pltpu.roll(a, EXT - 1, 0)[:rows]
            res = res + s * back(a[:rows]) + n * ahead(a[:rows])
            res = res + vertical * (u[l, v, :rows] + u[l + 2, v, :rows])
            for k in range(NV):
                res = res + mix[v][k] * now[k][:rows]
            out.append(res)
        return out

    def in_range(l):
        return (l >= 0) & (l < LEV)

    def adjoint_tick(k):
        @pl.when(in_range(k))
        def _():
            @pl.when(jnp.logical_not(last_group))
            def _():
                hop(hop_a, hop_a, 0, k, later).wait_recv()

            value = [hop_a[k, v] + forcing_ref[3, v, k] for v in range(NV)]
            pack(adj_out, k, 0, value)
            exchange(adj_out, adj_in, adj_sem, k)

            @pl.when(last_group)
            def _():
                send_forcing(k)

            for v in range(NV):
                u0[k + 1, v, :CX] = value[v]

        m = k - ADJ_DELAY

        @pl.when(in_range(m))
        def _():
            await_sides(adj_in, adj_sem, m)
            await_sides(force_in, force_sem, m)
            for v, tile in enumerate(join(adj_in, m, 0)):
                u0[m + 1, v, CX:] = tile
            for i in range(3):
                for v, tile in enumerate(join(force_in, m, 2 * i)):
                    fext[i, m, v] = tile

        for i, (src, dst) in enumerate(((u0, u1), (u1, u2), (u2, u3))):
            level = m - 1 - i

            @pl.when(in_range(level))
            def _():
                res = adjoint_level(src, level, EXT)
                for v in range(NV):
                    dst[level + 1, v, :CX] = res[v][:CX] + forcing_ref[2 - i, v, level]
                    dst[level + 1, v, CX:] = res[v][CX:] + fext[2 - i, level, v]

        level = m - 4

        @pl.when(in_range(level))
        def _():
            res = adjoint_level(u3, level, CX)
            for v in range(NV):
                fin_a[level, v] = res[v]

            @pl.when(jnp.logical_not(first_group))
            def _():
                hop(fin_a, hop_a, 0, level, earlier).start()

            pack(cov_out, level, 0, res)
            exchange(cov_out, cov_in, cov_sem, level)

    lane_low = jnp.where(iota((CX, NY), 1) > 0, 1.0, 0.0)
    lane_high = jnp.where(iota((CX, NY), 1) < NY - 1, 1.0, 0.0)
    keep = jnp.where(inside, 1.0, 0.0)

    def cov_tick(l):
        @pl.when(in_range(l))
        def _():
            await_sides(cov_in, cov_sem, l)
            for v, tile in enumerate(join(cov_in, l, 0)):
                scale = scalars[CX + v, l]
                ext = jnp.concatenate([fin_a[l, v], tile], axis=0) * (keep * scale)
                ext = 0.5 * ext + 0.25 * (pltpu.roll(ext, 1, 0) + pltpu.roll(ext, EXT - 1, 0))
                ext = ext * keep
                ext = 0.5 * ext + 0.25 * (pltpu.roll(ext, 1, 0) + pltpu.roll(ext, EXT - 1, 0))
                own = ext[:CX]
                for _ in range(2):
                    own = 0.5 * own + 0.25 * (lane_low * back(own) + lane_high * ahead(own))
                inc[l, v] = own * scale

    fwd_delay = jnp.where(first_group, FIRST_DELAY, FWD_DELAY)

    def forward_tick(k):
        @pl.when(in_range(k))
        def _():
            @pl.when(jnp.logical_not(first_group))
            def _():
                hop(hop_x, hop_x, 1, k, earlier).wait_recv()

            value = [hop_x[k, v] + inc[k, v] for v in range(NV)]
            pack(fwd_out, k, 0, value)
            exchange(fwd_out, fwd_in, fwd_sem, k)
            for v in range(NV):
                v0[k + 1, v, :CX] = value[v]

        m = k - fwd_delay

        @pl.when(in_range(m))
        def _():
            await_sides(fwd_in, fwd_sem, m)
            for v, tile in enumerate(join(fwd_in, m, 0)):
                v0[m + 1, v, CX:] = tile

        for i, (src, dst) in enumerate(((v0, v1), (v1, v2), (v2, v3))):
            level = m - 1 - i

            @pl.when(in_range(level))
            def _():
                res = forward_level(src, level, EXT)
                for v in range(NV):
                    dst[level + 1, v] = res[v]
                    state_ref[i, v, level] = res[v][:CX]

        level = m - 4

        @pl.when(in_range(level))
        def _():
            res = forward_level(v3, level, CX)
            for v in range(NV):
                state_ref[3, v, level] = res[v]
                fin_x[level, v] = res[v]

            @pl.when(jnp.logical_not(last_group))
            def _():
                hop(fin_x, hop_x, 1, level, later).start()

    adjoint_ticks = LEV + ADJ_DELAY + 4
    behind = jnp.where(first_group, ADJ_DELAY + 4 + COV_DELAY, adjoint_ticks)

    def tick(k, carry):
        adjoint_tick(k)
        cov_tick(k - (ADJ_DELAY + 4 + COV_DELAY))
        forward_tick(k - behind)
        return carry

    lax.fori_loop(0, behind + LEV + fwd_delay + 4, tick, 0)

    def drain(l, carry):
        for out, arrived, sems in (
            (adj_out, adj_in, adj_sem),
            (force_out, force_in, force_sem),
            (cov_out, cov_in, cov_sem),
            (fwd_out, fwd_in, fwd_sem),
        ):
            for side in range(2):
                to_side(
                    out.at[side, l], arrived.at[1 - side, l], sems, side, l
                ).wait_send()

        @pl.when(jnp.logical_not(first_group))
        def _():
            hop(fin_a, hop_a, 0, l, earlier).wait_send()

        @pl.when(jnp.logical_not(last_group))
        def _():
            hop(fin_x, hop_x, 1, l, later).wait_send()

        return carry

    lax.fori_loop(0, LEV, drain, 0)


def sweeps(forcing, coef):
    state = pltpu.VMEM((LEV, NV, CX, NY), F32)
    padded = pltpu.VMEM((LEV + 2, NV, EXT, NY), F32)
    edges = pltpu.VMEM((2, LEV, 2, CX, NY), F32)
    wide_edges = pltpu.VMEM((2, LEV, 6, CX, NY), F32)
    levels = pltpu.SemaphoreType.DMA((2, 2, LEV))
    return pl.pallas_call(
        sweep_kernel,
        out_shape=jax.ShapeDtypeStruct((STEPS, NV, LEV, CX, NY), F32),
        in_specs=[VMEM, VMEM],
        out_specs=VMEM,
        scratch_shapes=[
            pltpu.SMEM((EXT, CAP), F32),
            pltpu.SemaphoreType.DMA,
        ]
        + [state] * 4
        + [edges] * 2
        + [wide_edges] * 2
        + [edges] * 4
        + [pltpu.VMEM((3, LEV, NV, CX, NY), F32)]
        + [padded] * 8
        + [state]
        + [levels] * 5,
        compiler_params=params(34, collective_id=1, has_side_effects=True),
        name="sweeps",
    )(forcing, coef)


def per_device(
    dual_weights,
    direction,
    residual_dual,
    obs_var,
    obs_route,
    obs_cell,
    obs_interp,
    wind_x,
    wind_y,
    coupling,
    cov_scale,
):
    grid = (lax.axis_size("tm"), lax.axis_size("space"))
    devices = grid[0] * grid[1]
    rows = direction.shape[0]
    wide = (1, rows)
    route = obs_route.reshape(1, rows)
    tiles = pltpu.VMEM((devices, 8, CAP), F32)
    arrived, rank, coef = pl.pallas_call(
        route_kernel,
        out_shape=(
            jax.ShapeDtypeStruct((devices, 8, CAP), F32),
            jax.ShapeDtypeStruct((1, rows), jnp.int32),
            jax.ShapeDtypeStruct((5 * LEV + 1, EXT, NY), F32),
        ),
        in_specs=[ANY] * 10,
        out_specs=(VMEM, VMEM, VMEM),
        scratch_shapes=[
            tiles,
            tiles,
            pltpu.VMEM((devices, sum(PACK_PARTS) * CAP), F32),
            pltpu.VMEM((2, LEV, CX, NY), F32),
            pltpu.VMEM((3, 2, LEV, CX, NY), F32),
            pltpu.VMEM((1, rows), jnp.int32),
            pltpu.VMEM((1, rows), jnp.int32),
            pltpu.VMEM((4, rows), F32),
            pltpu.VMEM((1, rows), F32),
            pltpu.VMEM((1, rows), F32),
            pltpu.VMEM((1, rows), F32),
            pltpu.VMEM((1, LEV, CX, NY), F32),
            pltpu.VMEM((1, LEV, CX, NY), F32),
            pltpu.VMEM((NV, NV), F32),
            pltpu.VMEM((1, NV, LEV), F32),
            pltpu.SemaphoreType.DMA,
            pltpu.SemaphoreType.DMA,
            pltpu.SemaphoreType.DMA((2, 3)),
            pltpu.SemaphoreType.DMA((10,)),
        ],
        compiler_params=params(58, collective_id=2, has_side_effects=True),
        name="route",
    )(
        route,
        obs_cell.reshape(1, rows),
        obs_interp,
        direction.reshape(1, rows),
        residual_dual.reshape(1, rows),
        obs_var.reshape(1, rows),
        wind_x,
        wind_y,
        coupling,
        cov_scale,
    )
    slots = devices * CAP
    forcing, ordered, position, starts = pl.pallas_call(
        sort_scatter_kernel,
        out_shape=(
            jax.ShapeDtypeStruct((BUCKETS, ROWS, NY), F32),
            jax.ShapeDtypeStruct((SORT_PARTS // 2, SORT_ROWS, CAP), F32),
            jax.ShapeDtypeStruct((slots // CHUNK, CHUNK), jnp.int32),
            jax.ShapeDtypeStruct((1, CAP), jnp.int32),
        ),
        in_specs=[VMEM],
        out_specs=(VMEM, VMEM, VMEM, VMEM),
        scratch_shapes=[
            pltpu.VMEM((slots // CHUNK, CHUNK), F32),
            pltpu.VMEM((SORT_ROWS, SORT_PARTS * CAP), F32),
        ],
        compiler_params=params(20),
        name="sort_scatter",
    )(arrived)
    states = sweeps(forcing.reshape(STEPS, NV, LEV, CX, NY), coef)
    returning = pl.pallas_call(
        gather_kernel,
        out_shape=jax.ShapeDtypeStruct((devices, 2 * CAP), F32),
        in_specs=[SMEM, VMEM, VMEM, VMEM, VMEM, VMEM],
        out_specs=VMEM,
        scratch_shapes=[
            pltpu.VMEM((CAP, SUB), F32),
            pltpu.VMEM((BUCKETS, 2 * NY, 2 * ROWS), BF16),
        ],
        compiler_params=params(20),
        name="gather",
    )(
        starts,
        states.reshape(BUCKETS, ROWS, NY),
        ordered,
        position,
        arrived,
        residual_dual.reshape(wide),
    )
    out = jax.ShapeDtypeStruct(wide, F32)
    results = pl.pallas_call(
        final_kernel,
        out_shape=(out, out, out),
        in_specs=[VMEM] * 6,
        out_specs=(VMEM, VMEM, VMEM),
        scratch_shapes=[
            pltpu.VMEM(grid + (1, 2 * CAP), F32),
            pltpu.VMEM(grid + (1, 2 * CAP), F32),
            pltpu.VMEM((rows // CHUNK, devices, CHUNK), BF16),
            pltpu.SemaphoreType.DMA((2,)),
            pltpu.SemaphoreType.DMA((2,)),
        ],
        compiler_params=params(12, collective_id=3, has_side_effects=True),
        name="final",
    )(
        returning.reshape(grid + (1, 2 * CAP)),
        route.reshape(wide),
        rank.reshape(wide),
        dual_weights.reshape(wide),
        direction.reshape(wide),
        residual_dual.reshape(wide),
    )
    return tuple(r.reshape(rows) for r in results)


def solution(mesh):
    return jax.shard_map(
        per_device,
        mesh=mesh,
        in_specs=(
            P(("tm", "space")),
            P(("tm", "space")),
            P(("tm", "space")),
            P(("tm", "space")),
            P(("tm", "space"), None),
            P(("tm", "space")),
            P(None, ("tm", "space")),
            P("tm", None, "space", None),
            P("tm", None, "space", None),
            P(),
            P("tm", None, None),
        ),
        out_specs=(P(("tm", "space")), P(("tm", "space")), P(("tm", "space"))),
        check_vma=False,
    )
```
